32 devices in a mesh: section: 4 (over z), dp: 8 (over y, x, core).
Axes of the slice: x: 2, y: 2, z: 4, core: 2. Of those that a mesh axis runs over, the one named last changes fastest.
Arguments:
- inputs: bfloat16 [4, 256, 6144], P(None, 'dp', 'section'), may hold values from -6 to 6
- gain: float32 [4, 6144], P('section'), may hold values from 0.1 to 1.9
- repeats: int32 [4], P('section'), may hold values from 0 to 3
- order: int32 [4], replicated, may hold values from 0 to 3, each once
- hidden_grad: bfloat16 [4, 4, 256, 12288], P('section', None, 'dp'), may hold values from -6 to 6
Outputs:
- feature_factor: float32 [4, 3072, 128], P('section', 'dp')
- hidden_factor: float32 [4, 12288, 128], P('section', 'dp')
The draws below stay inside these ranges and needn't reach their ends.
Inputs may be any that keep to these rules, and one draw needn't show every extreme that they name: `order`: each micro-batch id once.
All inputs are finite; a program needn't handle non-finite values.
Results may differ from the reference program's by a relative error of at most 0.0085.
Values may be sent and summed in bfloat16 or wider, within the bound.
No kernel may reach another device: no remote copies, remote signals or barrier semaphores. Data moves between devices by JAX's collectives and lax.ppermute only.
A program may use at most 128 MiB of HBM per device.

```python
import jax
import jax.numpy as jnp
from jax import lax

D = 6144
AWIN = 3072
GWIN = 12288
BLK = 128
MB = 4
TOK = 32
SECTIONS = 4
TOKENS = 256
N_DP = 8


def with_ends(entries, rng, least, largest):
    spot = [jax.random.randint(jax.random.fold_in(rng, axis), (), 0, length) for axis, length in enumerate(entries.shape)]
    widest = entries.shape.index(max(entries.shape))
    neighbour = spot[:widest] + [(spot[widest] + 1) % entries.shape[widest]] + spot[widest + 1:]
    return entries.at[tuple(spot)].set(least).at[tuple(neighbour)].set(largest)


def spiked(result, rng, source, target, parts, factor):
    owner, partner = [(jnp.arange(result.shape[axis_at]) // (result.shape[axis_at] // parts)).reshape([-1 if axis == axis_at else 1 for axis in range(result.ndim)]) for axis_at in (source, target)]
    chosen = jax.random.permutation(rng, parts)[partner]
    strong = (owner == chosen) | (owner == (partner + parts // 2) % parts)
    return jnp.where(strong, factor * result, result)


def block_scale(key, dims, split, smallest, largest):
    level, own = 1.0, jax.random.fold_in(key, 6)
    for dim, parts in split:
        steps = jnp.exp(jax.random.uniform(jax.random.fold_in(own, dim), (parts,), jnp.float32, smallest / len(split), largest / len(split)))
        level = level * jnp.repeat(steps, dims[dim] // parts).reshape([-1 if axis == dim else 1 for axis in range(len(dims))])
    return level


def gaussian(own_key, extent, deviation, most, shards=(), held_as=jnp.bfloat16):
    level = block_scale(own_key, extent, shards, -0.22, 0.18) if shards else 1.0
    result = jax.random.normal(own_key, extent, jnp.float32) * deviation * level
    return jnp.minimum(jnp.maximum(result, -most), most).astype(held_as)


def bell_draw_with(rng, shape, scale, reach, pieces, heavy, held_as=jnp.bfloat16):
    array = scale * jax.random.normal(rng, shape, jnp.float32)
    if pieces:
        array = array * block_scale(rng, shape, pieces, -0.22, 0.18)
    return jnp.clip(spiked(array, jax.random.fold_in(rng, 3), *heavy), -reach, reach).astype(held_as)


def setup_inputs(seed: int = 0) -> dict:
    key_of = jax.random.split(jax.random.key(seed), 6)
    inputs = gaussian(key_of[0], (MB, TOKENS, D), 1.0, 6.0, ((1, 8), (2, 4)))
    gain = jnp.clip(1.0 + 0.18 * jax.random.normal(key_of[1], (SECTIONS, D), jnp.float32), 0.1, 1.9)
    repeats = with_ends(jax.random.randint(key_of[2], (SECTIONS,), 0, 4), jax.random.fold_in(key_of[2], 1), 0, 3).astype(jnp.int32)
    order = jax.random.permutation(key_of[3], MB).astype(jnp.int32)
    hidden_grad = bell_draw_with(key_of[4], (SECTIONS, MB, TOKENS, GWIN), 1.0, 6.0, ((0, 4), (2, 8)), (2, 3, 8, 2.0))
    return dict(inputs=inputs, gain=gain, repeats=repeats, order=order, hidden_grad=hidden_grad)


def normed(value, gain_row):
    wide = value.astype(jnp.float32)
    center = lax.optimization_barrier(jnp.mean(wide, axis=-1, keepdims=True))
    spread = lax.optimization_barrier(jnp.mean(jnp.square(wide - center), axis=-1, keepdims=True))
    return (wide - center) * lax.rsqrt(spread + 1e-05) * gain_row

def update(value, gain_row):
    return (value.astype(jnp.float32) + jax.nn.gelu(normed(value, gain_row))).astype(jnp.bfloat16)

def reference(inputs, gain, repeats, order, hidden_grad):
    slots = jnp.arange(MB, dtype=jnp.float32)
    slot_weight = 0.5 * jnp.power(0.5, MB - 1 - slots)
    onehot = (order[:, None] == jnp.arange(MB, dtype=jnp.int32)[None, :]).astype(jnp.float32)
    hidden_weight = jnp.dot(slot_weight, onehot, precision=lax.Precision.HIGHEST)
    current = jnp.take(inputs, order, axis=0)
    feature_list = []
    hidden_list = []
    for section_num in range(SECTIONS):
        gain_row = gain[section_num]
        current = lax.fori_loop(0, repeats[section_num] + 1, lambda i, v: update(v, gain_row), current)
        feats = normed(current, gain_row).astype(jnp.bfloat16)[:, :, :AWIN].astype(jnp.float32)
        feats = feats.reshape(MB, N_DP, TOK, AWIN // BLK, BLK)
        part = jnp.einsum('mptbi,mptbj,m->pbij', feats, feats, slot_weight, precision=lax.Precision.HIGHEST) / TOKENS
        part = lax.optimization_barrier(part.astype(jnp.bfloat16)).astype(jnp.float32)
        feature_list.append(lax.optimization_barrier(jnp.sum(part, axis=0)).reshape(AWIN, BLK))
        grads = hidden_grad[section_num].astype(jnp.float32).reshape(MB, N_DP, TOK, GWIN // BLK, BLK)
        hpart = jnp.einsum('mptbi,mptbj,m->pbij', grads, grads, hidden_weight, precision=lax.Precision.HIGHEST) / TOKENS
        hpart = lax.optimization_barrier(hpart.astype(jnp.bfloat16)).astype(jnp.float32)
        hidden_list.append(lax.optimization_barrier(jnp.sum(hpart, axis=0)).reshape(GWIN, BLK))
    return (jnp.stack(feature_list), jnp.stack(hidden_list))
```

```python
import functools

import jax
import jax.numpy as jnp
from jax import lax
from jax.experimental import pallas as pl
from jax.experimental.pallas import tpu as pltpu
from jax.sharding import PartitionSpec as P

AWIN = 3072
GWIN = 12288
BLK = 128
VMEM_LIMIT = 48 * 1024 * 1024

SMEM_SPEC = pl.BlockSpec(memory_space=pltpu.SMEM)
VMEM_SPEC = pl.BlockSpec(memory_space=pltpu.VMEM)


def params():
    return pltpu.CompilerParams(vmem_limit_bytes=VMEM_LIMIT)


def gelu(x):
    inner = 0.7978845608028654 * (x + 0.044715 * (x * x * x))
    return x * (0.5 * (1.0 + jnp.tanh(inner)))


def batch_weight(order_ref, batch_id, micro):
    weight = jnp.float32(0.0)
    for slot in range(micro):
        weight = jnp.where(order_ref[slot] == batch_id, jnp.float32(0.5 * 0.5 ** (micro - 1 - slot)), weight)
    return weight


def gram(left, right):
    return lax.dot_general(left, right, (((0,), (0,)), ((), ())), preferred_element_type=jnp.float32)


def iotas():
    row = lax.broadcasted_iota(jnp.int32, (BLK, BLK), 0)
    col = lax.broadcasted_iota(jnp.int32, (BLK, BLK), 1)
    return row, col


def packed_rows(pairs):
    return pairs * BLK + -(-pairs // 16) * 16


def hidden_kernel(micro, pairs, scale, order_ref, grad_ref, out_ref):
    row, col = iotas()
    weights = [batch_weight(order_ref, m, micro) for m in range(micro)]
    diagonals = []
    for pair in range(pairs):
        cols = slice(pair * 2 * BLK, (pair + 1) * 2 * BLK)
        parts = [grad_ref[0, m, :, cols] for m in range(micro)]
        plain = jnp.concatenate(parts, axis=0)
        scaled = jnp.concatenate(
            [(part.astype(jnp.float32) * weight).astype(jnp.bfloat16) for part, weight in zip(parts, weights)], axis=0
        )
        both = gram(scaled, plain) * scale
        first, second = both[:BLK, :BLK], both[BLK:, BLK:]
        out_ref[0, pair * BLK:(pair + 1) * BLK] = jnp.where(col >= row, first, second).astype(jnp.bfloat16)
        diagonals.append(jnp.sum(jnp.where(col == row, second, 0.0), axis=0, keepdims=True))
    rest = packed_rows(pairs) - pairs * BLK - pairs
    diagonals.append(jnp.zeros((rest, BLK), jnp.float32))
    out_ref[0, pairs * BLK:] = jnp.concatenate(diagonals, axis=0).astype(jnp.bfloat16)


def hidden_packed(order, hidden_grad, owners, scale):
    _, micro, rows, width = hidden_grad.shape
    own = width // owners
    pairs = own // (2 * BLK)
    return pl.pallas_call(
        functools.partial(hidden_kernel, micro, pairs, scale),
        grid=(owners,),
        out_shape=jax.ShapeDtypeStruct((owners, packed_rows(pairs), BLK), jnp.bfloat16),
        in_specs=[SMEM_SPEC, pl.BlockSpec((1, micro, rows, own), lambda i: (0, 0, 0, i))],
        out_specs=pl.BlockSpec((1, packed_rows(pairs), BLK), lambda i: (i, 0, 0)),
        compiler_params=params(),
        cost_estimate=pl.CostEstimate(flops=2 * micro * rows * width * 2 * BLK, bytes_accessed=6 << 20, transcendentals=0),
    )(order, hidden_grad)


def unpack_kernel(sources, pairs, in_ref, out_ref):
    row, col = iotas()
    tail = in_ref[0, pairs * BLK:].astype(jnp.float32)
    for source in range(1, sources):
        tail = tail + in_ref[source, pairs * BLK:].astype(jnp.float32)
    for pair in range(pairs):
        rows = slice(pair * BLK, (pair + 1) * BLK)
        total = in_ref[0, rows].astype(jnp.float32)
        for source in range(1, sources):
            total = total + in_ref[source, rows].astype(jnp.float32)
        turned = total.T
        out_ref[0, 2 * pair * BLK:(2 * pair + 1) * BLK] = jnp.where(col >= row, total, turned)
        second = jnp.where(col == row, tail[pair:pair + 1], turned)
        out_ref[0, (2 * pair + 1) * BLK:(2 * pair + 2) * BLK] = jnp.where(col < row, total, second)


def hidden_unpacked(packed, pairs):
    return pl.pallas_call(
        functools.partial(unpack_kernel, packed.shape[0], pairs),
        out_shape=jax.ShapeDtypeStruct((1, pairs * 2 * BLK, BLK), jnp.float32),
        in_specs=[VMEM_SPEC],
        out_specs=VMEM_SPEC,
        compiler_params=params(),
        cost_estimate=pl.CostEstimate(flops=4 << 20, bytes_accessed=3 << 20, transcendentals=0),
    )(packed)


def relay_kernel(sections, owners, chunk, in_ref, gain_ref, out_ref, held):
    rows, width = held.shape
    own = out_ref.shape[3]
    part = in_ref.shape[2]
    step = 512 if part % 512 == 0 else BLK

    def folded(value):
        return sum(value[:, i * BLK:(i + 1) * BLK] for i in range(value.shape[1] // BLK))

    def stats(total):
        center = jnp.sum(total, axis=-1, keepdims=True) * (1.0 / width)
        square = jnp.zeros((rows, BLK), jnp.float32)
        for at in range(0, width, step):
            square = square + folded(jnp.square(held[:, at:at + step] - center))
        spread = jnp.sum(square, axis=-1, keepdims=True) * (1.0 / width)
        return center, lax.rsqrt(spread + 1e-05)

    total = jnp.zeros((rows, BLK), jnp.float32)
    for source in range(sections):
        for at in range(0, part, step):
            value = in_ref[source, :, at:at + step].astype(jnp.float32)
            held[:, source * part + at:source * part + at + step] = value
            total = total + folded(value)

    def section(s, total):
        repeats = jnp.max(gain_ref[s, 0:1, width:width + BLK]).astype(jnp.int32)

        def apply(_, total):
            center, scale = stats(total)
            total = jnp.zeros((rows, BLK), jnp.float32)
            for at in range(0, width, step):
                value = held[:, at:at + step]
                normed = (value - center) * scale * gain_ref[s, 0:1, at:at + step]
                value = (value + gelu(normed)).astype(jnp.bfloat16).astype(jnp.float32)
                held[:, at:at + step] = value
                total = total + folded(value)
            return total

        total = lax.fori_loop(0, repeats + 1, apply, total)
        center, scale = stats(total)
        for owner in range(owners):
            cols = slice(owner * own, (owner + 1) * own)
            normed = (held[:, cols] - center) * scale * gain_ref[s, 0:1, cols]
            out_ref[owner, s] = normed.astype(jnp.bfloat16)
        return total

    lax.fori_loop(0, sections, section, total)


def relay(pieces, gains, owners):
    sections, rows, part = pieces.shape
    width = sections * part
    own = AWIN // owners
    return pl.pallas_call(
        functools.partial(relay_kernel, sections, owners, part),
        out_shape=jax.ShapeDtypeStruct((owners, sections, rows, own), jnp.bfloat16),
        in_specs=[VMEM_SPEC, VMEM_SPEC],
        out_specs=VMEM_SPEC,
        scratch_shapes=[pltpu.VMEM((rows, width), jnp.float32)],
        compiler_params=params(),
        cost_estimate=pl.CostEstimate(flops=40 * rows * width * 14, bytes_accessed=2 << 20, transcendentals=rows * width * 10),
    )(pieces, gains)


def feature_kernel(micro, blocks, scale, order_ref, in_ref, out_ref):
    weight = batch_weight(order_ref, lax.axis_index("section"), micro) * scale
    sources, sections = in_ref.shape[0], in_ref.shape[1]
    for s in range(sections):
        for block in range(blocks):
            cols = slice(block * BLK, (block + 1) * BLK)
            feats = jnp.concatenate([in_ref[source, s, :, cols] for source in range(sources)], axis=0)
            out_ref[s, cols] = (gram(feats, feats) * weight).astype(jnp.bfloat16)


def feature_terms(order, gathered, micro, scale):
    sources, sections, rows, own = gathered.shape
    return pl.pallas_call(
        functools.partial(feature_kernel, micro, own // BLK, scale),
        out_shape=jax.ShapeDtypeStruct((sections, own, BLK), jnp.bfloat16),
        in_specs=[SMEM_SPEC, VMEM_SPEC],
        out_specs=VMEM_SPEC,
        compiler_params=params(),
        cost_estimate=pl.CostEstimate(flops=2 * sources * sections * rows * own * BLK, bytes_accessed=2 << 20, transcendentals=0),
    )(order, gathered)


def fast_body(inputs, gain, repeats, order, hidden_grad):
    micro, tok_rows, _ = inputs.shape
    dp_count = lax.axis_size("dp")
    scale = 1.0 / (tok_rows * dp_count)
    told = jnp.concatenate([gain, jnp.broadcast_to(repeats.astype(jnp.float32)[:, None], (1, BLK))], axis=1)
    gains = lax.all_gather(told, "section", axis=0)
    pieces = lax.all_to_all(inputs, "section", 0, 0, tiled=True)
    packed = hidden_packed(order, hidden_grad, dp_count, scale)
    packed = lax.all_to_all(packed, "dp", 0, 0, tiled=True)
    feats = relay(pieces, gains, dp_count)
    feats = lax.all_to_all(feats, "dp", 0, 0, tiled=True)
    terms = feature_terms(order, feats, micro, scale)
    terms = lax.all_to_all(terms, "section", 0, 0, tiled=True)
    feature_rows = jnp.sum(terms.astype(jnp.float32), axis=0)
    hidden_rows = hidden_unpacked(packed, GWIN // dp_count // (2 * BLK))
    return (feature_rows[None], hidden_rows)


def normed(value, gain_row):
    center = jnp.mean(value, axis=-1, keepdims=True)
    spread = jnp.mean(jnp.square(value - center), axis=-1, keepdims=True)
    return (value - center) * lax.rsqrt(spread + 1e-05) * gain_row


def weighted_gram(feats, weights):
    shaped = feats.reshape(feats.shape[0], -1, BLK)
    scaled = shaped * weights[:, None, None].astype(shaped.dtype)
    return jnp.einsum("tbi,tbj->bij", scaled, shaped, preferred_element_type=jnp.float32)


def plain_body(inputs, gain, repeats, order, hidden_grad):
    micro, tok_rows, part = inputs.shape
    sections = lax.axis_size("section")
    total_tok = tok_rows * lax.axis_size("dp")
    slot_weight = 0.5 * jnp.power(0.5, micro - 1 - jnp.arange(micro, dtype=jnp.float32))
    hidden_weight = jnp.zeros((micro,), jnp.float32).at[order].set(slot_weight)
    row_weight = jnp.repeat(hidden_weight, tok_rows)
    hidden = weighted_gram(hidden_grad.reshape(micro * tok_rows, GWIN), row_weight) / total_tok
    gains = lax.all_gather(gain[0], "section", axis=0)
    counts = lax.all_gather(repeats[0], "section", axis=0)
    pieces = lax.all_to_all(inputs.reshape(micro * tok_rows, part), "section", 0, 1, tiled=True)

    def section(s, carry):
        value, feats = carry
        value = lax.fori_loop(
            0,
            counts[s] + 1,
            lambda i, v: (v + gelu(normed(v, gains[s]))).astype(jnp.bfloat16).astype(jnp.float32),
            value,
        )
        now = normed(value, gains[s]).astype(jnp.bfloat16)[:, :AWIN]
        return value, lax.dynamic_update_index_in_dim(feats, now, s, 0)

    start = jnp.zeros((sections, pieces.shape[0], AWIN), jnp.bfloat16)
    _, feats = lax.fori_loop(0, sections, section, (pieces.astype(jnp.float32), start))
    feats = lax.all_to_all(feats, "section", 0, 0, tiled=True).reshape(micro * tok_rows, AWIN)
    feature = weighted_gram(feats, row_weight) / total_tok

    def shared(term):
        term = term.reshape(-1, BLK).astype(jnp.bfloat16)
        return lax.psum_scatter(term, "dp", scatter_dimension=0, tiled=True).astype(jnp.float32)[None]

    return (shared(feature), shared(hidden))


def solution(mesh):
    sections, dp_count = mesh.shape["section"], mesh.shape["dp"]

    def body(inputs, gain, repeats, order, hidden_grad):
        aligned = (
            inputs.shape[0] == sections
            and inputs.shape[1] % 16 == 0
            and AWIN % (dp_count * BLK) == 0
            and GWIN % (dp_count * 2 * BLK) == 0
        )
        return (fast_body if aligned else plain_body)(inputs, gain, repeats, order, hidden_grad)

    placed = (
        P(None, "dp", "section"),
        P("section", None),
        P("section"),
        P(),
        P("section", None, "dp", None),
    )
    return jax.shard_map(
        body,
        mesh=mesh,
        in_specs=placed,
        out_specs=(P("section", "dp", None), P("section", "dp", None)),
        check_vma=False,
    )
```

```python
import functools

import jax
import jax.numpy as jnp
from jax import lax
from jax.experimental import pallas as pl
from jax.experimental.pallas import tpu as pltpu
from jax.sharding import PartitionSpec as P

AWIN = 3072
GWIN = 12288
BLK = 128
VMEM_LIMIT = 48 * 1024 * 1024
ROOT = 0.7978845608028654

SMEM_SPEC = pl.BlockSpec(memory_space=pltpu.SMEM)
VMEM_SPEC = pl.BlockSpec(memory_space=pltpu.VMEM)


def params(limit=VMEM_LIMIT):
    return pltpu.CompilerParams(vmem_limit_bytes=limit)


def gelu(x):
    inner = ROOT * (x + 0.044715 * (x * x * x))
    return x * (0.5 * (1.0 + jnp.tanh(inner)))


def batch_weight(order_ref, batch_id, micro):
    weight = jnp.float32(0.0)
    for slot in range(micro):
        weight = jnp.where(order_ref[slot] == batch_id, jnp.float32(0.5 * 0.5 ** (micro - 1 - slot)), weight)
    return weight


def gram(left, right):
    return lax.dot_general(left, right, (((0,), (0,)), ((), ())), preferred_element_type=jnp.float32)


def iotas():
    row = lax.broadcasted_iota(jnp.int32, (BLK, BLK), 0)
    col = lax.broadcasted_iota(jnp.int32, (BLK, BLK), 1)
    return row, col


def packed_rows(pairs):
    return pairs * BLK + -(-pairs // 16) * 16


def hidden_kernel(micro, pairs, scale, order_ref, grad_ref, out_ref):
    row, col = iotas()
    weights = [batch_weight(order_ref, m, micro) for m in range(micro)]
    diagonals = []
    for pair in range(pairs):
        cols = slice(pair * 2 * BLK, (pair + 1) * 2 * BLK)
        parts = [grad_ref[0, m, :, cols] for m in range(micro)]
        plain = jnp.concatenate(parts, axis=0)
        scaled = jnp.concatenate(
            [(part.astype(jnp.float32) * weight).astype(jnp.bfloat16) for part, weight in zip(parts, weights)], axis=0
        )
        both = gram(scaled, plain) * scale
        first, second = both[:BLK, :BLK], both[BLK:, BLK:]
        out_ref[0, pair * BLK:(pair + 1) * BLK] = jnp.where(col >= row, first, second).astype(jnp.bfloat16)
        diagonals.append(jnp.sum(jnp.where(col == row, second, 0.0), axis=0, keepdims=True))
    rest = packed_rows(pairs) - pairs * BLK - pairs
    diagonals.append(jnp.zeros((rest, BLK), jnp.float32))
    out_ref[0, pairs * BLK:] = jnp.concatenate(diagonals, axis=0).astype(jnp.bfloat16)


def hidden_packed(order, hidden_grad, owners, scale):
    _, micro, rows, width = hidden_grad.shape
    own = width // owners
    pairs = own // (2 * BLK)
    return pl.pallas_call(
        functools.partial(hidden_kernel, micro, pairs, scale),
        grid=(owners,),
        out_shape=jax.ShapeDtypeStruct((owners, packed_rows(pairs), BLK), jnp.bfloat16),
        in_specs=[SMEM_SPEC, pl.BlockSpec((1, micro, rows, own), lambda i: (0, 0, 0, i))],
        out_specs=pl.BlockSpec((1, packed_rows(pairs), BLK), lambda i: (i, 0, 0)),
        compiler_params=params(60 * 1024 * 1024),
        cost_estimate=pl.CostEstimate(flops=2 * micro * rows * width * 2 * BLK, bytes_accessed=6 << 20, transcendentals=0),
    )(order, hidden_grad)


def unpack_kernel(sources, pairs, in_ref, out_ref):
    row, col = iotas()
    tail = in_ref[0, pairs * BLK:].astype(jnp.float32)
    for source in range(1, sources):
        tail = tail + in_ref[source, pairs * BLK:].astype(jnp.float32)
    for pair in range(pairs):
        rows = slice(pair * BLK, (pair + 1) * BLK)
        total = in_ref[0, rows].astype(jnp.float32)
        for source in range(1, sources):
            total = total + in_ref[source, rows].astype(jnp.float32)
        turned = total.T
        out_ref[0, 2 * pair * BLK:(2 * pair + 1) * BLK] = jnp.where(col >= row, total, turned)
        second = jnp.where(col == row, tail[pair:pair + 1], turned)
        out_ref[0, (2 * pair + 1) * BLK:(2 * pair + 2) * BLK] = jnp.where(col < row, total, second)


def hidden_unpacked(packed, pairs):
    return pl.pallas_call(
        functools.partial(unpack_kernel, packed.shape[0], pairs),
        out_shape=jax.ShapeDtypeStruct((1, pairs * 2 * BLK, BLK), jnp.float32),
        in_specs=[VMEM_SPEC],
        out_specs=VMEM_SPEC,
        compiler_params=params(),
        cost_estimate=pl.CostEstimate(flops=4 << 20, bytes_accessed=3 << 20, transcendentals=0),
    )(packed)


def message_kernel(in_ref, gain_ref, repeats_ref, out_ref):
    micro, rows, part = in_ref.shape
    chunks, gain_rows = part // BLK, gain_ref.shape[0]
    gain = gain_ref[...]
    high = gain.astype(jnp.bfloat16)
    low = (gain - high.astype(jnp.float32)).astype(jnp.bfloat16)
    count = jnp.full((16, BLK), repeats_ref[0], jnp.int32).astype(jnp.float32).astype(jnp.bfloat16)
    at = chunks * rows
    for m in range(micro):
        for chunk in range(chunks):
            out_ref[m, chunk * rows:(chunk + 1) * rows] = in_ref[m, :, chunk * BLK:(chunk + 1) * BLK]
        out_ref[m, at:at + gain_rows] = high
        out_ref[m, at + gain_rows:at + 2 * gain_rows] = low
        out_ref[m, at + 2 * gain_rows:] = count


def messages(inputs, gain, repeats):
    micro, rows, part = inputs.shape
    gain_rows = gain.shape[1] // BLK
    return pl.pallas_call(
        message_kernel,
        out_shape=jax.ShapeDtypeStruct((micro, part // BLK * rows + 2 * gain_rows + 16, BLK), jnp.bfloat16),
        in_specs=[VMEM_SPEC, VMEM_SPEC, SMEM_SPEC],
        out_specs=VMEM_SPEC,
        compiler_params=params(),
        cost_estimate=pl.CostEstimate(flops=1 << 20, bytes_accessed=1 << 20, transcendentals=0),
    )(inputs, gain.reshape(gain_rows, BLK), repeats)


def relay_kernel(sections, rows, owners, in_ref, out_ref, held, gains):
    chunks, own = held.shape[0], out_ref.shape[3]
    width = chunks * BLK
    part = chunks // sections
    at = part * rows
    none = jnp.zeros((rows, BLK), jnp.float32)

    def mean(total):
        return jnp.sum(total, axis=-1, keepdims=True) * (1.0 / width)

    total = none
    for source in range(sections):
        gains[source] = in_ref[source, at:at + chunks].astype(jnp.float32) + in_ref[
            source, at + chunks:at + 2 * chunks
        ].astype(jnp.float32)
        for chunk in range(part):
            value = in_ref[source, chunk * rows:(chunk + 1) * rows].astype(jnp.float32)
            held[source * part + chunk] = value
            total = total + value
    center = mean(total)
    square = none
    for chunk in range(chunks):
        square = square + jnp.square(held[chunk] - center)
    start = (center, lax.rsqrt(mean(square) + 1e-05))

    def section(s, carry):
        repeats = jnp.max(in_ref[s, at + 2 * chunks:].astype(jnp.float32)).astype(jnp.int32)

        def apply(_, carry):
            center, scale = carry
            half = 0.5 * scale
            total, square = none, none
            for chunk in range(chunks):
                value = held[chunk]
                y = (value - center) * half * gains[s, chunk:chunk + 1]
                inner = y * (2.0 * ROOT + (8.0 * 0.044715 * ROOT) * (y * y))
                value = (value + (y + y * jnp.tanh(inner))).astype(jnp.bfloat16).astype(jnp.float32)
                held[chunk] = value
                moved = value - center
                total = total + moved
                square = square + moved * moved
            shift = mean(total)
            spread = jnp.maximum(mean(square) - shift * shift, 0.0)
            return center + shift, lax.rsqrt(spread + 1e-05)

        carry = lax.fori_loop(0, repeats + 1, apply, carry)
        center, scale = carry
        for chunk in range(owners * own // BLK):
            normed = (held[chunk] - center) * scale * gains[s, chunk:chunk + 1]
            owner, col = chunk * BLK // own, chunk * BLK % own
            out_ref[s, owner, :, col:col + BLK] = normed.astype(jnp.bfloat16)
        return carry

    lax.fori_loop(0, sections, section, start)


def relay(pieces, rows, part, owners):
    sections = pieces.shape[0]
    chunks = sections * part // BLK
    own = AWIN // owners
    return pl.pallas_call(
        functools.partial(relay_kernel, sections, rows, owners),
        out_shape=jax.ShapeDtypeStruct((sections, owners, rows, own), jnp.bfloat16),
        in_specs=[VMEM_SPEC],
        out_specs=VMEM_SPEC,
        scratch_shapes=[pltpu.VMEM((chunks, rows, BLK), jnp.float32), pltpu.VMEM((sections, chunks, BLK), jnp.float32)],
        compiler_params=params(),
        cost_estimate=pl.CostEstimate(flops=1 << 34, bytes_accessed=2 << 20, transcendentals=0),
    )(pieces)


def feature_kernel(micro, scale, order_ref, in_ref, out_ref):
    sources, rows, own = in_ref.shape
    group = sources // micro
    weights = [batch_weight(order_ref, m, micro) * scale for m in range(micro)]
    for at in range(0, own, BLK):
        total = jnp.zeros((BLK, BLK), jnp.float32)
        for m in range(micro):
            feats = in_ref[m * group:(m + 1) * group, :, at:at + BLK].reshape(group * rows, BLK)
            total = total + gram(feats, feats) * weights[m]
        out_ref[0, at:at + BLK] = total


def feature_factor(order, gathered, micro, scale):
    sources, rows, own = gathered.shape
    return pl.pallas_call(
        functools.partial(feature_kernel, micro, scale),
        out_shape=jax.ShapeDtypeStruct((1, own, BLK), jnp.float32),
        in_specs=[SMEM_SPEC, VMEM_SPEC],
        out_specs=VMEM_SPEC,
        compiler_params=params(),
        cost_estimate=pl.CostEstimate(flops=2 * sources * rows * own * BLK, bytes_accessed=1 << 20, transcendentals=0),
    )(order, gathered)


def fast_body(inputs, gain, repeats, order, hidden_grad):
    micro, tok_rows, part = inputs.shape
    dp_count = lax.axis_size("dp")
    scale = 1.0 / (tok_rows * dp_count)
    pieces = lax.all_to_all(messages(inputs, gain, repeats), "section", 0, 0, tiled=True)
    packed = hidden_packed(order, hidden_grad, dp_count, scale)
    pieces, _ = lax.optimization_barrier((pieces, packed))
    packed = lax.psum_scatter(packed.reshape(-1, BLK), "dp", scatter_dimension=0, tiled=True)
    feats = relay(pieces, tok_rows, part, dp_count)
    feats = feats.reshape((-1,) + feats.shape[2:])
    feats = lax.all_to_all(feats, ("section", "dp"), 0, 0, tiled=True)
    feature_rows = feature_factor(order, feats, micro, scale)
    hidden_rows = hidden_unpacked(packed[None], GWIN // dp_count // (2 * BLK))
    return (feature_rows, hidden_rows)


def normed(value, gain_row):
    center = jnp.mean(value, axis=-1, keepdims=True)
    spread = jnp.mean(jnp.square(value - center), axis=-1, keepdims=True)
    return (value - center) * lax.rsqrt(spread + 1e-05) * gain_row


def weighted_gram(feats, weights):
    shaped = feats.reshape(feats.shape[0], -1, BLK)
    scaled = shaped * weights[:, None, None].astype(shaped.dtype)
    return jnp.einsum("tbi,tbj->bij", scaled, shaped, preferred_element_type=jnp.float32)


def plain_body(inputs, gain, repeats, order, hidden_grad):
    micro, tok_rows, part = inputs.shape
    sections = lax.axis_size("section")
    total_tok = tok_rows * lax.axis_size("dp")
    slot_weight = 0.5 * jnp.power(0.5, micro - 1 - jnp.arange(micro, dtype=jnp.float32))
    hidden_weight = jnp.zeros((micro,), jnp.float32).at[order].set(slot_weight)
    row_weight = jnp.repeat(hidden_weight, tok_rows)
    hidden = weighted_gram(hidden_grad.reshape(micro * tok_rows, GWIN), row_weight) / total_tok
    gains = lax.all_gather(gain[0], "section", axis=0)
    counts = lax.all_gather(repeats[0], "section", axis=0)
    pieces = lax.all_to_all(inputs.reshape(micro * tok_rows, part), "section", 0, 1, tiled=True)

    def section(s, carry):
        value, feats = carry
        value = lax.fori_loop(
            0,
            counts[s] + 1,
            lambda i, v: (v + gelu(normed(v, gains[s]))).astype(jnp.bfloat16).astype(jnp.float32),
            value,
        )
        now = normed(value, gains[s]).astype(jnp.bfloat16)[:, :AWIN]
        return value, lax.dynamic_update_index_in_dim(feats, now, s, 0)

    start = jnp.zeros((sections, pieces.shape[0], AWIN), jnp.bfloat16)
    _, feats = lax.fori_loop(0, sections, section, (pieces.astype(jnp.float32), start))
    feats = lax.all_to_all(feats, "section", 0, 0, tiled=True).reshape(micro * tok_rows, AWIN)
    feature = weighted_gram(feats, row_weight) / total_tok

    def shared(term):
        term = term.reshape(-1, BLK).astype(jnp.bfloat16)
        return lax.psum_scatter(term, "dp", scatter_dimension=0, tiled=True).astype(jnp.float32)[None]

    return (shared(feature), shared(hidden))


def solution(mesh):
    sections, dp_count = mesh.shape["section"], mesh.shape["dp"]

    def body(inputs, gain, repeats, order, hidden_grad):
        aligned = (
            inputs.shape[0] == sections
            and inputs.shape[2] * sections % (16 * BLK) == 0
            and inputs.shape[1] % 16 == 0
            and AWIN % (dp_count * BLK) == 0
            and GWIN % (dp_count * 2 * BLK) == 0
        )
        return (fast_body if aligned else plain_body)(inputs, gain, repeats, order, hidden_grad)

    placed = (
        P(None, "dp", "section"),
        P("section", None),
        P("section"),
        P(),
        P("section", None, "dp", None),
    )
    return jax.shard_map(
        body,
        mesh=mesh,
        in_specs=placed,
        out_specs=(P("section", "dp", None), P("section", "dp", None)),
        check_vma=False,
    )
```

```python
import functools

import jax
import jax.numpy as jnp
from jax import lax
from jax.experimental import pallas as pl
from jax.experimental.pallas import tpu as pltpu
from jax.sharding import PartitionSpec as P

AWIN = 3072
GWIN = 12288
BLK = 128
VMEM_LIMIT = 16 * 1024 * 1024
ROOT = 0.7978845608028654

SMEM_SPEC = pl.BlockSpec(memory_space=pltpu.SMEM)
VMEM_SPEC = pl.BlockSpec(memory_space=pltpu.VMEM)


def params(limit=VMEM_LIMIT):
    return pltpu.CompilerParams(vmem_limit_bytes=limit)


def gelu(x):
    inner = ROOT * (x + 0.044715 * (x * x * x))
    return x * (0.5 * (1.0 + jnp.tanh(inner)))


def batch_weight(order_ref, batch_id, micro):
    weight = jnp.float32(0.0)
    for slot in range(micro):
        weight = jnp.where(order_ref[slot] == batch_id, jnp.float32(0.5 * 0.5 ** (micro - 1 - slot)), weight)
    return weight


def gram(left, right):
    return lax.dot_general(left, right, (((0,), (0,)), ((), ())), preferred_element_type=jnp.float32)


def iotas():
    row = lax.broadcasted_iota(jnp.int32, (BLK, BLK), 0)
    col = lax.broadcasted_iota(jnp.int32, (BLK, BLK), 1)
    return row, col


def packed_rows(pairs):
    return pairs * BLK + -(-pairs // 16) * 16


def hidden_kernel(micro, pairs, scale, order_ref, _, grad_ref, *refs):
    received, out_ref = refs[:-1], refs[-1]
    row, col = iotas()
    weights = [batch_weight(order_ref, m, micro) for m in range(micro)]
    tail = jnp.zeros((packed_rows(pairs) - pairs * BLK, BLK), jnp.float32)
    tail_row = lax.broadcasted_iota(jnp.int32, tail.shape, 0)
    for pair in range(pairs):
        both = []
        for at in (pair * 2 * BLK, pair * 2 * BLK + BLK):
            parts = [grad_ref[0, m, :, at:at + BLK] for m in range(micro)]
            scaled = [(part.astype(jnp.float32) * weight).astype(jnp.bfloat16) for part, weight in zip(parts, weights)]
            both.append(gram(jnp.concatenate(scaled, axis=0), jnp.concatenate(parts, axis=0)) * scale)
        first, second = both
        rows = slice(pair * BLK, (pair + 1) * BLK)
        packed = jnp.where(col >= row, first, second)
        for ref in received:
            packed = packed + ref[0, rows].astype(jnp.float32)
        out_ref[0, rows] = packed.astype(jnp.bfloat16)
        diagonal = jnp.sum(jnp.where(col == row, second, 0.0), axis=0, keepdims=True)
        tail = jnp.where(tail_row == pair, diagonal, tail)
    for ref in received:
        tail = tail + ref[0, pairs * BLK:].astype(jnp.float32)
    out_ref[0, pairs * BLK:] = tail.astype(jnp.bfloat16)


def hidden_terms(order, hidden_grad, me, flip, dp_count, scale, received=()):
    _, micro, rows, width = hidden_grad.shape
    own = width // dp_count
    pairs = own // (2 * BLK)
    high = packed_rows(pairs)
    packed_spec = pl.BlockSpec((1, high, BLK), lambda i, order, me: (i, 0, 0))

    def owner(i, order, me):
        return 0, 0, 0, jnp.bitwise_xor(me[0], flip + 4 - 4 * i)

    return pl.pallas_call(
        functools.partial(hidden_kernel, micro, pairs, scale),
        out_shape=jax.ShapeDtypeStruct((2, high, BLK), jnp.bfloat16),
        grid_spec=pltpu.PrefetchScalarGridSpec(
            num_scalar_prefetch=2,
            grid=(2,),
            in_specs=[pl.BlockSpec((1, micro, rows, own), owner)] + [packed_spec] * len(received),
            out_specs=packed_spec,
        ),
        compiler_params=params(60 * 1024 * 1024),
        cost_estimate=pl.CostEstimate(flops=1 << 20, bytes_accessed=1 << 10, transcendentals=0),
    )(order, me, hidden_grad, *received)


def unpack_kernel(pairs, own_ref, received_ref, out_ref):
    row, col = iotas()

    def total(rows):
        return own_ref[0, rows].astype(jnp.float32) + received_ref[0, rows].astype(jnp.float32)

    tail = total(slice(pairs * BLK, None))
    for pair in range(pairs):
        value = total(slice(pair * BLK, (pair + 1) * BLK))
        turned = value.T
        out_ref[0, 2 * pair * BLK:(2 * pair + 1) * BLK] = jnp.where(col >= row, value, turned)
        second = jnp.where(col == row, tail[pair:pair + 1], turned)
        out_ref[0, (2 * pair + 1) * BLK:(2 * pair + 2) * BLK] = jnp.where(col < row, value, second)


def unpacked(both, received, pairs):
    high = packed_rows(pairs)
    return pl.pallas_call(
        functools.partial(unpack_kernel, pairs),
        grid=(1,),
        out_shape=jax.ShapeDtypeStruct((1, pairs * 2 * BLK, BLK), jnp.float32),
        in_specs=[pl.BlockSpec((1, high, BLK), lambda i: (1, 0, 0)), pl.BlockSpec((1, high, BLK), lambda i: (0, 0, 0))],
        out_specs=pl.BlockSpec((1, pairs * 2 * BLK, BLK), lambda i: (0, 0, 0)),
        compiler_params=params(),
        cost_estimate=pl.CostEstimate(flops=1 << 20, bytes_accessed=1 << 10, transcendentals=0),
    )(both, received)


def swapped(shard, mask):
    return lax.ppermute(shard, "dp", [(i, i ^ mask) for i in range(lax.axis_size("dp"))])


def message_kernel(in_ref, gain_ref, repeats_ref, out_ref):
    micro, rows, part = in_ref.shape
    chunks, gain_rows = part // BLK, gain_ref.shape[0]
    gain = gain_ref[...]
    high = gain.astype(jnp.bfloat16)
    low = (gain - high.astype(jnp.float32)).astype(jnp.bfloat16)
    count = jnp.full((16, BLK), repeats_ref[0], jnp.int32).astype(jnp.float32).astype(jnp.bfloat16)
    at = chunks * rows
    for m in range(micro):
        for chunk in range(chunks):
            out_ref[m, chunk * rows:(chunk + 1) * rows] = in_ref[m, :, chunk * BLK:(chunk + 1) * BLK]
        out_ref[m, at:at + gain_rows] = high
        out_ref[m, at + gain_rows:at + 2 * gain_rows] = low
        out_ref[m, at + 2 * gain_rows:] = count


def messages(inputs, gain, repeats):
    micro, rows, part = inputs.shape
    gain_rows = gain.shape[1] // BLK
    return pl.pallas_call(
        message_kernel,
        out_shape=jax.ShapeDtypeStruct((micro, part // BLK * rows + 2 * gain_rows + 16, BLK), jnp.bfloat16),
        in_specs=[VMEM_SPEC, VMEM_SPEC, SMEM_SPEC],
        out_specs=VMEM_SPEC,
        compiler_params=params(60 * 1024 * 1024),
        cost_estimate=pl.CostEstimate(flops=1 << 20, bytes_accessed=1 << 20, transcendentals=0),
    )(inputs, gain.reshape(gain_rows, BLK), repeats)


def relay_kernel(sections, rows, owners, in_ref, out_ref, held, gains):
    chunks, own = held.shape[0], out_ref.shape[3]
    width = chunks * BLK
    part = chunks // sections
    at = part * rows
    none = jnp.zeros((rows, BLK), jnp.float32)

    def mean(total):
        return jnp.sum(total, axis=-1, keepdims=True) * (1.0 / width)

    total = none
    for source in range(sections):
        gains[source] = in_ref[source, at:at + chunks].astype(jnp.float32) + in_ref[
            source, at + chunks:at + 2 * chunks
        ].astype(jnp.float32)
        for chunk in range(part):
            value = in_ref[source, chunk * rows:(chunk + 1) * rows].astype(jnp.float32)
            held[source * part + chunk] = value
            total = total + value
    center = mean(total)
    square = none
    for chunk in range(chunks):
        square = square + jnp.square(held[chunk] - center)
    start = (center, lax.rsqrt(mean(square) + 1e-05))

    def section(s, carry):
        repeats = jnp.max(in_ref[s, at + 2 * chunks:].astype(jnp.float32)).astype(jnp.int32)

        def apply(_, carry):
            center, scale = carry
            half = 0.5 * scale
            total, square = none, none
            for chunk in range(chunks):
                value = held[chunk]
                y = (value - center) * half * gains[s, chunk:chunk + 1]
                inner = y * (2.0 * ROOT + (8.0 * 0.044715 * ROOT) * (y * y))
                value = (value + (y + y * jnp.tanh(inner))).astype(jnp.bfloat16).astype(jnp.float32)
                held[chunk] = value
                moved = value - center
                total = total + moved
                square = square + moved * moved
            shift = mean(total)
            spread = jnp.maximum(mean(square) - shift * shift, 0.0)
            return center + shift, lax.rsqrt(spread + 1e-05)

        carry = lax.fori_loop(0, repeats + 1, apply, carry)
        center, scale = carry
        for chunk in range(owners * own // BLK):
            normed = (held[chunk] - center) * scale * gains[s, chunk:chunk + 1]
            owner, col = chunk * BLK // own, chunk * BLK % own
            out_ref[s, owner, :, col:col + BLK] = normed.astype(jnp.bfloat16)
        return carry

    lax.fori_loop(0, sections, section, start)


def relay(pieces, rows, part, owners):
    sections = pieces.shape[0]
    chunks = sections * part // BLK
    own = AWIN // owners
    return pl.pallas_call(
        functools.partial(relay_kernel, sections, rows, owners),
        out_shape=jax.ShapeDtypeStruct((sections, owners, rows, own), jnp.bfloat16),
        in_specs=[VMEM_SPEC],
        out_specs=VMEM_SPEC,
        scratch_shapes=[pltpu.VMEM((chunks, rows, BLK), jnp.float32), pltpu.VMEM((sections, chunks, BLK), jnp.float32)],
        compiler_params=params(),
        cost_estimate=pl.CostEstimate(flops=1 << 33, bytes_accessed=2 << 20, transcendentals=0),
    )(pieces)


def feature_kernel(micro, scale, order_ref, in_ref, out_ref):
    sources, rows, own = in_ref.shape
    group = sources // micro
    weights = [batch_weight(order_ref, m, micro) * scale for m in range(micro)]
    for at in range(0, own, BLK):
        total = jnp.zeros((BLK, BLK), jnp.float32)
        for m in range(micro):
            feats = in_ref[m * group:(m + 1) * group, :, at:at + BLK].reshape(group * rows, BLK)
            total = total + gram(feats, feats) * weights[m]
        out_ref[0, at:at + BLK] = total


def feature_factor(order, gathered, micro, scale):
    sources, rows, own = gathered.shape
    return pl.pallas_call(
        functools.partial(feature_kernel, micro, scale),
        out_shape=jax.ShapeDtypeStruct((1, own, BLK), jnp.float32),
        in_specs=[SMEM_SPEC, VMEM_SPEC],
        out_specs=VMEM_SPEC,
        compiler_params=params(),
        cost_estimate=pl.CostEstimate(flops=2 * sources * rows * own * BLK, bytes_accessed=1 << 20, transcendentals=0),
    )(order, gathered)


def fast_body(inputs, gain, repeats, order, hidden_grad):
    micro, tok_rows, part = inputs.shape
    dp_count = lax.axis_size("dp")
    scale = 1.0 / (tok_rows * dp_count)
    told, order = lax.optimization_barrier((messages(inputs, gain, repeats), order))
    pieces = lax.all_to_all(told, "section", 0, 0, tiled=True)

    me = lax.axis_index("dp").reshape(1)
    terms = functools.partial(hidden_terms, hidden_grad=hidden_grad, dp_count=dp_count, scale=scale)
    sent = terms(order, me=me, flip=2, received=(swapped(terms(order, me=me, flip=3), 1),))
    came = swapped(sent, 2)
    pieces, _ = lax.optimization_barrier((pieces, sent))
    feats, came, order = lax.optimization_barrier((relay(pieces, tok_rows, part, dp_count), came, order))
    feats = feats.reshape((-1,) + feats.shape[2:])
    feats = lax.all_to_all(feats, ("section", "dp"), 0, 0, tiled=True)
    both = terms(order, me=me, flip=0, received=(swapped(terms(order, me=me, flip=1), 1), came))
    hidden_rows = unpacked(both, swapped(both[:1], 4), GWIN // dp_count // (2 * BLK))
    feature_rows = feature_factor(order, feats, micro, scale)
    return (feature_rows, hidden_rows)


def normed(value, gain_row):
    center = jnp.mean(value, axis=-1, keepdims=True)
    spread = jnp.mean(jnp.square(value - center), axis=-1, keepdims=True)
    return (value - center) * lax.rsqrt(spread + 1e-05) * gain_row


def weighted_gram(feats, weights):
    shaped = feats.reshape(feats.shape[0], -1, BLK)
    scaled = shaped * weights[:, None, None].astype(shaped.dtype)
    return jnp.einsum("tbi,tbj->bij", scaled, shaped, preferred_element_type=jnp.float32)


def plain_body(inputs, gain, repeats, order, hidden_grad):
    micro, tok_rows, part = inputs.shape
    sections = lax.axis_size("section")
    total_tok = tok_rows * lax.axis_size("dp")
    slot_weight = 0.5 * jnp.power(0.5, micro - 1 - jnp.arange(micro, dtype=jnp.float32))
    hidden_weight = jnp.zeros((micro,), jnp.float32).at[order].set(slot_weight)
    row_weight = jnp.repeat(hidden_weight, tok_rows)
    hidden = weighted_gram(hidden_grad.reshape(micro * tok_rows, GWIN), row_weight) / total_tok
    gains = lax.all_gather(gain[0], "section", axis=0)
    counts = lax.all_gather(repeats[0], "section", axis=0)
    pieces = lax.all_to_all(inputs.reshape(micro * tok_rows, part), "section", 0, 1, tiled=True)

    def section(s, carry):
        value, feats = carry
        value = lax.fori_loop(
            0,
            counts[s] + 1,
            lambda i, v: (v + gelu(normed(v, gains[s]))).astype(jnp.bfloat16).astype(jnp.float32),
            value,
        )
        now = normed(value, gains[s]).astype(jnp.bfloat16)[:, :AWIN]
        return value, lax.dynamic_update_index_in_dim(feats, now, s, 0)

    start = jnp.zeros((sections, pieces.shape[0], AWIN), jnp.bfloat16)
    _, feats = lax.fori_loop(0, sections, section, (pieces.astype(jnp.float32), start))
    feats = lax.all_to_all(feats, "section", 0, 0, tiled=True).reshape(micro * tok_rows, AWIN)
    feature = weighted_gram(feats, row_weight) / total_tok

    def shared(term):
        term = term.reshape(-1, BLK).astype(jnp.bfloat16)
        return lax.psum_scatter(term, "dp", scatter_dimension=0, tiled=True).astype(jnp.float32)[None]

    return (shared(feature), shared(hidden))


def solution(mesh):
    sections, dp_count = mesh.shape["section"], mesh.shape["dp"]

    def body(inputs, gain, repeats, order, hidden_grad):
        aligned = (
            inputs.shape[0] == sections
            and inputs.shape[2] * sections % (16 * BLK) == 0
            and inputs.shape[1] % 16 == 0
            and dp_count == 8
            and AWIN % (dp_count * BLK) == 0
            and GWIN % (dp_count * 2 * BLK) == 0
        )
        return (fast_body if aligned else plain_body)(inputs, gain, repeats, order, hidden_grad)

    placed = (
        P(None, "dp", "section"),
        P("section", None),
        P("section"),
        P(),
        P("section", None, "dp", None),
    )
    return jax.shard_map(
        body,
        mesh=mesh,
        in_specs=placed,
        out_specs=(P("section", "dp", None), P("section", "dp", None)),
        check_vma=False,
    )
```

```python
import functools

import jax
import jax.numpy as jnp
from jax import lax
from jax.experimental import pallas as pl
from jax.experimental.pallas import tpu as pltpu
from jax.sharding import PartitionSpec as P

AWIN = 3072
GWIN = 12288
BLK = 128
VMEM_LIMIT = 16 * 1024 * 1024
HIDDEN_COST = 1 << 31
ROOT = 0.7978845608028654

SMEM_SPEC = pl.BlockSpec(memory_space=pltpu.SMEM)
VMEM_SPEC = pl.BlockSpec(memory_space=pltpu.VMEM)


def params(limit=VMEM_LIMIT):
    return pltpu.CompilerParams(vmem_limit_bytes=limit)


def gelu(x):
    inner = ROOT * (x + 0.044715 * (x * x * x))
    return x * (0.5 * (1.0 + jnp.tanh(inner)))


def batch_weight(order_ref, batch_id, micro):
    weight = jnp.float32(0.0)
    for slot in range(micro):
        weight = jnp.where(order_ref[slot] == batch_id, jnp.float32(0.5 * 0.5 ** (micro - 1 - slot)), weight)
    return weight


def gram(left, right):
    return lax.dot_general(left, right, (((0,), (0,)), ((), ())), preferred_element_type=jnp.float32)


def iotas():
    row = lax.broadcasted_iota(jnp.int32, (BLK, BLK), 0)
    col = lax.broadcasted_iota(jnp.int32, (BLK, BLK), 1)
    return row, col


def packed_rows(pairs):
    return pairs * BLK + -(-pairs // 16) * 16


def hidden_kernel(micro, pairs, scale, order_ref, _, grad_ref, far_ref, near_ref):
    row, col = iotas()
    weights = [batch_weight(order_ref, m, micro) for m in range(micro)]
    far = pl.program_id(0) < pl.num_programs(0) // 2
    tail_row = lax.broadcasted_iota(jnp.int32, (packed_rows(pairs) - pairs * BLK, BLK), 0)

    def store(half, rows, value):
        @pl.when(far)
        def _():
            far_ref[0, half, rows] = value

        @pl.when(jnp.logical_not(far))
        def _():
            near_ref[0, half, rows] = value

    for half in range(2):
        tail = jnp.zeros(tail_row.shape, jnp.float32)
        for pair in range(pairs):
            at = (half * pairs + pair) * 2 * BLK
            parts = [grad_ref[0, m, :, at:at + 2 * BLK] for m in range(micro)]
            scaled = [(part.astype(jnp.float32) * weight).astype(jnp.bfloat16) for part, weight in zip(parts, weights)]
            both = gram(jnp.concatenate(scaled, axis=0), jnp.concatenate(parts, axis=0)) * scale
            first, second = both[:BLK, :BLK], both[BLK:, BLK:]
            packed = jnp.where(col >= row, first, second).astype(jnp.bfloat16)
            store(half, slice(pair * BLK, (pair + 1) * BLK), packed)
            diagonal = jnp.sum(jnp.where(col == row, second, 0.0), axis=0, keepdims=True)
            tail = jnp.where(tail_row == pair, diagonal, tail)
        store(half, slice(pairs * BLK, None), tail.astype(jnp.bfloat16))


def hidden_terms(order, hidden_grad, me, dp_count, scale):
    _, micro, rows, width = hidden_grad.shape
    own = width // dp_count
    pairs = own // (4 * BLK)
    shape, half = (2, packed_rows(pairs), BLK), dp_count // 2

    def owner(i, order, me):
        return 0, 0, 0, jnp.bitwise_xor(me[0], 7 - i // half - 2 * (i // 2 % 2) - 4 * (i % 2))

    return pl.pallas_call(
        functools.partial(hidden_kernel, micro, pairs, scale),
        out_shape=(jax.ShapeDtypeStruct((half,) + shape, jnp.bfloat16),) * 2,
        grid_spec=pltpu.PrefetchScalarGridSpec(
            num_scalar_prefetch=2,
            grid=(dp_count,),
            in_specs=[pl.BlockSpec((1, micro, rows, own), owner)],
            out_specs=(
                pl.BlockSpec((1,) + shape, lambda i, order, me: (jnp.minimum(i, half - 1), 0, 0, 0)),
                pl.BlockSpec((1,) + shape, lambda i, order, me: (jnp.maximum(i - half, 0), 0, 0, 0)),
            ),
        ),
        compiler_params=params(),
        cost_estimate=pl.CostEstimate(flops=HIDDEN_COST, bytes_accessed=1 << 10, transcendentals=0),
    )(order, me, hidden_grad)


def small_call(kernel, shapes, *operands):
    return pl.pallas_call(
        kernel,
        out_shape=shapes,
        in_specs=[VMEM_SPEC] * len(operands),
        out_specs=jax.tree.map(lambda _: VMEM_SPEC, shapes),
        compiler_params=params(),
        cost_estimate=pl.CostEstimate(flops=1 << 20, bytes_accessed=1 << 10, transcendentals=0),
    )(*operands)


def core_sum_kernel(near_ref, came_ref, along_x_ref, along_y_ref, first_ref, second_ref):
    def total(place, half):
        return near_ref[place, half].astype(jnp.float32) + came_ref[place, half].astype(jnp.float32)

    for i in range(2):
        along_x_ref[i] = total(i, 0).astype(jnp.bfloat16)
        along_y_ref[i] = total(2 * i, 1).astype(jnp.bfloat16)
        first_ref[i] = total(2 + i, 0)
        second_ref[i] = total(1 + 2 * i, 1)


def pair_sum_kernel(first_ref, came_x_ref, second_ref, came_y_ref, along_y_ref, along_x_ref, kept_ref):
    along_y_ref[...] = (first_ref[0] + came_x_ref[0].astype(jnp.float32)).astype(jnp.bfloat16)
    along_x_ref[...] = (second_ref[0] + came_y_ref[0].astype(jnp.float32)).astype(jnp.bfloat16)
    kept_ref[0] = first_ref[1] + came_x_ref[1].astype(jnp.float32)
    kept_ref[1] = second_ref[1] + came_y_ref[1].astype(jnp.float32)


def unpack_kernel(pairs, kept_ref, came_y_ref, came_x_ref, out_ref):
    row, col = iotas()
    for half, came_ref in enumerate((came_y_ref, came_x_ref)):

        def total(rows):
            return kept_ref[half, rows] + came_ref[rows].astype(jnp.float32)

        tail = total(slice(pairs * BLK, None))
        for pair in range(pairs):
            value = total(slice(pair * BLK, (pair + 1) * BLK))
            turned = value.T
            at = (half * pairs + pair) * 2 * BLK
            out_ref[0, at:at + BLK] = jnp.where(col >= row, value, turned)
            second = jnp.where(col == row, tail[pair:pair + 1], turned)
            out_ref[0, at + BLK:at + 2 * BLK] = jnp.where(col < row, value, second)


def hidden_factor(near, came):
    rows = near.shape[2]
    pairs = rows // BLK
    one = (rows, BLK)
    sent = jax.ShapeDtypeStruct((2,) + one, jnp.bfloat16)
    kept = jax.ShapeDtypeStruct((2,) + one, jnp.float32)
    along_x, along_y, first, second = small_call(core_sum_kernel, (sent, sent, kept, kept), near, came)
    last = jax.ShapeDtypeStruct(one, jnp.bfloat16)
    along_y, along_x, own = small_call(
        pair_sum_kernel, (last, last, kept), first, swapped(along_x, "dp", 2), second, swapped(along_y, "dp", 4)
    )
    out = jax.ShapeDtypeStruct((1, 4 * pairs * BLK, BLK), jnp.float32)
    return small_call(
        functools.partial(unpack_kernel, pairs), out, own, swapped(along_y, "dp", 4), swapped(along_x, "dp", 2)
    )


def swapped(shard, axis, mask):
    return lax.ppermute(shard, axis, [(i, i ^ mask) for i in range(lax.axis_size(axis))])


def message_kernel(in_ref, gain_ref, repeats_ref, me_ref, *out_refs):
    _, rows, part = in_ref.shape
    chunks, gain_rows = part // BLK, gain_ref.shape[0]
    gain = gain_ref[...]
    high = gain.astype(jnp.bfloat16)
    low = (gain - high.astype(jnp.float32)).astype(jnp.bfloat16)
    count = jnp.full((16, BLK), repeats_ref[0], jnp.int32).astype(jnp.float32).astype(jnp.bfloat16)
    at = chunks * rows
    for mask, out_ref in enumerate(out_refs, 1):
        target = jnp.bitwise_xor(me_ref[0], mask)
        for chunk in range(chunks):
            out_ref[chunk * rows:(chunk + 1) * rows] = in_ref[target, :, chunk * BLK:(chunk + 1) * BLK]
        out_ref[at:at + gain_rows] = high
        out_ref[at + gain_rows:at + 2 * gain_rows] = low
        out_ref[at + 2 * gain_rows:] = count


def messages(inputs, gain, repeats, me):
    micro, rows, part = inputs.shape
    shape = jax.ShapeDtypeStruct((part // BLK * rows + 2 * gain.shape[0] + 16, BLK), jnp.bfloat16)
    return pl.pallas_call(
        message_kernel,
        out_shape=(shape,) * (micro - 1),
        in_specs=[VMEM_SPEC, VMEM_SPEC, SMEM_SPEC, SMEM_SPEC],
        out_specs=(VMEM_SPEC,) * (micro - 1),
        compiler_params=params(60 * 1024 * 1024),
        cost_estimate=pl.CostEstimate(flops=1 << 20, bytes_accessed=1 << 20, transcendentals=0),
    )(inputs, gain, repeats, me)


def relay_kernel(sections, owners, own_ref, gain_ref, repeats_ref, me_ref, *refs):
    received, (out_ref, held, gains) = refs[:-3], refs[-3:]
    chunks, rows, _ = held.shape
    own = out_ref.shape[3]
    width = chunks * BLK
    part = chunks // sections
    at = part * rows
    me = me_ref[0]
    none = jnp.zeros((rows, BLK), jnp.float32)

    def mean(total):
        return jnp.sum(total, axis=-1, keepdims=True) * (1.0 / width)

    gains[me, :chunks] = gain_ref[...]
    gains[me, chunks:] = jnp.full((8, BLK), repeats_ref[0], jnp.int32).astype(jnp.float32)
    total = none
    for chunk in range(part):
        value = own_ref[me, :, chunk * BLK:(chunk + 1) * BLK].astype(jnp.float32)
        held[me * part + chunk] = value
        total = total + value
    for mask, ref in enumerate(received, 1):
        source = jnp.bitwise_xor(me, mask)
        gains[source, :chunks] = ref[at:at + chunks].astype(jnp.float32) + ref[at + chunks:at + 2 * chunks].astype(jnp.float32)
        gains[source, chunks:] = ref[at + 2 * chunks:].astype(jnp.float32)[:8]
        for chunk in range(part):
            value = ref[chunk * rows:(chunk + 1) * rows].astype(jnp.float32)
            held[source * part + chunk] = value
            total = total + value
    center = mean(total)
    square = none
    for chunk in range(chunks):
        square = square + jnp.square(held[chunk] - center)
    start = (center, lax.rsqrt(mean(square) + 1e-05))

    def section(s, carry):
        repeats = jnp.max(gains[s, chunks:]).astype(jnp.int32)

        def apply(_, carry):
            center, scale = carry
            half = 0.5 * scale
            total, square = none, none
            for chunk in range(chunks):
                value = held[chunk]
                y = (value - center) * half * gains[s, chunk:chunk + 1]
                inner = y * (2.0 * ROOT + (8.0 * 0.044715 * ROOT) * (y * y))
                value = (value + (y + y * jnp.tanh(inner))).astype(jnp.bfloat16).astype(jnp.float32)
                held[chunk] = value
                moved = value - center
                total = total + moved
                square = square + moved * moved
            shift = mean(total)
            spread = jnp.maximum(mean(square) - shift * shift, 0.0)
            return center + shift, lax.rsqrt(spread + 1e-05)

        carry = lax.fori_loop(0, repeats + 1, apply, carry)
        center, scale = carry
        for chunk in range(owners * own // BLK):
            normed = (held[chunk] - center) * scale * gains[s, chunk:chunk + 1]
            owner, col = chunk * BLK // own, chunk * BLK % own
            out_ref[s, owner, :, col:col + BLK] = normed.astype(jnp.bfloat16)
        return carry

    lax.fori_loop(0, sections, section, start)


def relay(inputs, gain, repeats, me, received, owners):
    sections, rows, part = inputs.shape
    chunks = sections * part // BLK
    own = AWIN // owners
    return pl.pallas_call(
        functools.partial(relay_kernel, sections, owners),
        out_shape=jax.ShapeDtypeStruct((sections, owners, rows, own), jnp.bfloat16),
        in_specs=[VMEM_SPEC, VMEM_SPEC, SMEM_SPEC, SMEM_SPEC] + [VMEM_SPEC] * len(received),
        out_specs=VMEM_SPEC,
        scratch_shapes=[pltpu.VMEM((chunks, rows, BLK), jnp.float32), pltpu.VMEM((sections, chunks + 8, BLK), jnp.float32)],
        compiler_params=params(),
        cost_estimate=pl.CostEstimate(flops=1 << 33, bytes_accessed=2 << 20, transcendentals=0),
    )(inputs, gain, repeats, me, *received)


def feature_kernel(micro, scale, order_ref, in_ref, out_ref):
    sources, rows, own = in_ref.shape
    group = sources // micro
    weights = [batch_weight(order_ref, m, micro) * scale for m in range(micro)]
    for at in range(0, own, BLK):
        total = jnp.zeros((BLK, BLK), jnp.float32)
        for m in range(micro):
            feats = in_ref[m * group:(m + 1) * group, :, at:at + BLK].reshape(group * rows, BLK)
            total = total + gram(feats, feats) * weights[m]
        out_ref[0, at:at + BLK] = total


def feature_factor(order, gathered, micro, scale):
    sources, rows, own = gathered.shape
    return pl.pallas_call(
        functools.partial(feature_kernel, micro, scale),
        out_shape=jax.ShapeDtypeStruct((1, own, BLK), jnp.float32),
        in_specs=[SMEM_SPEC, VMEM_SPEC],
        out_specs=VMEM_SPEC,
        compiler_params=params(),
        cost_estimate=pl.CostEstimate(flops=2 * sources * rows * own * BLK, bytes_accessed=1 << 20, transcendentals=0),
    )(order, gathered)


def fast_body(inputs, gain, repeats, order, hidden_grad):
    micro, tok_rows, _ = inputs.shape
    dp_count = lax.axis_size("dp")
    scale = 1.0 / (tok_rows * dp_count)
    gain = gain.reshape(-1, BLK)
    plane = lax.axis_index("section").reshape(1)
    told, order = lax.optimization_barrier((messages(inputs, gain, repeats, plane), order))
    pieces = tuple(swapped(one, "section", mask) for mask, one in enumerate(told, 1))

    far, near = hidden_terms(order, hidden_grad, lax.axis_index("dp").reshape(1), dp_count, scale)
    came = swapped(far, "dp", 1)
    pieces, near = lax.optimization_barrier((pieces, near))
    feats = relay(inputs, gain, repeats, plane, pieces, dp_count)
    feats, near, came, order = lax.optimization_barrier((feats, near, came, order))
    feats = feats.reshape((-1,) + feats.shape[2:])
    feats = lax.all_to_all(feats, ("section", "dp"), 0, 0, tiled=True)
    hidden_rows = hidden_factor(near, came)
    feature_rows = feature_factor(order, feats, micro, scale)
    return (feature_rows, hidden_rows)


def normed(value, gain_row):
    center = jnp.mean(value, axis=-1, keepdims=True)
    spread = jnp.mean(jnp.square(value - center), axis=-1, keepdims=True)
    return (value - center) * lax.rsqrt(spread + 1e-05) * gain_row


def weighted_gram(feats, weights):
    shaped = feats.reshape(feats.shape[0], -1, BLK)
    scaled = shaped * weights[:, None, None].astype(shaped.dtype)
    return jnp.einsum("tbi,tbj->bij", scaled, shaped, preferred_element_type=jnp.float32)


def plain_body(inputs, gain, repeats, order, hidden_grad):
    micro, tok_rows, part = inputs.shape
    sections = lax.axis_size("section")
    total_tok = tok_rows * lax.axis_size("dp")
    slot_weight = 0.5 * jnp.power(0.5, micro - 1 - jnp.arange(micro, dtype=jnp.float32))
    hidden_weight = jnp.zeros((micro,), jnp.float32).at[order].set(slot_weight)
    row_weight = jnp.repeat(hidden_weight, tok_rows)
    hidden = weighted_gram(hidden_grad.reshape(micro * tok_rows, GWIN), row_weight) / total_tok
    gains = lax.all_gather(gain[0], "section", axis=0)
    counts = lax.all_gather(repeats[0], "section", axis=0)
    pieces = lax.all_to_all(inputs.reshape(micro * tok_rows, part), "section", 0, 1, tiled=True)

    def section(s, carry):
        value, feats = carry
        value = lax.fori_loop(
            0,
            counts[s] + 1,
            lambda i, v: (v + gelu(normed(v, gains[s]))).astype(jnp.bfloat16).astype(jnp.float32),
            value,
        )
        now = normed(value, gains[s]).astype(jnp.bfloat16)[:, :AWIN]
        return value, lax.dynamic_update_index_in_dim(feats, now, s, 0)

    start = jnp.zeros((sections, pieces.shape[0], AWIN), jnp.bfloat16)
    _, feats = lax.fori_loop(0, sections, section, (pieces.astype(jnp.float32), start))
    feats = lax.all_to_all(feats, "section", 0, 0, tiled=True).reshape(micro * tok_rows, AWIN)
    feature = weighted_gram(feats, row_weight) / total_tok

    def shared(term):
        term = term.reshape(-1, BLK).astype(jnp.bfloat16)
        return lax.psum_scatter(term, "dp", scatter_dimension=0, tiled=True).astype(jnp.float32)[None]

    return (shared(feature), shared(hidden))


def solution(mesh):
    sections, dp_count = mesh.shape["section"], mesh.shape["dp"]

    def body(inputs, gain, repeats, order, hidden_grad):
        aligned = (
            inputs.shape[0] == sections == 4
            and inputs.shape[2] * sections % (16 * BLK) == 0
            and inputs.shape[1] % 16 == 0
            and dp_count == 8
            and AWIN % (dp_count * BLK) == 0
            and GWIN % (dp_count * 4 * BLK) == 0
        )
        return (fast_body if aligned else plain_body)(inputs, gain, repeats, order, hidden_grad)

    placed = (
        P(None, "dp", "section"),
        P("section", None),
        P("section"),
        P(),
        P("section", None, "dp", None),
    )
    return jax.shard_map(
        body,
        mesh=mesh,
        in_specs=placed,
        out_specs=(P("section", "dp", None), P("section", "dp", None)),
        check_vma=False,
    )
```

```python
import functools

import jax
import jax.numpy as jnp
from jax import lax
from jax.experimental import pallas as pl
from jax.experimental.pallas import tpu as pltpu
from jax.sharding import PartitionSpec as P

AWIN = 3072
GWIN = 12288
BLK = 128
VMEM_LIMIT = 16 * 1024 * 1024
HIDDEN_COST = 1 << 31
ROOT = 0.7978845608028654

SMEM_SPEC = pl.BlockSpec(memory_space=pltpu.SMEM)
VMEM_SPEC = pl.BlockSpec(memory_space=pltpu.VMEM)


def params(limit=VMEM_LIMIT):
    return pltpu.CompilerParams(vmem_limit_bytes=limit)


def gelu(x):
    inner = ROOT * (x + 0.044715 * (x * x * x))
    return x * (0.5 * (1.0 + jnp.tanh(inner)))


def batch_weight(order_ref, batch_id, micro):
    weight = jnp.float32(0.0)
    for slot in range(micro):
        weight = jnp.where(order_ref[slot] == batch_id, jnp.float32(0.5 * 0.5 ** (micro - 1 - slot)), weight)
    return weight


def gram(left, right):
    return lax.dot_general(left, right, (((0,), (0,)), ((), ())), preferred_element_type=jnp.float32)


def iotas():
    row = lax.broadcasted_iota(jnp.int32, (BLK, BLK), 0)
    col = lax.broadcasted_iota(jnp.int32, (BLK, BLK), 1)
    return row, col


def packed_rows(pairs):
    return pairs * BLK + -(-pairs // 16) * 16


def hidden_kernel(micro, pairs, scale, order_ref, _, far_grad_ref, near_grad_ref, far_ref, near_ref):
    row, col = iotas()
    weights = [batch_weight(order_ref, m, micro) for m in range(micro)]
    tail_row = lax.broadcasted_iota(jnp.int32, (packed_rows(pairs) - pairs * BLK, BLK), 0)
    for grad_ref, out_ref in ((far_grad_ref, far_ref), (near_grad_ref, near_ref)):
        for half in range(2):
            tail = jnp.zeros(tail_row.shape, jnp.float32)
            for pair in range(pairs):
                at = (half * pairs + pair) * 2 * BLK
                parts = [grad_ref[0, m, :, at:at + 2 * BLK] for m in range(micro)]
                scaled = [(part.astype(jnp.float32) * weight).astype(jnp.bfloat16) for part, weight in zip(parts, weights)]
                both = gram(jnp.concatenate(scaled, axis=0), jnp.concatenate(parts, axis=0)) * scale
                first, second = both[:BLK, :BLK], both[BLK:, BLK:]
                out_ref[0, half, pair * BLK:(pair + 1) * BLK] = jnp.where(col >= row, first, second).astype(jnp.bfloat16)
                diagonal = jnp.sum(jnp.where(col == row, second, 0.0), axis=0, keepdims=True)
                tail = jnp.where(tail_row == pair, diagonal, tail)
            out_ref[0, half, pairs * BLK:] = tail.astype(jnp.bfloat16)


def hidden_terms(order, hidden_grad, me, dp_count, scale):
    _, micro, rows, width = hidden_grad.shape
    own = width // dp_count
    pairs = own // (4 * BLK)
    shape, count = (2, packed_rows(pairs), BLK), dp_count // 2

    def owner(flip):
        return lambda i, order, me: (0, 0, 0, jnp.bitwise_xor(me[0], 6 + flip - 2 * (i // 2) - 4 * (i % 2)))

    out_spec = pl.BlockSpec((1,) + shape, lambda i, order, me: (i, 0, 0, 0))
    return pl.pallas_call(
        functools.partial(hidden_kernel, micro, pairs, scale),
        out_shape=(jax.ShapeDtypeStruct((count,) + shape, jnp.bfloat16),) * 2,
        grid_spec=pltpu.PrefetchScalarGridSpec(
            num_scalar_prefetch=2,
            grid=(count,),
            in_specs=[pl.BlockSpec((1, micro, rows, own), owner(1)), pl.BlockSpec((1, micro, rows, own), owner(0))],
            out_specs=(out_spec, out_spec),
        ),
        compiler_params=params(),
        cost_estimate=pl.CostEstimate(flops=HIDDEN_COST, bytes_accessed=1 << 10, transcendentals=0),
    )(order, me, hidden_grad, hidden_grad)


def small_call(kernel, shapes, *operands):
    return pl.pallas_call(
        kernel,
        out_shape=shapes,
        in_specs=[VMEM_SPEC] * len(operands),
        out_specs=jax.tree.map(lambda _: VMEM_SPEC, shapes),
        compiler_params=params(),
        cost_estimate=pl.CostEstimate(flops=1 << 20, bytes_accessed=1 << 10, transcendentals=0),
    )(*operands)


def core_sum_kernel(near_ref, came_ref, along_x_ref, along_y_ref, first_ref, second_ref):
    def total(place, half):
        return near_ref[place, half].astype(jnp.float32) + came_ref[place, half].astype(jnp.float32)

    for i in range(2):
        along_x_ref[i] = total(i, 0).astype(jnp.bfloat16)
        along_y_ref[i] = total(2 * i, 1).astype(jnp.bfloat16)
        first_ref[i] = total(2 + i, 0)
        second_ref[i] = total(1 + 2 * i, 1)


def pair_sum_kernel(first_ref, came_x_ref, second_ref, came_y_ref, along_y_ref, along_x_ref, kept_ref):
    along_y_ref[...] = (first_ref[0] + came_x_ref[0].astype(jnp.float32)).astype(jnp.bfloat16)
    along_x_ref[...] = (second_ref[0] + came_y_ref[0].astype(jnp.float32)).astype(jnp.bfloat16)
    kept_ref[0] = first_ref[1] + came_x_ref[1].astype(jnp.float32)
    kept_ref[1] = second_ref[1] + came_y_ref[1].astype(jnp.float32)


def unpack_kernel(pairs, kept_ref, came_y_ref, came_x_ref, out_ref):
    row, col = iotas()
    for half, came_ref in enumerate((came_y_ref, came_x_ref)):

        def total(rows):
            return kept_ref[half, rows] + came_ref[rows].astype(jnp.float32)

        tail = total(slice(pairs * BLK, None))
        for pair in range(pairs):
            value = total(slice(pair * BLK, (pair + 1) * BLK))
            turned = value.T
            at = (half * pairs + pair) * 2 * BLK
            out_ref[0, at:at + BLK] = jnp.where(col >= row, value, turned)
            second = jnp.where(col == row, tail[pair:pair + 1], turned)
            out_ref[0, at + BLK:at + 2 * BLK] = jnp.where(col < row, value, second)


def core_sum(near, came):
    one = near.shape[2:]
    sent = jax.ShapeDtypeStruct((2,) + one, jnp.bfloat16)
    kept = jax.ShapeDtypeStruct((2,) + one, jnp.float32)
    return small_call(core_sum_kernel, (sent, sent, kept, kept), near, came)


def pair_sum(first, came_x, second, came_y):
    last = jax.ShapeDtypeStruct(first.shape[1:], jnp.bfloat16)
    return small_call(pair_sum_kernel, (last, last, first), first, came_x, second, came_y)


def unpacked(kept, came_y, came_x):
    pairs = kept.shape[1] // BLK
    out = jax.ShapeDtypeStruct((1, 4 * pairs * BLK, BLK), jnp.float32)
    return small_call(functools.partial(unpack_kernel, pairs), out, kept, came_y, came_x)


def swapped(shard, axis, mask):
    return lax.ppermute(shard, axis, [(i, i ^ mask) for i in range(lax.axis_size(axis))])


def message_kernel(in_ref, gain_ref, repeats_ref, me_ref, *out_refs):
    _, rows, part = in_ref.shape
    chunks, gain_rows = part // BLK, gain_ref.shape[0]
    gain = gain_ref[...]
    high = gain.astype(jnp.bfloat16)
    low = (gain - high.astype(jnp.float32)).astype(jnp.bfloat16)
    count = jnp.full((16, BLK), repeats_ref[0], jnp.int32).astype(jnp.float32).astype(jnp.bfloat16)
    at = chunks * rows
    for mask, out_ref in enumerate(out_refs, 1):
        target = jnp.bitwise_xor(me_ref[0], mask)
        for chunk in range(chunks):
            out_ref[chunk * rows:(chunk + 1) * rows] = in_ref[target, :, chunk * BLK:(chunk + 1) * BLK]
        out_ref[at:at + gain_rows] = high
        out_ref[at + gain_rows:at + 2 * gain_rows] = low
        out_ref[at + 2 * gain_rows:] = count


def messages(inputs, gain, repeats, me):
    micro, rows, part = inputs.shape
    shape = jax.ShapeDtypeStruct((part // BLK * rows + 2 * gain.shape[0] + 16, BLK), jnp.bfloat16)
    return pl.pallas_call(
        message_kernel,
        out_shape=(shape,) * (micro - 1),
        in_specs=[VMEM_SPEC, VMEM_SPEC, SMEM_SPEC, SMEM_SPEC],
        out_specs=(VMEM_SPEC,) * (micro - 1),
        compiler_params=params(60 * 1024 * 1024),
        cost_estimate=pl.CostEstimate(flops=1 << 20, bytes_accessed=1 << 20, transcendentals=0),
    )(inputs, gain, repeats, me)


def relay_kernel(sections, owners, own_ref, gain_ref, repeats_ref, me_ref, *refs):
    received, out_refs, (held, gains) = refs[:sections - 1], refs[sections - 1:-2], refs[-2:]
    chunks, rows, _ = held.shape
    own = AWIN // owners // BLK
    width = chunks * BLK
    part = chunks // sections
    at = part * rows
    me = me_ref[0]
    none = jnp.zeros((rows, BLK), jnp.float32)

    def mean(total):
        return jnp.sum(total, axis=-1, keepdims=True) * (1.0 / width)

    gains[me, :chunks] = gain_ref[...]
    gains[me, chunks:] = jnp.full((8, BLK), repeats_ref[0], jnp.int32).astype(jnp.float32)
    total = none
    for chunk in range(part):
        value = own_ref[me, :, chunk * BLK:(chunk + 1) * BLK].astype(jnp.float32)
        held[me * part + chunk] = value
        total = total + value
    for mask, ref in enumerate(received, 1):
        source = jnp.bitwise_xor(me, mask)
        gains[source, :chunks] = ref[at:at + chunks].astype(jnp.float32) + ref[at + chunks:at + 2 * chunks].astype(jnp.float32)
        gains[source, chunks:] = ref[at + 2 * chunks:].astype(jnp.float32)[:8]
        for chunk in range(part):
            value = ref[chunk * rows:(chunk + 1) * rows].astype(jnp.float32)
            held[source * part + chunk] = value
            total = total + value
    center = mean(total)
    square = none
    for chunk in range(chunks):
        square = square + jnp.square(held[chunk] - center)
    start = (center, lax.rsqrt(mean(square) + 1e-05))

    def section(s, carry):
        repeats = jnp.max(gains[s, chunks:]).astype(jnp.int32)

        def apply(_, carry):
            center, scale = carry
            half = 0.5 * scale
            total, square = none, none
            for chunk in range(chunks):
                value = held[chunk]
                y = (value - center) * half * gains[s, chunk:chunk + 1]
                inner = y * (2.0 * ROOT + (8.0 * 0.044715 * ROOT) * (y * y))
                value = (value + (y + y * jnp.tanh(inner))).astype(jnp.bfloat16).astype(jnp.float32)
                held[chunk] = value
                moved = value - center
                total = total + moved
                square = square + moved * moved
            shift = mean(total)
            spread = jnp.maximum(mean(square) - shift * shift, 0.0)
            return center + shift, lax.rsqrt(spread + 1e-05)

        carry = lax.fori_loop(0, repeats + 1, apply, carry)
        center, scale = carry
        for mask, out_ref in enumerate(out_refs):
            place = jnp.bitwise_xor(me_ref[1], mask) * own
            for i in range(own):
                normed = (held[place + i] - center) * scale * gains[s, pl.ds(place + i, 1)]
                out_ref[s, :, i * BLK:(i + 1) * BLK] = normed.astype(jnp.bfloat16)
        return carry

    lax.fori_loop(0, sections, section, start)


def relay(inputs, gain, repeats, me, received, owners):
    sections, rows, part = inputs.shape
    chunks = sections * part // BLK
    shape = jax.ShapeDtypeStruct((sections, rows, AWIN // owners), jnp.bfloat16)
    return pl.pallas_call(
        functools.partial(relay_kernel, sections, owners),
        out_shape=(shape,) * owners,
        in_specs=[VMEM_SPEC, VMEM_SPEC, SMEM_SPEC, SMEM_SPEC] + [VMEM_SPEC] * len(received),
        out_specs=(VMEM_SPEC,) * owners,
        scratch_shapes=[pltpu.VMEM((chunks, rows, BLK), jnp.float32), pltpu.VMEM((sections, chunks + 8, BLK), jnp.float32)],
        compiler_params=params(),
        cost_estimate=pl.CostEstimate(flops=1 << 33, bytes_accessed=2 << 20, transcendentals=0),
    )(inputs, gain, repeats, me, *received)


HALF = BLK // 2
FEATURE_ROWS = BLK + HALF + 16


def pack_three(first, second, third):
    row, col = iotas()
    low_row, low_col = row[:HALF], col[:HALF]
    turned = pltpu.roll(third[HALF:], HALF, 1)
    two = jnp.where(col >= row, first, second)
    half = jnp.where(low_col < low_row, turned, third[:HALF])
    tail_row = lax.broadcasted_iota(jnp.int32, (16, BLK), 0)
    diagonal = jnp.sum(jnp.where(col == row, second, 0.0), axis=0, keepdims=True)
    last = jnp.sum(jnp.where(low_col == low_row + HALF, third[HALF:], 0.0), axis=0, keepdims=True)
    tail = jnp.where(tail_row == 0, diagonal, jnp.where(tail_row == 1, last, 0.0))
    return jnp.concatenate([two, half, tail], axis=0)


def unpack_three(packed):
    row, col = iotas()
    low_row, low_col = row[:HALF], col[:HALF]
    two, half, tail = packed[:BLK], packed[BLK:BLK + HALF], packed[BLK + HALF:]
    turned = two.T
    first = jnp.where(col >= row, two, turned)
    second = jnp.where(col < row, two, jnp.where(col == row, tail[0:1], turned))
    across = jnp.concatenate([half, jnp.zeros_like(half)], axis=0).T
    upper = jnp.where(low_col < low_row, across[:HALF], half)
    corner = pltpu.roll(jnp.where(low_col < low_row, half, across[:HALF]), HALF, 1)
    lower = jnp.where(low_col < HALF, across[HALF:], jnp.where(low_col == low_row + HALF, tail[1:2], corner))
    return jnp.concatenate([first, second, upper, lower], axis=0)


def feature_kernel(micro, scale, order_ref, me_ref, *refs):
    in_refs, (own_ref, *out_refs) = refs[:-micro], refs[-micro:]
    weight = batch_weight(order_ref, me_ref[0], micro) * scale
    for mask, out_ref in enumerate([own_ref] + out_refs):
        s = jnp.bitwise_xor(me_ref[0], mask)
        blocks = []
        for at in range(0, 3 * BLK, BLK):
            feats = jnp.concatenate([ref[s, :, at:at + BLK] for ref in in_refs], axis=0)
            blocks.append(gram(feats, feats) * weight)
        out_ref[...] = pack_three(*blocks).astype(out_ref.dtype)


def feature_terms(order, me, feats, micro, scale):
    return pl.pallas_call(
        functools.partial(feature_kernel, micro, scale),
        out_shape=(jax.ShapeDtypeStruct((FEATURE_ROWS, BLK), jnp.float32),)
        + (jax.ShapeDtypeStruct((FEATURE_ROWS, BLK), jnp.bfloat16),) * (micro - 1),
        in_specs=[SMEM_SPEC, SMEM_SPEC] + [VMEM_SPEC] * len(feats),
        out_specs=(VMEM_SPEC,) * micro,
        compiler_params=params(),
        cost_estimate=pl.CostEstimate(flops=1 << 31, bytes_accessed=1 << 20, transcendentals=0),
    )(order, me, *feats)


def feature_sum_kernel(*refs):
    total = refs[0][...]
    for ref in refs[1:-1]:
        total = total + ref[...].astype(jnp.float32)
    refs[-1][0] = unpack_three(total)


def fast_body(inputs, gain, repeats, order, hidden_grad):
    micro, tok_rows, _ = inputs.shape
    dp_count = lax.axis_size("dp")
    scale = 1.0 / (tok_rows * dp_count)
    gain = gain.reshape(-1, BLK)
    plane, place = lax.axis_index("section").reshape(1), lax.axis_index("dp").reshape(1)
    me = jnp.concatenate([plane, place])
    told, order = lax.optimization_barrier((messages(inputs, gain, repeats, plane), order))
    pieces = tuple(swapped(one, "section", mask) for mask, one in enumerate(told, 1))

    far, near = hidden_terms(order, hidden_grad, place, dp_count, scale)
    came = swapped(far, "dp", 1)
    pieces, near = lax.optimization_barrier((pieces, near))
    feats = relay(inputs, gain, repeats, me, pieces, dp_count)
    feats, near, came = lax.optimization_barrier((feats, near, came))
    gathered = [feats[0]] + [swapped(one, "dp", mask) for mask, one in enumerate(feats[1:], 1)]
    gathered, near = lax.optimization_barrier((gathered, near))
    along_x, along_y, first, second = core_sum(near, came)
    came_x, came_y = swapped(along_x, "dp", 2), swapped(along_y, "dp", 4)
    own, *terms = feature_terms(order, plane, gathered, micro, scale)
    own, first = lax.optimization_barrier((own, first))
    terms = [swapped(one, "section", mask) for mask, one in enumerate(terms, 1)]
    along_y, along_x, kept = pair_sum(first, came_x, second, came_y)
    came_y, came_x = swapped(along_y, "dp", 4), swapped(along_x, "dp", 2)
    hidden_rows = unpacked(kept, came_y, came_x)
    feature_rows = small_call(feature_sum_kernel, jax.ShapeDtypeStruct((1, 3 * BLK, BLK), jnp.float32), own, *terms)
    return (feature_rows, hidden_rows)


def normed(value, gain_row):
    center = jnp.mean(value, axis=-1, keepdims=True)
    spread = jnp.mean(jnp.square(value - center), axis=-1, keepdims=True)
    return (value - center) * lax.rsqrt(spread + 1e-05) * gain_row


def weighted_gram(feats, weights):
    shaped = feats.reshape(feats.shape[0], -1, BLK)
    scaled = shaped * weights[:, None, None].astype(shaped.dtype)
    return jnp.einsum("tbi,tbj->bij", scaled, shaped, preferred_element_type=jnp.float32)


def plain_body(inputs, gain, repeats, order, hidden_grad):
    micro, tok_rows, part = inputs.shape
    sections = lax.axis_size("section")
    total_tok = tok_rows * lax.axis_size("dp")
    slot_weight = 0.5 * jnp.power(0.5, micro - 1 - jnp.arange(micro, dtype=jnp.float32))
    hidden_weight = jnp.zeros((micro,), jnp.float32).at[order].set(slot_weight)
    row_weight = jnp.repeat(hidden_weight, tok_rows)
    hidden = weighted_gram(hidden_grad.reshape(micro * tok_rows, GWIN), row_weight) / total_tok
    gains = lax.all_gather(gain[0], "section", axis=0)
    counts = lax.all_gather(repeats[0], "section", axis=0)
    pieces = lax.all_to_all(inputs.reshape(micro * tok_rows, part), "section", 0, 1, tiled=True)

    def section(s, carry):
        value, feats = carry
        value = lax.fori_loop(
            0,
            counts[s] + 1,
            lambda i, v: (v + gelu(normed(v, gains[s]))).astype(jnp.bfloat16).astype(jnp.float32),
            value,
        )
        now = normed(value, gains[s]).astype(jnp.bfloat16)[:, :AWIN]
        return value, lax.dynamic_update_index_in_dim(feats, now, s, 0)

    start = jnp.zeros((sections, pieces.shape[0], AWIN), jnp.bfloat16)
    _, feats = lax.fori_loop(0, sections, section, (pieces.astype(jnp.float32), start))
    feats = lax.all_to_all(feats, "section", 0, 0, tiled=True).reshape(micro * tok_rows, AWIN)
    feature = weighted_gram(feats, row_weight) / total_tok

    def shared(term):
        term = term.reshape(-1, BLK).astype(jnp.bfloat16)
        return lax.psum_scatter(term, "dp", scatter_dimension=0, tiled=True).astype(jnp.float32)[None]

    return (shared(feature), shared(hidden))


def solution(mesh):
    sections, dp_count = mesh.shape["section"], mesh.shape["dp"]

    def body(inputs, gain, repeats, order, hidden_grad):
        aligned = (
            inputs.shape[0] == sections == 4
            and inputs.shape[2] * sections % (16 * BLK) == 0
            and inputs.shape[1] % 16 == 0
            and dp_count == 8
            and AWIN == dp_count * 3 * BLK
            and GWIN % (dp_count * 4 * BLK) == 0
        )
        return (fast_body if aligned else plain_body)(inputs, gain, repeats, order, hidden_grad)

    placed = (
        P(None, "dp", "section"),
        P("section", None),
        P("section"),
        P(),
        P("section", None, "dp", None),
    )
    return jax.shard_map(
        body,
        mesh=mesh,
        in_specs=placed,
        out_specs=(P("section", "dp", None), P("section", "dp", None)),
        check_vma=False,
    )
```

```python
import functools

import jax
import jax.numpy as jnp
from jax import lax
from jax.experimental import pallas as pl
from jax.experimental.pallas import tpu as pltpu
from jax.sharding import PartitionSpec as P

AWIN = 3072
GWIN = 12288
BLK = 128
VMEM_LIMIT = 16 * 1024 * 1024
ROOT = 0.7978845608028654

SMEM_SPEC = pl.BlockSpec(memory_space=pltpu.SMEM)
VMEM_SPEC = pl.BlockSpec(memory_space=pltpu.VMEM)


def params(limit=VMEM_LIMIT):
    return pltpu.CompilerParams(vmem_limit_bytes=limit)


def gelu(x):
    inner = ROOT * (x + 0.044715 * (x * x * x))
    return x * (0.5 * (1.0 + jnp.tanh(inner)))


def batch_weight(order_ref, batch_id, micro):
    weight = jnp.float32(0.0)
    for slot in range(micro):
        weight = jnp.where(order_ref[slot] == batch_id, jnp.float32(0.5 * 0.5 ** (micro - 1 - slot)), weight)
    return weight


def gram(left, right):
    return lax.dot_general(left, right, (((0,), (0,)), ((), ())), preferred_element_type=jnp.float32)


def iotas():
    row = lax.broadcasted_iota(jnp.int32, (BLK, BLK), 0)
    col = lax.broadcasted_iota(jnp.int32, (BLK, BLK), 1)
    return row, col


def packed_rows(pairs):
    return pairs * BLK + -(-pairs // 16) * 16


def hidden_kernel(micro, pairs, scale, order_ref, _, *refs):
    grad_refs, out_ref = refs[:-1], refs[-1]
    row, col = iotas()
    weights = [batch_weight(order_ref, m, micro) for m in range(micro)]
    tail_row = lax.broadcasted_iota(jnp.int32, (packed_rows(pairs) - pairs * BLK, BLK), 0)
    for place, grad_ref in enumerate(grad_refs):
        for half in range(2):
            tail = jnp.zeros(tail_row.shape, jnp.float32)
            for pair in range(pairs):
                at = (half * pairs + pair) * 2 * BLK
                parts = [grad_ref[0, m, :, at:at + 2 * BLK] for m in range(micro)]
                scaled = [(part.astype(jnp.float32) * weight).astype(jnp.bfloat16) for part, weight in zip(parts, weights)]
                both = gram(jnp.concatenate(scaled, axis=0), jnp.concatenate(parts, axis=0)) * scale
                first, second = both[:BLK, :BLK], both[BLK:, BLK:]
                packed = jnp.where(col >= row, first, second).astype(jnp.bfloat16)
                out_ref[place, half, pair * BLK:(pair + 1) * BLK] = packed
                diagonal = jnp.sum(jnp.where(col == row, second, 0.0), axis=0, keepdims=True)
                tail = jnp.where(tail_row == pair, diagonal, tail)
            out_ref[place, half, pairs * BLK:] = tail.astype(jnp.bfloat16)


def hidden_terms(order, hidden_grad, me, dp_count, scale, cost):
    _, micro, rows, width = hidden_grad.shape
    own = width // dp_count
    pairs = own // (4 * BLK)
    shape, count = (2, packed_rows(pairs), BLK), dp_count // 2

    def owner(flip):
        return lambda i, order, me: (0, 0, 0, jnp.bitwise_xor(me[0], 2 - 2 * i + flip))

    return pl.pallas_call(
        functools.partial(hidden_kernel, micro, pairs, scale),
        out_shape=jax.ShapeDtypeStruct((count,) + shape, jnp.bfloat16),
        grid_spec=pltpu.PrefetchScalarGridSpec(
            num_scalar_prefetch=2,
            grid=(count // 2,),
            in_specs=[pl.BlockSpec((1, micro, rows, own), owner(4)), pl.BlockSpec((1, micro, rows, own), owner(0))],
            out_specs=pl.BlockSpec((2,) + shape, lambda i, order, me: (i, 0, 0, 0)),
        ),
        compiler_params=params(60 * 1024 * 1024),
        cost_estimate=pl.CostEstimate(flops=cost, bytes_accessed=1 << 10, transcendentals=0),
    )(order, me, hidden_grad, hidden_grad)


def small_call(kernel, shapes, *operands, cost=1 << 20):
    return pl.pallas_call(
        kernel,
        out_shape=shapes,
        in_specs=[VMEM_SPEC] * len(operands),
        out_specs=jax.tree.map(lambda _: VMEM_SPEC, shapes),
        compiler_params=params(),
        cost_estimate=pl.CostEstimate(flops=cost, bytes_accessed=1 << 10, transcendentals=0),
    )(*operands)


def core_sum_kernel(near_ref, came_ref, along_x_ref, along_y_ref, first_ref, second_ref):
    def total(place, half):
        return near_ref[place, half].astype(jnp.float32) + came_ref[place, half].astype(jnp.float32)

    for i in range(2):
        along_x_ref[i] = total(i, 0).astype(jnp.bfloat16)
        along_y_ref[i] = total(2 * i, 1).astype(jnp.bfloat16)
        first_ref[i] = total(2 + i, 0)
        second_ref[i] = total(1 + 2 * i, 1)


def pair_sum_kernel(first_ref, came_x_ref, second_ref, came_y_ref, along_y_ref, along_x_ref, kept_ref):
    along_y_ref[...] = (first_ref[0] + came_x_ref[0].astype(jnp.float32)).astype(jnp.bfloat16)
    along_x_ref[...] = (second_ref[0] + came_y_ref[0].astype(jnp.float32)).astype(jnp.bfloat16)
    kept_ref[0] = first_ref[1] + came_x_ref[1].astype(jnp.float32)
    kept_ref[1] = second_ref[1] + came_y_ref[1].astype(jnp.float32)


def unpack_kernel(pairs, kept_ref, came_y_ref, came_x_ref, out_ref):
    row, col = iotas()
    for half, came_ref in enumerate((came_y_ref, came_x_ref)):

        def total(rows):
            return kept_ref[half, rows] + came_ref[rows].astype(jnp.float32)

        tail = total(slice(pairs * BLK, None))
        for pair in range(pairs):
            value = total(slice(pair * BLK, (pair + 1) * BLK))
            turned = value.T
            at = (half * pairs + pair) * 2 * BLK
            out_ref[0, at:at + BLK] = jnp.where(col >= row, value, turned)
            second = jnp.where(col == row, tail[pair:pair + 1], turned)
            out_ref[0, at + BLK:at + 2 * BLK] = jnp.where(col < row, value, second)


def core_sum(near, came):
    one = near.shape[2:]
    sent = jax.ShapeDtypeStruct((2,) + one, jnp.bfloat16)
    kept = jax.ShapeDtypeStruct((2,) + one, jnp.float32)
    return small_call(core_sum_kernel, (sent, sent, kept, kept), near, came)


def pair_sum(first, came_x, second, came_y):
    last = jax.ShapeDtypeStruct(first.shape[1:], jnp.bfloat16)
    return small_call(pair_sum_kernel, (last, last, first), first, came_x, second, came_y)


def unpacked(kept, came_y, came_x):
    pairs = kept.shape[1] // BLK
    out = jax.ShapeDtypeStruct((1, 4 * pairs * BLK, BLK), jnp.float32)
    return small_call(functools.partial(unpack_kernel, pairs), out, kept, came_y, came_x)


def swapped(shard, axis, mask):
    return lax.ppermute(shard, axis, [(i, i ^ mask) for i in range(lax.axis_size(axis))])


def message_kernel(in_ref, gain_ref, repeats_ref, me_ref, *out_refs):
    _, rows, part = in_ref.shape
    chunks, gain_rows = part // BLK, gain_ref.shape[0]
    gain = gain_ref[...]
    high = gain.astype(jnp.bfloat16)
    low = (gain - high.astype(jnp.float32)).astype(jnp.bfloat16)
    count = jnp.full((16, BLK), repeats_ref[0], jnp.int32).astype(jnp.float32).astype(jnp.bfloat16)
    at = chunks * rows
    for mask, out_ref in enumerate(out_refs, 1):
        target = jnp.bitwise_xor(me_ref[0], mask)
        for chunk in range(chunks):
            out_ref[chunk * rows:(chunk + 1) * rows] = in_ref[target, :, chunk * BLK:(chunk + 1) * BLK]
        out_ref[at:at + gain_rows] = high
        out_ref[at + gain_rows:at + 2 * gain_rows] = low
        out_ref[at + 2 * gain_rows:] = count


def messages(inputs, gain, repeats, me):
    micro, rows, part = inputs.shape
    shape = jax.ShapeDtypeStruct((part // BLK * rows + 2 * gain.shape[0] + 16, BLK), jnp.bfloat16)
    return pl.pallas_call(
        message_kernel,
        out_shape=(shape,) * (micro - 1),
        in_specs=[VMEM_SPEC, VMEM_SPEC, SMEM_SPEC, SMEM_SPEC],
        out_specs=(VMEM_SPEC,) * (micro - 1),
        compiler_params=params(60 * 1024 * 1024),
        cost_estimate=pl.CostEstimate(flops=1 << 20, bytes_accessed=1 << 20, transcendentals=0),
    )(inputs, gain, repeats, me)


def relay_kernel(sections, owners, own_ref, gain_ref, repeats_ref, me_ref, *refs):
    received, out_refs, (held, gains) = refs[:sections - 1], refs[sections - 1:-2], refs[-2:]
    chunks, rows, _ = held.shape
    own = AWIN // owners // BLK
    width = chunks * BLK
    part = chunks // sections
    at = part * rows
    me = me_ref[0]
    none = jnp.zeros((rows, BLK), jnp.float32)

    def mean(total):
        return jnp.sum(total, axis=-1, keepdims=True) * (1.0 / width)

    gains[me, :chunks] = gain_ref[...]
    gains[me, chunks:] = jnp.full((8, BLK), repeats_ref[0], jnp.int32).astype(jnp.float32)
    total = none
    for chunk in range(part):
        value = own_ref[me, :, chunk * BLK:(chunk + 1) * BLK].astype(jnp.float32)
        held[me * part + chunk] = value
        total = total + value
    for mask, ref in enumerate(received, 1):
        source = jnp.bitwise_xor(me, mask)
        gains[source, :chunks] = ref[at:at + chunks].astype(jnp.float32) + ref[at + chunks:at + 2 * chunks].astype(jnp.float32)
        gains[source, chunks:] = ref[at + 2 * chunks:].astype(jnp.float32)[:8]
        for chunk in range(part):
            value = ref[chunk * rows:(chunk + 1) * rows].astype(jnp.float32)
            held[source * part + chunk] = value
            total = total + value
    center = mean(total)
    square = none
    for chunk in range(chunks):
        square = square + jnp.square(held[chunk] - center)
    start = (center, lax.rsqrt(mean(square) + 1e-05))

    def section(s, carry):
        repeats = jnp.max(gains[s, chunks:]).astype(jnp.int32)

        def apply(_, carry):
            center, scale = carry
            half = 0.5 * scale
            total, square = none, none
            for chunk in range(chunks):
                value = held[chunk]
                y = (value - center) * half * gains[s, chunk:chunk + 1]
                inner = y * (2.0 * ROOT + (8.0 * 0.044715 * ROOT) * (y * y))
                value = (value + (y + y * jnp.tanh(inner))).astype(jnp.bfloat16).astype(jnp.float32)
                held[chunk] = value
                moved = value - center
                total = total + moved
                square = square + moved * moved
            shift = mean(total)
            spread = jnp.maximum(mean(square) - shift * shift, 0.0)
            return center + shift, lax.rsqrt(spread + 1e-05)

        carry = lax.fori_loop(0, repeats + 1, apply, carry)
        center, scale = carry
        for mask, out_ref in enumerate(out_refs):
            place = jnp.bitwise_xor(me_ref[1], mask) * own
            for i in range(own):
                normed = (held[place + i] - center) * scale * gains[s, pl.ds(place + i, 1)]
                out_ref[s, :, i * BLK:(i + 1) * BLK] = normed.astype(jnp.bfloat16)
        return carry

    lax.fori_loop(0, sections, section, start)


def relay(inputs, gain, repeats, me, received, owners):
    sections, rows, part = inputs.shape
    chunks = sections * part // BLK
    shape = jax.ShapeDtypeStruct((sections, rows, AWIN // owners), jnp.bfloat16)
    return pl.pallas_call(
        functools.partial(relay_kernel, sections, owners),
        out_shape=(shape,) * owners,
        in_specs=[VMEM_SPEC, VMEM_SPEC, SMEM_SPEC, SMEM_SPEC] + [VMEM_SPEC] * len(received),
        out_specs=(VMEM_SPEC,) * owners,
        scratch_shapes=[pltpu.VMEM((chunks, rows, BLK), jnp.float32), pltpu.VMEM((sections, chunks + 8, BLK), jnp.float32)],
        compiler_params=params(),
        cost_estimate=pl.CostEstimate(flops=1 << 33, bytes_accessed=2 << 20, transcendentals=0),
    )(inputs, gain, repeats, me, *received)


HALF = BLK // 2
FEATURE_ROWS = BLK + HALF + 16


def pack_three(first, second, third):
    row, col = iotas()
    low_row, low_col = row[:HALF], col[:HALF]
    turned = pltpu.roll(third[HALF:], HALF, 1)
    two = jnp.where(col >= row, first, second)
    half = jnp.where(low_col < low_row, turned, third[:HALF])
    tail_row = lax.broadcasted_iota(jnp.int32, (16, BLK), 0)
    diagonal = jnp.sum(jnp.where(col == row, second, 0.0), axis=0, keepdims=True)
    last = jnp.sum(jnp.where(low_col == low_row + HALF, third[HALF:], 0.0), axis=0, keepdims=True)
    tail = jnp.where(tail_row == 0, diagonal, jnp.where(tail_row == 1, last, 0.0))
    return jnp.concatenate([two, half, tail], axis=0)


def unpack_three(packed):
    row, col = iotas()
    low_row, low_col = row[:HALF], col[:HALF]
    two, half, tail = packed[:BLK], packed[BLK:BLK + HALF], packed[BLK + HALF:]
    turned = two.T
    first = jnp.where(col >= row, two, turned)
    second = jnp.where(col < row, two, jnp.where(col == row, tail[0:1], turned))
    across = jnp.concatenate([half, jnp.zeros_like(half)], axis=0).T
    upper = jnp.where(low_col < low_row, across[:HALF], half)
    corner = pltpu.roll(jnp.where(low_col < low_row, half, across[:HALF]), HALF, 1)
    lower = jnp.where(low_col < HALF, across[HALF:], jnp.where(low_col == low_row + HALF, tail[1:2], corner))
    return jnp.concatenate([first, second, upper, lower], axis=0)


def feature_kernel(micro, scale, order_ref, me_ref, *refs):
    in_refs, (own_ref, *out_refs) = refs[:-micro], refs[-micro:]
    weight = batch_weight(order_ref, me_ref[0], micro) * scale
    for mask, out_ref in enumerate([own_ref] + out_refs):
        s = jnp.bitwise_xor(me_ref[0], mask)
        blocks = []
        for at in range(0, 3 * BLK, BLK):
            feats = jnp.concatenate([ref[s, :, at:at + BLK] for ref in in_refs], axis=0)
            blocks.append(gram(feats, feats) * weight)
        out_ref[...] = pack_three(*blocks).astype(out_ref.dtype)


def feature_terms(order, me, feats, micro, scale):
    return pl.pallas_call(
        functools.partial(feature_kernel, micro, scale),
        out_shape=(jax.ShapeDtypeStruct((FEATURE_ROWS, BLK), jnp.float32),)
        + (jax.ShapeDtypeStruct((FEATURE_ROWS, BLK), jnp.bfloat16),) * (micro - 1),
        in_specs=[SMEM_SPEC, SMEM_SPEC] + [VMEM_SPEC] * len(feats),
        out_specs=(VMEM_SPEC,) * micro,
        compiler_params=params(),
        cost_estimate=pl.CostEstimate(flops=1 << 31, bytes_accessed=1 << 20, transcendentals=0),
    )(order, me, *feats)


def feature_sum_kernel(*refs):
    total = refs[0][...]
    for ref in refs[1:-1]:
        total = total + ref[...].astype(jnp.float32)
    refs[-1][0] = unpack_three(total)


def fast_body(inputs, gain, repeats, order, hidden_grad):
    micro, tok_rows, _ = inputs.shape
    dp_count = lax.axis_size("dp")
    scale = 1.0 / (tok_rows * dp_count)
    gain = gain.reshape(-1, BLK)
    plane, place = lax.axis_index("section").reshape(1), lax.axis_index("dp").reshape(1)
    me = jnp.concatenate([plane, place])
    told, order = lax.optimization_barrier((messages(inputs, gain, repeats, plane), order))
    pieces = {mask: swapped(told[mask - 1], "section", mask) for mask in (2, 3, 1)}
    pieces = tuple(pieces[mask] for mask in (1, 2, 3))

    came = swapped(hidden_terms(order, hidden_grad, place ^ 1, dp_count, scale, 1 << 20), "dp", 1)
    near = hidden_terms(order, hidden_grad, place, dp_count, scale, 1 << 34)
    along_x, along_y, first, second = core_sum(near, came)
    came_x, came_y = swapped(along_x, "dp", 2), swapped(along_y, "dp", 4)
    pieces, first = lax.optimization_barrier((pieces, first))

    feats = relay(inputs, gain, repeats, me, pieces, dp_count)
    feats, came_x, came_y = lax.optimization_barrier((feats, came_x, came_y))
    gathered = [feats[0]] + [swapped(feats[mask], "dp", mask) for mask in (6, 7, 4, 2, 5, 3, 1)]
    own, *terms = feature_terms(order, plane, gathered, micro, scale)
    terms = [swapped(terms[mask - 1], "section", mask) for mask in (2, 3, 1)]
    own, first = lax.optimization_barrier((own, first))
    along_y, along_x, kept = pair_sum(first, came_x, second, came_y)
    came_y, came_x = swapped(along_y, "dp", 4), swapped(along_x, "dp", 2)
    feature_rows = small_call(feature_sum_kernel, jax.ShapeDtypeStruct((1, 3 * BLK, BLK), jnp.float32), own, *terms, cost=1 << 34)
    kept, feature_rows = lax.optimization_barrier((kept, feature_rows))
    hidden_rows = unpacked(kept, came_y, came_x)
    return (feature_rows, hidden_rows)


def normed(value, gain_row):
    center = jnp.mean(value, axis=-1, keepdims=True)
    spread = jnp.mean(jnp.square(value - center), axis=-1, keepdims=True)
    return (value - center) * lax.rsqrt(spread + 1e-05) * gain_row


def weighted_gram(feats, weights):
    shaped = feats.reshape(feats.shape[0], -1, BLK)
    scaled = shaped * weights[:, None, None].astype(shaped.dtype)
    return jnp.einsum("tbi,tbj->bij", scaled, shaped, preferred_element_type=jnp.float32)


def plain_body(inputs, gain, repeats, order, hidden_grad):
    micro, tok_rows, part = inputs.shape
    sections = lax.axis_size("section")
    total_tok = tok_rows * lax.axis_size("dp")
    slot_weight = 0.5 * jnp.power(0.5, micro - 1 - jnp.arange(micro, dtype=jnp.float32))
    hidden_weight = jnp.zeros((micro,), jnp.float32).at[order].set(slot_weight)
    row_weight = jnp.repeat(hidden_weight, tok_rows)
    hidden = weighted_gram(hidden_grad.reshape(micro * tok_rows, GWIN), row_weight) / total_tok
    gains = lax.all_gather(gain[0], "section", axis=0)
    counts = lax.all_gather(repeats[0], "section", axis=0)
    pieces = lax.all_to_all(inputs.reshape(micro * tok_rows, part), "section", 0, 1, tiled=True)

    def section(s, carry):
        value, feats = carry
        value = lax.fori_loop(
            0,
            counts[s] + 1,
            lambda i, v: (v + gelu(normed(v, gains[s]))).astype(jnp.bfloat16).astype(jnp.float32),
            value,
        )
        now = normed(value, gains[s]).astype(jnp.bfloat16)[:, :AWIN]
        return value, lax.dynamic_update_index_in_dim(feats, now, s, 0)

    start = jnp.zeros((sections, pieces.shape[0], AWIN), jnp.bfloat16)
    _, feats = lax.fori_loop(0, sections, section, (pieces.astype(jnp.float32), start))
    feats = lax.all_to_all(feats, "section", 0, 0, tiled=True).reshape(micro * tok_rows, AWIN)
    feature = weighted_gram(feats, row_weight) / total_tok

    def shared(term):
        term = term.reshape(-1, BLK).astype(jnp.bfloat16)
        return lax.psum_scatter(term, "dp", scatter_dimension=0, tiled=True).astype(jnp.float32)[None]

    return (shared(feature), shared(hidden))


def solution(mesh):
    sections, dp_count = mesh.shape["section"], mesh.shape["dp"]

    def body(inputs, gain, repeats, order, hidden_grad):
        aligned = (
            inputs.shape[0] == sections == 4
            and inputs.shape[2] * sections % (16 * BLK) == 0
            and inputs.shape[1] % 16 == 0
            and dp_count == 8
            and AWIN == dp_count * 3 * BLK
            and GWIN % (dp_count * 4 * BLK) == 0
        )
        return (fast_body if aligned else plain_body)(inputs, gain, repeats, order, hidden_grad)

    placed = (
        P(None, "dp", "section"),
        P("section", None),
        P("section"),
        P(),
        P("section", None, "dp", None),
    )
    return jax.shard_map(
        body,
        mesh=mesh,
        in_specs=placed,
        out_specs=(P("section", "dp", None), P("section", "dp", None)),
        check_vma=False,
    )
```

```python
import functools

import jax
import jax.numpy as jnp
from jax import lax
from jax.experimental import pallas as pl
from jax.experimental.pallas import tpu as pltpu
from jax.sharding import PartitionSpec as P

AWIN = 3072
GWIN = 12288
BLK = 128
VMEM_LIMIT = 16 * 1024 * 1024
ROOT = 0.7978845608028654

SMEM_SPEC = pl.BlockSpec(memory_space=pltpu.SMEM)
VMEM_SPEC = pl.BlockSpec(memory_space=pltpu.VMEM)


def params(limit=VMEM_LIMIT):
    return pltpu.CompilerParams(vmem_limit_bytes=limit)


def gelu(x):
    inner = ROOT * (x + 0.044715 * (x * x * x))
    return x * (0.5 * (1.0 + jnp.tanh(inner)))


def batch_weight(order_ref, batch_id, micro):
    weight = jnp.float32(0.0)
    for slot in range(micro):
        weight = jnp.where(order_ref[slot] == batch_id, jnp.float32(0.5 * 0.5 ** (micro - 1 - slot)), weight)
    return weight


def gram(left, right):
    return lax.dot_general(left, right, (((0,), (0,)), ((), ())), preferred_element_type=jnp.float32)


def iotas():
    row = lax.broadcasted_iota(jnp.int32, (BLK, BLK), 0)
    col = lax.broadcasted_iota(jnp.int32, (BLK, BLK), 1)
    return row, col


def packed_rows(pairs):
    return pairs * BLK + -(-pairs // 16) * 16


def hidden_kernel(micro, pairs, scale, order_ref, me_ref, grad_ref, out_ref, held, semaphores):
    owners, _, _, own = held.shape
    copies = []
    for place in range(owners):
        first = pl.multiple_of(jnp.bitwise_xor(me_ref[0], 6 - 2 * (place // 2) - 4 * (place % 2)) * own, own)
        copy = pltpu.make_async_copy(grad_ref.at[0, :, :, pl.ds(first, own)], held.at[place], semaphores.at[place])
        copy.start()
        copies.append(copy)
    row, col = iotas()
    weights = [batch_weight(order_ref, m, micro) for m in range(micro)]
    tail_row = lax.broadcasted_iota(jnp.int32, (packed_rows(pairs) - pairs * BLK, BLK), 0)
    for place, copy in enumerate(copies):
        copy.wait()
        tail = jnp.zeros(tail_row.shape, jnp.float32)
        for pair in range(pairs):
            parts = [held[place, m, :, pair * 2 * BLK:(pair + 1) * 2 * BLK] for m in range(micro)]
            scaled = [(part.astype(jnp.float32) * weight).astype(jnp.bfloat16) for part, weight in zip(parts, weights)]
            both = gram(jnp.concatenate(scaled, axis=0), jnp.concatenate(parts, axis=0)) * scale
            first, second = both[:BLK, :BLK], both[BLK:, BLK:]
            out_ref[place, pair * BLK:(pair + 1) * BLK] = jnp.where(col >= row, first, second).astype(jnp.bfloat16)
            diagonal = jnp.sum(jnp.where(col == row, second, 0.0), axis=0, keepdims=True)
            tail = jnp.where(tail_row == pair, diagonal, tail)
        out_ref[place, pairs * BLK:] = tail.astype(jnp.bfloat16)


def hidden_terms(order, hidden_grad, me, dp_count, scale, cost):
    _, micro, rows, width = hidden_grad.shape
    own, count = width // dp_count, dp_count // 2
    pairs = own // (2 * BLK)
    return pl.pallas_call(
        functools.partial(hidden_kernel, micro, pairs, scale),
        out_shape=jax.ShapeDtypeStruct((count, packed_rows(pairs), BLK), jnp.bfloat16),
        in_specs=[SMEM_SPEC, SMEM_SPEC, pl.BlockSpec(memory_space=pltpu.HBM)],
        out_specs=VMEM_SPEC,
        scratch_shapes=[pltpu.VMEM((count, micro, rows, own), jnp.bfloat16), pltpu.SemaphoreType.DMA((count,))],
        compiler_params=params(58 * 1024 * 1024),
        cost_estimate=pl.CostEstimate(flops=cost, bytes_accessed=1 << 10, transcendentals=0),
    )(order, me, hidden_grad)


def small_call(kernel, shapes, *operands, cost=1 << 20):
    return pl.pallas_call(
        kernel,
        out_shape=shapes,
        in_specs=[VMEM_SPEC] * len(operands),
        out_specs=jax.tree.map(lambda _: VMEM_SPEC, shapes),
        compiler_params=params(),
        cost_estimate=pl.CostEstimate(flops=cost, bytes_accessed=1 << 10, transcendentals=0),
    )(*operands)


def sum_kernel(own_ref, came_ref, sent_ref, kept_ref):
    half = sent_ref.shape[0]
    total = own_ref[...].astype(jnp.float32) + came_ref[...].astype(jnp.float32)
    sent_ref[...] = total[:half].astype(jnp.bfloat16)
    kept_ref[...] = total[half:]


def summed(own, came):
    half = (own.shape[0] // 2,) + own.shape[1:]
    shapes = (jax.ShapeDtypeStruct(half, jnp.bfloat16), jax.ShapeDtypeStruct(half, jnp.float32))
    return small_call(sum_kernel, shapes, own, came)


def unpack_kernel(kept_ref, came_ref, out_ref):
    row, col = iotas()
    pairs = kept_ref.shape[1] // BLK

    def total(rows):
        return kept_ref[0, rows] + came_ref[0, rows].astype(jnp.float32)

    tail = total(slice(pairs * BLK, None))
    for pair in range(pairs):
        value = total(slice(pair * BLK, (pair + 1) * BLK))
        turned = value.T
        at = pair * 2 * BLK
        out_ref[0, at:at + BLK] = jnp.where(col >= row, value, turned)
        second = jnp.where(col == row, tail[pair:pair + 1], turned)
        out_ref[0, at + BLK:at + 2 * BLK] = jnp.where(col < row, value, second)


def swapped(shard, axis, mask):
    return lax.ppermute(shard, axis, [(i, i ^ mask) for i in range(lax.axis_size(axis))])


def message_kernel(in_ref, gain_ref, repeats_ref, me_ref, *out_refs):
    _, rows, part = in_ref.shape
    chunks, gain_rows = part // BLK, gain_ref.shape[0]
    gain = gain_ref[...]
    high = gain.astype(jnp.bfloat16)
    low = (gain - high.astype(jnp.float32)).astype(jnp.bfloat16)
    count = jnp.full((16, BLK), repeats_ref[0], jnp.int32).astype(jnp.float32).astype(jnp.bfloat16)
    at = chunks * rows
    for mask, out_ref in enumerate(out_refs, 1):
        target = jnp.bitwise_xor(me_ref[0], mask)
        for chunk in range(chunks):
            out_ref[chunk * rows:(chunk + 1) * rows] = in_ref[target, :, chunk * BLK:(chunk + 1) * BLK]
        out_ref[at:at + gain_rows] = high
        out_ref[at + gain_rows:at + 2 * gain_rows] = low
        out_ref[at + 2 * gain_rows:] = count


def messages(inputs, gain, repeats, me):
    micro, rows, part = inputs.shape
    shape = jax.ShapeDtypeStruct((part // BLK * rows + 2 * gain.shape[0] + 16, BLK), jnp.bfloat16)
    return pl.pallas_call(
        message_kernel,
        out_shape=(shape,) * (micro - 1),
        in_specs=[VMEM_SPEC, VMEM_SPEC, SMEM_SPEC, SMEM_SPEC],
        out_specs=(VMEM_SPEC,) * (micro - 1),
        compiler_params=params(60 * 1024 * 1024),
        cost_estimate=pl.CostEstimate(flops=1 << 20, bytes_accessed=1 << 20, transcendentals=0),
    )(inputs, gain, repeats, me)


def relay_kernel(sections, owners, own_ref, gain_ref, repeats_ref, me_ref, *refs):
    received, out_refs, (held, gains) = refs[:sections - 1], refs[sections - 1:-2], refs[-2:]
    chunks, rows, _ = held.shape
    own = AWIN // owners // BLK
    width = chunks * BLK
    part = chunks // sections
    at = part * rows
    me = me_ref[0]
    none = jnp.zeros((rows, BLK), jnp.float32)

    def mean(total):
        return jnp.sum(total, axis=-1, keepdims=True) * (1.0 / width)

    gains[me, :chunks] = gain_ref[...]
    gains[me, chunks:] = jnp.full((8, BLK), repeats_ref[0], jnp.int32).astype(jnp.float32)
    total = none
    for chunk in range(part):
        value = own_ref[me, :, chunk * BLK:(chunk + 1) * BLK].astype(jnp.float32)
        held[me * part + chunk] = value
        total = total + value
    for mask, ref in enumerate(received, 1):
        source = jnp.bitwise_xor(me, mask)
        gains[source, :chunks] = ref[at:at + chunks].astype(jnp.float32) + ref[at + chunks:at + 2 * chunks].astype(jnp.float32)
        gains[source, chunks:] = ref[at + 2 * chunks:].astype(jnp.float32)[:8]
        for chunk in range(part):
            value = ref[chunk * rows:(chunk + 1) * rows].astype(jnp.float32)
            held[source * part + chunk] = value
            total = total + value
    center = mean(total)
    square = none
    for chunk in range(chunks):
        square = square + jnp.square(held[chunk] - center)
    start = (center, lax.rsqrt(mean(square) + 1e-05))

    def section(s, carry):
        repeats = jnp.max(gains[s, chunks:]).astype(jnp.int32)

        def apply(_, carry):
            center, scale = carry
            half = 0.5 * scale
            total, square = none, none
            for chunk in range(chunks):
                value = held[chunk]
                y = (value - center) * half * gains[s, chunk:chunk + 1]
                inner = y * (2.0 * ROOT + (8.0 * 0.044715 * ROOT) * (y * y))
                value = (value + (y + y * jnp.tanh(inner))).astype(jnp.bfloat16).astype(jnp.float32)
                held[chunk] = value
                moved = value - center
                total = total + moved
                square = square + moved * moved
            shift = mean(total)
            spread = jnp.maximum(mean(square) - shift * shift, 0.0)
            return center + shift, lax.rsqrt(spread + 1e-05)

        carry = lax.fori_loop(0, repeats + 1, apply, carry)
        center, scale = carry
        for mask, out_ref in enumerate(out_refs):
            place = jnp.bitwise_xor(me_ref[1], mask) * own
            for i in range(own):
                normed = (held[place + i] - center) * scale * gains[s, pl.ds(place + i, 1)]
                out_ref[s, :, i * BLK:(i + 1) * BLK] = normed.astype(jnp.bfloat16)
        return carry

    lax.fori_loop(0, sections, section, start)


def relay(inputs, gain, repeats, me, received, owners):
    sections, rows, part = inputs.shape
    chunks = sections * part // BLK
    shape = jax.ShapeDtypeStruct((sections, rows, AWIN // owners), jnp.bfloat16)
    return pl.pallas_call(
        functools.partial(relay_kernel, sections, owners),
        out_shape=(shape,) * owners,
        in_specs=[VMEM_SPEC, VMEM_SPEC, SMEM_SPEC, SMEM_SPEC] + [VMEM_SPEC] * len(received),
        out_specs=(VMEM_SPEC,) * owners,
        scratch_shapes=[pltpu.VMEM((chunks, rows, BLK), jnp.float32), pltpu.VMEM((sections, chunks + 8, BLK), jnp.float32)],
        compiler_params=params(),
        cost_estimate=pl.CostEstimate(flops=1 << 33, bytes_accessed=2 << 20, transcendentals=0),
    )(inputs, gain, repeats, me, *received)


HALF = BLK // 2
FEATURE_ROWS = BLK + HALF + 16


def pack_three(first, second, third):
    row, col = iotas()
    low_row, low_col = row[:HALF], col[:HALF]
    turned = pltpu.roll(third[HALF:], HALF, 1)
    two = jnp.where(col >= row, first, second)
    half = jnp.where(low_col < low_row, turned, third[:HALF])
    tail_row = lax.broadcasted_iota(jnp.int32, (16, BLK), 0)
    diagonal = jnp.sum(jnp.where(col == row, second, 0.0), axis=0, keepdims=True)
    last = jnp.sum(jnp.where(low_col == low_row + HALF, third[HALF:], 0.0), axis=0, keepdims=True)
    tail = jnp.where(tail_row == 0, diagonal, jnp.where(tail_row == 1, last, 0.0))
    return jnp.concatenate([two, half, tail], axis=0)


def unpack_three(packed):
    row, col = iotas()
    low_row, low_col = row[:HALF], col[:HALF]
    two, half, tail = packed[:BLK], packed[BLK:BLK + HALF], packed[BLK + HALF:]
    turned = two.T
    first = jnp.where(col >= row, two, turned)
    second = jnp.where(col < row, two, jnp.where(col == row, tail[0:1], turned))
    across = jnp.concatenate([half, jnp.zeros_like(half)], axis=0).T
    upper = jnp.where(low_col < low_row, across[:HALF], half)
    corner = pltpu.roll(jnp.where(low_col < low_row, half, across[:HALF]), HALF, 1)
    lower = jnp.where(low_col < HALF, across[HALF:], jnp.where(low_col == low_row + HALF, tail[1:2], corner))
    return jnp.concatenate([first, second, upper, lower], axis=0)


def feature_kernel(micro, scale, order_ref, me_ref, *refs):
    in_refs, (own_ref, *out_refs) = refs[:-micro], refs[-micro:]
    weight = batch_weight(order_ref, me_ref[0], micro) * scale
    for mask, out_ref in enumerate([own_ref] + out_refs):
        s = jnp.bitwise_xor(me_ref[0], mask)
        blocks = []
        for at in range(0, 3 * BLK, BLK):
            feats = jnp.concatenate([ref[s, :, at:at + BLK] for ref in in_refs], axis=0)
            blocks.append(gram(feats, feats) * weight)
        out_ref[...] = pack_three(*blocks).astype(out_ref.dtype)


def feature_terms(order, me, feats, micro, scale):
    return pl.pallas_call(
        functools.partial(feature_kernel, micro, scale),
        out_shape=(jax.ShapeDtypeStruct((FEATURE_ROWS, BLK), jnp.float32),)
        + (jax.ShapeDtypeStruct((FEATURE_ROWS, BLK), jnp.bfloat16),) * (micro - 1),
        in_specs=[SMEM_SPEC, SMEM_SPEC] + [VMEM_SPEC] * len(feats),
        out_specs=(VMEM_SPEC,) * micro,
        compiler_params=params(),
        cost_estimate=pl.CostEstimate(flops=1 << 31, bytes_accessed=1 << 20, transcendentals=0),
    )(order, me, *feats)


def feature_sum_kernel(*refs):
    total = refs[0][...]
    for ref in refs[1:-1]:
        total = total + ref[...].astype(jnp.float32)
    refs[-1][0] = unpack_three(total)


def fast_body(inputs, gain, repeats, order, hidden_grad):
    micro, tok_rows, _ = inputs.shape
    dp_count = lax.axis_size("dp")
    scale = 1.0 / (tok_rows * dp_count)
    gain = gain.reshape(-1, BLK)
    plane, place = lax.axis_index("section").reshape(1), lax.axis_index("dp").reshape(1)
    me = jnp.concatenate([plane, place])
    told, order = lax.optimization_barrier((messages(inputs, gain, repeats, plane), order))
    pieces = {mask: swapped(told[mask - 1], "section", mask) for mask in (2, 3, 1)}
    pieces = tuple(pieces[mask] for mask in (1, 2, 3))

    came = swapped(hidden_terms(order, hidden_grad, place ^ 1, dp_count, scale, 1 << 20), "dp", 1)
    sent, kept = summed(hidden_terms(order, hidden_grad, place, dp_count, scale, 1 << 34), came)
    came = swapped(sent, "dp", 2)
    pieces, kept = lax.optimization_barrier((pieces, kept))

    feats = relay(inputs, gain, repeats, me, pieces, dp_count)
    feats, came = lax.optimization_barrier((feats, came))
    gathered = [feats[0]] + [swapped(feats[mask], "dp", mask) for mask in (6, 7, 4, 2, 5, 3, 1)]
    own, *terms = feature_terms(order, plane, gathered, micro, scale)
    own, kept = lax.optimization_barrier((own, kept))
    terms = [swapped(terms[mask - 1], "section", mask) for mask in (2, 3, 1)]
    sent, kept = summed(kept, came)
    shape = jax.ShapeDtypeStruct((1, 3 * BLK, BLK), jnp.float32)
    feature_rows = small_call(feature_sum_kernel, shape, own, *terms, cost=1 << 34)
    kept, feature_rows = lax.optimization_barrier((kept, feature_rows))
    shape = jax.ShapeDtypeStruct((1, GWIN // dp_count, BLK), jnp.float32)
    return (feature_rows, small_call(unpack_kernel, shape, kept, swapped(sent, "dp", 4)))


def normed(value, gain_row):
    center = jnp.mean(value, axis=-1, keepdims=True)
    spread = jnp.mean(jnp.square(value - center), axis=-1, keepdims=True)
    return (value - center) * lax.rsqrt(spread + 1e-05) * gain_row


def weighted_gram(feats, weights):
    shaped = feats.reshape(feats.shape[0], -1, BLK)
    scaled = shaped * weights[:, None, None].astype(shaped.dtype)
    return jnp.einsum("tbi,tbj->bij", scaled, shaped, preferred_element_type=jnp.float32)


def plain_body(inputs, gain, repeats, order, hidden_grad):
    micro, tok_rows, part = inputs.shape
    sections = lax.axis_size("section")
    total_tok = tok_rows * lax.axis_size("dp")
    slot_weight = 0.5 * jnp.power(0.5, micro - 1 - jnp.arange(micro, dtype=jnp.float32))
    hidden_weight = jnp.zeros((micro,), jnp.float32).at[order].set(slot_weight)
    row_weight = jnp.repeat(hidden_weight, tok_rows)
    hidden = weighted_gram(hidden_grad.reshape(micro * tok_rows, GWIN), row_weight) / total_tok
    gains = lax.all_gather(gain[0], "section", axis=0)
    counts = lax.all_gather(repeats[0], "section", axis=0)
    pieces = lax.all_to_all(inputs.reshape(micro * tok_rows, part), "section", 0, 1, tiled=True)

    def section(s, carry):
        value, feats = carry
        value = lax.fori_loop(
            0,
            counts[s] + 1,
            lambda i, v: (v + gelu(normed(v, gains[s]))).astype(jnp.bfloat16).astype(jnp.float32),
            value,
        )
        now = normed(value, gains[s]).astype(jnp.bfloat16)[:, :AWIN]
        return value, lax.dynamic_update_index_in_dim(feats, now, s, 0)

    start = jnp.zeros((sections, pieces.shape[0], AWIN), jnp.bfloat16)
    _, feats = lax.fori_loop(0, sections, section, (pieces.astype(jnp.float32), start))
    feats = lax.all_to_all(feats, "section", 0, 0, tiled=True).reshape(micro * tok_rows, AWIN)
    feature = weighted_gram(feats, row_weight) / total_tok

    def shared(term):
        term = term.reshape(-1, BLK).astype(jnp.bfloat16)
        return lax.psum_scatter(term, "dp", scatter_dimension=0, tiled=True).astype(jnp.float32)[None]

    return (shared(feature), shared(hidden))


def solution(mesh):
    sections, dp_count = mesh.shape["section"], mesh.shape["dp"]

    def body(inputs, gain, repeats, order, hidden_grad):
        aligned = (
            inputs.shape[0] == sections == 4
            and inputs.shape[2] * sections % (16 * BLK) == 0
            and inputs.shape[1] % 16 == 0
            and dp_count == 8
            and AWIN == dp_count * 3 * BLK
            and GWIN % (dp_count * 2 * BLK) == 0
        )
        return (fast_body if aligned else plain_body)(inputs, gain, repeats, order, hidden_grad)

    placed = (
        P(None, "dp", "section"),
        P("section", None),
        P("section"),
        P(),
        P("section", None, "dp", None),
    )
    return jax.shard_map(
        body,
        mesh=mesh,
        in_specs=placed,
        out_specs=(P("section", "dp", None), P("section", "dp", None)),
        check_vma=False,
    )
```

```python
import functools

import jax
import jax.numpy as jnp
from jax import lax
from jax.experimental import pallas as pl
from jax.experimental.pallas import tpu as pltpu
from jax.sharding import PartitionSpec as P

AWIN = 3072
GWIN = 12288
BLK = 128
VMEM_LIMIT = 16 * 1024 * 1024
ROOT = 0.7978845608028654

SMEM_SPEC = pl.BlockSpec(memory_space=pltpu.SMEM)
VMEM_SPEC = pl.BlockSpec(memory_space=pltpu.VMEM)


def params(limit=VMEM_LIMIT):
    return pltpu.CompilerParams(vmem_limit_bytes=limit)


def gelu(x):
    inner = ROOT * (x + 0.044715 * (x * x * x))
    return x * (0.5 * (1.0 + jnp.tanh(inner)))


def batch_weight(order_ref, batch_id, micro):
    weight = jnp.float32(0.0)
    for slot in range(micro):
        weight = jnp.where(order_ref[slot] == batch_id, jnp.float32(0.5 * 0.5 ** (micro - 1 - slot)), weight)
    return weight


def gram(left, right):
    return lax.dot_general(left, right, (((0,), (0,)), ((), ())), preferred_element_type=jnp.float32)


def iotas():
    row = lax.broadcasted_iota(jnp.int32, (BLK, BLK), 0)
    col = lax.broadcasted_iota(jnp.int32, (BLK, BLK), 1)
    return row, col


def packed_rows(pairs):
    return pairs * BLK + -(-pairs // 16) * 16


def hidden_kernel(micro, pairs, scale, order_ref, _, *refs):
    grad_refs, out_ref = refs[:-1], refs[-1]
    row, col = iotas()
    weights = [batch_weight(order_ref, m, micro) for m in range(micro)]
    tail_row = lax.broadcasted_iota(jnp.int32, (packed_rows(pairs) - pairs * BLK, BLK), 0)
    for place, grad_ref in enumerate(grad_refs):
        for half in range(2):
            tail = jnp.zeros(tail_row.shape, jnp.float32)
            for pair in range(pairs):
                at = (half * pairs + pair) * 2 * BLK
                parts = [grad_ref[0, m, :, at:at + 2 * BLK] for m in range(micro)]
                scaled = [(part.astype(jnp.float32) * weight).astype(jnp.bfloat16) for part, weight in zip(parts, weights)]
                both = gram(jnp.concatenate(scaled, axis=0), jnp.concatenate(parts, axis=0)) * scale
                first, second = both[:BLK, :BLK], both[BLK:, BLK:]
                packed = jnp.where(col >= row, first, second).astype(jnp.bfloat16)
                out_ref[place, half, pair * BLK:(pair + 1) * BLK] = packed
                diagonal = jnp.sum(jnp.where(col == row, second, 0.0), axis=0, keepdims=True)
                tail = jnp.where(tail_row == pair, diagonal, tail)
            out_ref[place, half, pairs * BLK:] = tail.astype(jnp.bfloat16)


def hidden_terms(order, hidden_grad, me, dp_count, scale, cost):
    _, micro, rows, width = hidden_grad.shape
    own = width // dp_count
    pairs = own // (4 * BLK)
    shape, count = (2, packed_rows(pairs), BLK), dp_count // 2

    def owner(flip):
        return lambda i, order, me: (0, 0, 0, jnp.bitwise_xor(me[0], 2 - 2 * i + flip))

    return pl.pallas_call(
        functools.partial(hidden_kernel, micro, pairs, scale),
        out_shape=jax.ShapeDtypeStruct((count,) + shape, jnp.bfloat16),
        grid_spec=pltpu.PrefetchScalarGridSpec(
            num_scalar_prefetch=2,
            grid=(count // 2,),
            in_specs=[pl.BlockSpec((1, micro, rows, own), owner(4)), pl.BlockSpec((1, micro, rows, own), owner(0))],
            out_specs=pl.BlockSpec((2,) + shape, lambda i, order, me: (i, 0, 0, 0)),
        ),
        compiler_params=params(),
        cost_estimate=pl.CostEstimate(flops=cost, bytes_accessed=1 << 10, transcendentals=0),
    )(order, me, hidden_grad, hidden_grad)


def small_call(kernel, shapes, *operands, cost=1 << 20):
    return pl.pallas_call(
        kernel,
        out_shape=shapes,
        in_specs=[VMEM_SPEC] * len(operands),
        out_specs=jax.tree.map(lambda _: VMEM_SPEC, shapes),
        compiler_params=params(),
        cost_estimate=pl.CostEstimate(flops=cost, bytes_accessed=1 << 10, transcendentals=0),
    )(*operands)


def core_sum_kernel(near_ref, came_ref, along_x_ref, along_y_ref, first_ref, second_ref):
    def total(place, half):
        return near_ref[place, half].astype(jnp.float32) + came_ref[place, half].astype(jnp.float32)

    for i in range(2):
        along_x_ref[i] = total(i, 0).astype(jnp.bfloat16)
        along_y_ref[i] = total(2 * i, 1).astype(jnp.bfloat16)
        first_ref[i] = total(2 + i, 0)
        second_ref[i] = total(1 + 2 * i, 1)


def pair_sum_kernel(first_ref, came_x_ref, second_ref, came_y_ref, along_y_ref, along_x_ref, kept_ref):
    along_y_ref[...] = (first_ref[0] + came_x_ref[0].astype(jnp.float32)).astype(jnp.bfloat16)
    along_x_ref[...] = (second_ref[0] + came_y_ref[0].astype(jnp.float32)).astype(jnp.bfloat16)
    kept_ref[0] = first_ref[1] + came_x_ref[1].astype(jnp.float32)
    kept_ref[1] = second_ref[1] + came_y_ref[1].astype(jnp.float32)


def unpack_kernel(pairs, kept_ref, came_y_ref, came_x_ref, out_ref):
    row, col = iotas()
    for half, came_ref in enumerate((came_y_ref, came_x_ref)):

        def total(rows):
            return kept_ref[half, rows] + came_ref[rows].astype(jnp.float32)

        tail = total(slice(pairs * BLK, None))
        for pair in range(pairs):
            value = total(slice(pair * BLK, (pair + 1) * BLK))
            turned = value.T
            at = (half * pairs + pair) * 2 * BLK
            out_ref[0, at:at + BLK] = jnp.where(col >= row, value, turned)
            second = jnp.where(col == row, tail[pair:pair + 1], turned)
            out_ref[0, at + BLK:at + 2 * BLK] = jnp.where(col < row, value, second)


def core_sum(near, came):
    one = near.shape[2:]
    sent = jax.ShapeDtypeStruct((2,) + one, jnp.bfloat16)
    kept = jax.ShapeDtypeStruct((2,) + one, jnp.float32)
    return small_call(core_sum_kernel, (sent, sent, kept, kept), near, came)


def pair_sum(first, came_x, second, came_y):
    last = jax.ShapeDtypeStruct(first.shape[1:], jnp.bfloat16)
    return small_call(pair_sum_kernel, (last, last, first), first, came_x, second, came_y)


def unpacked(kept, came_y, came_x):
    pairs = kept.shape[1] // BLK
    out = jax.ShapeDtypeStruct((1, 4 * pairs * BLK, BLK), jnp.float32)
    return small_call(functools.partial(unpack_kernel, pairs), out, kept, came_y, came_x)


def swapped(shard, axis, mask):
    return lax.ppermute(shard, axis, [(i, i ^ mask) for i in range(lax.axis_size(axis))])


def message_kernel(in_ref, gain_ref, repeats_ref, me_ref, *out_refs):
    _, rows, part = in_ref.shape
    chunks, gain_rows = part // BLK, gain_ref.shape[0]
    gain = gain_ref[...]
    high = gain.astype(jnp.bfloat16)
    low = (gain - high.astype(jnp.float32)).astype(jnp.bfloat16)
    count = jnp.full((16, BLK), repeats_ref[0], jnp.int32).astype(jnp.float32).astype(jnp.bfloat16)
    at = chunks * rows
    for mask, out_ref in enumerate(out_refs, 1):
        target = jnp.bitwise_xor(me_ref[0], mask)
        for chunk in range(chunks):
            out_ref[chunk * rows:(chunk + 1) * rows] = in_ref[target, :, chunk * BLK:(chunk + 1) * BLK]
        out_ref[at:at + gain_rows] = high
        out_ref[at + gain_rows:at + 2 * gain_rows] = low
        out_ref[at + 2 * gain_rows:] = count


def messages(inputs, gain, repeats, me):
    micro, rows, part = inputs.shape
    shape = jax.ShapeDtypeStruct((part // BLK * rows + 2 * gain.shape[0] + 16, BLK), jnp.bfloat16)
    return pl.pallas_call(
        message_kernel,
        out_shape=(shape,) * (micro - 1),
        in_specs=[VMEM_SPEC, VMEM_SPEC, SMEM_SPEC, SMEM_SPEC],
        out_specs=(VMEM_SPEC,) * (micro - 1),
        compiler_params=params(),
        cost_estimate=pl.CostEstimate(flops=1 << 33, bytes_accessed=1 << 20, transcendentals=0),
    )(inputs, gain, repeats, me)


def relay_kernel(sections, owners, own_ref, gain_ref, repeats_ref, me_ref, *refs):
    received, out_refs, (held, gains) = refs[:sections - 1], refs[sections - 1:-2], refs[-2:]
    chunks, rows, _ = held.shape
    own = AWIN // owners // BLK
    width = chunks * BLK
    part = chunks // sections
    at = part * rows
    me = me_ref[0]
    none = jnp.zeros((rows, BLK), jnp.float32)

    def mean(total):
        return jnp.sum(total, axis=-1, keepdims=True) * (1.0 / width)

    gains[me, :chunks] = gain_ref[...]
    gains[me, chunks:] = jnp.full((8, BLK), repeats_ref[0], jnp.int32).astype(jnp.float32)
    total = none
    for chunk in range(part):
        value = own_ref[me, :, chunk * BLK:(chunk + 1) * BLK].astype(jnp.float32)
        held[me * part + chunk] = value
        total = total + value
    for mask, ref in enumerate(received, 1):
        source = jnp.bitwise_xor(me, mask)
        gains[source, :chunks] = ref[at:at + chunks].astype(jnp.float32) + ref[at + chunks:at + 2 * chunks].astype(jnp.float32)
        gains[source, chunks:] = ref[at + 2 * chunks:].astype(jnp.float32)[:8]
        for chunk in range(part):
            value = ref[chunk * rows:(chunk + 1) * rows].astype(jnp.float32)
            held[source * part + chunk] = value
            total = total + value
    center = mean(total)
    square = none
    for chunk in range(chunks):
        square = square + jnp.square(held[chunk] - center)
    start = (center, lax.rsqrt(mean(square) + 1e-05))

    def section(s, carry):
        repeats = jnp.max(gains[s, chunks:]).astype(jnp.int32)

        def apply(_, carry):
            center, scale = carry
            half = 0.5 * scale
            total, square = none, none
            for chunk in range(chunks):
                value = held[chunk]
                y = (value - center) * half * gains[s, chunk:chunk + 1]
                inner = y * (2.0 * ROOT + (8.0 * 0.044715 * ROOT) * (y * y))
                value = (value + (y + y * jnp.tanh(inner))).astype(jnp.bfloat16).astype(jnp.float32)
                held[chunk] = value
                moved = value - center
                total = total + moved
                square = square + moved * moved
            shift = mean(total)
            spread = jnp.maximum(mean(square) - shift * shift, 0.0)
            return center + shift, lax.rsqrt(spread + 1e-05)

        carry = lax.fori_loop(0, repeats + 1, apply, carry)
        center, scale = carry
        for mask, out_ref in enumerate(out_refs):
            place = jnp.bitwise_xor(me_ref[1], mask) * own
            for i in range(own):
                normed = (held[place + i] - center) * scale * gains[s, pl.ds(place + i, 1)]
                out_ref[s, :, i * BLK:(i + 1) * BLK] = normed.astype(jnp.bfloat16)
        return carry

    lax.fori_loop(0, sections, section, start)


def relay(inputs, gain, repeats, me, received, owners):
    sections, rows, part = inputs.shape
    chunks = sections * part // BLK
    shape = jax.ShapeDtypeStruct((sections, rows, AWIN // owners), jnp.bfloat16)
    return pl.pallas_call(
        functools.partial(relay_kernel, sections, owners),
        out_shape=(shape,) * owners,
        in_specs=[VMEM_SPEC, VMEM_SPEC, SMEM_SPEC, SMEM_SPEC] + [VMEM_SPEC] * len(received),
        out_specs=(VMEM_SPEC,) * owners,
        scratch_shapes=[pltpu.VMEM((chunks, rows, BLK), jnp.float32), pltpu.VMEM((sections, chunks + 8, BLK), jnp.float32)],
        compiler_params=params(),
        cost_estimate=pl.CostEstimate(flops=1 << 33, bytes_accessed=2 << 20, transcendentals=0),
    )(inputs, gain, repeats, me, *received)


HALF = BLK // 2
FEATURE_ROWS = BLK + HALF + 16


def pack_three(first, second, third):
    row, col = iotas()
    low_row, low_col = row[:HALF], col[:HALF]
    turned = pltpu.roll(third[HALF:], HALF, 1)
    two = jnp.where(col >= row, first, second)
    half = jnp.where(low_col < low_row, turned, third[:HALF])
    tail_row = lax.broadcasted_iota(jnp.int32, (16, BLK), 0)
    diagonal = jnp.sum(jnp.where(col == row, second, 0.0), axis=0, keepdims=True)
    last = jnp.sum(jnp.where(low_col == low_row + HALF, third[HALF:], 0.0), axis=0, keepdims=True)
    tail = jnp.where(tail_row == 0, diagonal, jnp.where(tail_row == 1, last, 0.0))
    return jnp.concatenate([two, half, tail], axis=0)


def unpack_three(packed):
    row, col = iotas()
    low_row, low_col = row[:HALF], col[:HALF]
    two, half, tail = packed[:BLK], packed[BLK:BLK + HALF], packed[BLK + HALF:]
    turned = two.T
    first = jnp.where(col >= row, two, turned)
    second = jnp.where(col < row, two, jnp.where(col == row, tail[0:1], turned))
    across = jnp.concatenate([half, jnp.zeros_like(half)], axis=0).T
    upper = jnp.where(low_col < low_row, across[:HALF], half)
    corner = pltpu.roll(jnp.where(low_col < low_row, half, across[:HALF]), HALF, 1)
    lower = jnp.where(low_col < HALF, across[HALF:], jnp.where(low_col == low_row + HALF, tail[1:2], corner))
    return jnp.concatenate([first, second, upper, lower], axis=0)


def feature_kernel(micro, scale, order_ref, me_ref, *refs):
    in_refs, (own_ref, *out_refs) = refs[:-micro], refs[-micro:]
    weight = batch_weight(order_ref, me_ref[0], micro) * scale
    for mask, out_ref in enumerate([own_ref] + out_refs):
        s = jnp.bitwise_xor(me_ref[0], mask)
        blocks = []
        for at in range(0, 3 * BLK, BLK):
            feats = jnp.concatenate([ref[s, :, at:at + BLK] for ref in in_refs], axis=0)
            blocks.append(gram(feats, feats) * weight)
        out_ref[...] = pack_three(*blocks).astype(out_ref.dtype)


def feature_terms(order, me, feats, micro, scale):
    return pl.pallas_call(
        functools.partial(feature_kernel, micro, scale),
        out_shape=(jax.ShapeDtypeStruct((FEATURE_ROWS, BLK), jnp.float32),)
        + (jax.ShapeDtypeStruct((FEATURE_ROWS, BLK), jnp.bfloat16),) * (micro - 1),
        in_specs=[SMEM_SPEC, SMEM_SPEC] + [VMEM_SPEC] * len(feats),
        out_specs=(VMEM_SPEC,) * micro,
        compiler_params=params(),
        cost_estimate=pl.CostEstimate(flops=1 << 31, bytes_accessed=1 << 20, transcendentals=0),
    )(order, me, *feats)


def feature_sum_kernel(*refs):
    total = refs[0][...]
    for ref in refs[1:-1]:
        total = total + ref[...].astype(jnp.float32)
    refs[-1][0] = unpack_three(total)


def fast_body(inputs, gain, repeats, order, hidden_grad):
    micro, tok_rows, _ = inputs.shape
    dp_count = lax.axis_size("dp")
    scale = 1.0 / (tok_rows * dp_count)
    gain = gain.reshape(-1, BLK)
    plane, place = lax.axis_index("section").reshape(1), lax.axis_index("dp").reshape(1)
    me = jnp.concatenate([plane, place])
    told, order = lax.optimization_barrier((messages(inputs, gain, repeats, plane), order))
    pieces = {mask: swapped(told[mask - 1], "section", mask) for mask in (2, 3, 1)}
    pieces = tuple(pieces[mask] for mask in (1, 2, 3))

    came = swapped(hidden_terms(order, hidden_grad, place ^ 1, dp_count, scale, 1 << 20), "dp", 1)
    near = hidden_terms(order, hidden_grad, place, dp_count, scale, 1 << 34)
    along_x, along_y, first, second = core_sum(near, came)
    came_x, came_y = swapped(along_x, "dp", 2), swapped(along_y, "dp", 4)
    pieces, first = lax.optimization_barrier((pieces, first))

    feats = relay(inputs, gain, repeats, me, pieces, dp_count)
    feats, came_x, came_y = lax.optimization_barrier((feats, came_x, came_y))
    gathered = [feats[0]] + [swapped(feats[mask], "dp", mask) for mask in (6, 7, 4, 2, 5, 3, 1)]
    own, *terms = feature_terms(order, plane, gathered, micro, scale)
    terms = [swapped(terms[mask - 1], "section", mask) for mask in (2, 3, 1)]
    own, first = lax.optimization_barrier((own, first))
    along_y, along_x, kept = pair_sum(first, came_x, second, came_y)
    came_y, came_x = swapped(along_y, "dp", 4), swapped(along_x, "dp", 2)
    feature_rows = small_call(feature_sum_kernel, jax.ShapeDtypeStruct((1, 3 * BLK, BLK), jnp.float32), own, *terms, cost=1 << 34)
    kept, feature_rows = lax.optimization_barrier((kept, feature_rows))
    hidden_rows = unpacked(kept, came_y, came_x)
    return (feature_rows, hidden_rows)


def normed(value, gain_row):
    center = jnp.mean(value, axis=-1, keepdims=True)
    spread = jnp.mean(jnp.square(value - center), axis=-1, keepdims=True)
    return (value - center) * lax.rsqrt(spread + 1e-05) * gain_row


def weighted_gram(feats, weights):
    shaped = feats.reshape(feats.shape[0], -1, BLK)
    scaled = shaped * weights[:, None, None].astype(shaped.dtype)
    return jnp.einsum("tbi,tbj->bij", scaled, shaped, preferred_element_type=jnp.float32)


def plain_body(inputs, gain, repeats, order, hidden_grad):
    micro, tok_rows, part = inputs.shape
    sections = lax.axis_size("section")
    total_tok = tok_rows * lax.axis_size("dp")
    slot_weight = 0.5 * jnp.power(0.5, micro - 1 - jnp.arange(micro, dtype=jnp.float32))
    hidden_weight = jnp.zeros((micro,), jnp.float32).at[order].set(slot_weight)
    row_weight = jnp.repeat(hidden_weight, tok_rows)
    hidden = weighted_gram(hidden_grad.reshape(micro * tok_rows, GWIN), row_weight) / total_tok
    gains = lax.all_gather(gain[0], "section", axis=0)
    counts = lax.all_gather(repeats[0], "section", axis=0)
    pieces = lax.all_to_all(inputs.reshape(micro * tok_rows, part), "section", 0, 1, tiled=True)

    def section(s, carry):
        value, feats = carry
        value = lax.fori_loop(
            0,
            counts[s] + 1,
            lambda i, v: (v + gelu(normed(v, gains[s]))).astype(jnp.bfloat16).astype(jnp.float32),
            value,
        )
        now = normed(value, gains[s]).astype(jnp.bfloat16)[:, :AWIN]
        return value, lax.dynamic_update_index_in_dim(feats, now, s, 0)

    start = jnp.zeros((sections, pieces.shape[0], AWIN), jnp.bfloat16)
    _, feats = lax.fori_loop(0, sections, section, (pieces.astype(jnp.float32), start))
    feats = lax.all_to_all(feats, "section", 0, 0, tiled=True).reshape(micro * tok_rows, AWIN)
    feature = weighted_gram(feats, row_weight) / total_tok

    def shared(term):
        term = term.reshape(-1, BLK).astype(jnp.bfloat16)
        return lax.psum_scatter(term, "dp", scatter_dimension=0, tiled=True).astype(jnp.float32)[None]

    return (shared(feature), shared(hidden))


def solution(mesh):
    sections, dp_count = mesh.shape["section"], mesh.shape["dp"]

    def body(inputs, gain, repeats, order, hidden_grad):
        aligned = (
            inputs.shape[0] == sections == 4
            and inputs.shape[2] * sections % (16 * BLK) == 0
            and inputs.shape[1] % 16 == 0
            and dp_count == 8
            and AWIN == dp_count * 3 * BLK
            and GWIN % (dp_count * 4 * BLK) == 0
        )
        return (fast_body if aligned else plain_body)(inputs, gain, repeats, order, hidden_grad)

    placed = (
        P(None, "dp", "section"),
        P("section", None),
        P("section"),
        P(),
        P("section", None, "dp", None),
    )
    return jax.shard_map(
        body,
        mesh=mesh,
        in_specs=placed,
        out_specs=(P("section", "dp", None), P("section", "dp", None)),
        check_vma=False,
    )
```

```python
import functools

import jax
import jax.numpy as jnp
from jax import lax
from jax.experimental import pallas as pl
from jax.experimental.pallas import tpu as pltpu
from jax.sharding import PartitionSpec as P

AWIN = 3072
GWIN = 12288
BLK = 128
VMEM_LIMIT = 16 * 1024 * 1024
ROOT = 0.7978845608028654

SMEM_SPEC = pl.BlockSpec(memory_space=pltpu.SMEM)
VMEM_SPEC = pl.BlockSpec(memory_space=pltpu.VMEM)


def params(limit=VMEM_LIMIT):
    return pltpu.CompilerParams(vmem_limit_bytes=limit)


def gelu(x):
    inner = ROOT * (x + 0.044715 * (x * x * x))
    return x * (0.5 * (1.0 + jnp.tanh(inner)))


def batch_weight(order_ref, batch_id, micro):
    weight = jnp.float32(0.0)
    for slot in range(micro):
        weight = jnp.where(order_ref[slot] == batch_id, jnp.float32(0.5 * 0.5 ** (micro - 1 - slot)), weight)
    return weight


def gram(left, right):
    return lax.dot_general(left, right, (((0,), (0,)), ((), ())), preferred_element_type=jnp.float32)


def iotas():
    row = lax.broadcasted_iota(jnp.int32, (BLK, BLK), 0)
    col = lax.broadcasted_iota(jnp.int32, (BLK, BLK), 1)
    return row, col


def packed_rows(pairs):
    return pairs * BLK + -(-pairs // 16) * 16


def hidden_kernel(micro, pairs, scale, order_ref, _, *refs):
    grad_refs, out_ref = refs[:-1], refs[-1]
    row, col = iotas()
    weights = [batch_weight(order_ref, m, micro) for m in range(micro)]
    tail_row = lax.broadcasted_iota(jnp.int32, (packed_rows(pairs) - pairs * BLK, BLK), 0)
    for place, grad_ref in enumerate(grad_refs):
        for half in range(2):
            tail = jnp.zeros(tail_row.shape, jnp.float32)
            for pair in range(pairs):
                at = (half * pairs + pair) * 2 * BLK
                parts = [grad_ref[0, m, :, at:at + 2 * BLK] for m in range(micro)]
                scaled = [(part.astype(jnp.float32) * weight).astype(jnp.bfloat16) for part, weight in zip(parts, weights)]
                both = gram(jnp.concatenate(scaled, axis=0), jnp.concatenate(parts, axis=0)) * scale
                first, second = both[:BLK, :BLK], both[BLK:, BLK:]
                packed = jnp.where(col >= row, first, second).astype(jnp.bfloat16)
                out_ref[place, half, pair * BLK:(pair + 1) * BLK] = packed
                diagonal = jnp.sum(jnp.where(col == row, second, 0.0), axis=0, keepdims=True)
                tail = jnp.where(tail_row == pair, diagonal, tail)
            out_ref[place, half, pairs * BLK:] = tail.astype(jnp.bfloat16)


def hidden_terms(order, hidden_grad, me, dp_count, scale, cost):
    _, micro, rows, width = hidden_grad.shape
    own = width // dp_count
    pairs = own // (4 * BLK)
    shape, count = (2, packed_rows(pairs), BLK), dp_count // 2

    def owner(flip):
        return lambda i, order, me: (0, 0, 0, jnp.bitwise_xor(me[0], 2 - 2 * i + flip))

    return pl.pallas_call(
        functools.partial(hidden_kernel, micro, pairs, scale),
        out_shape=jax.ShapeDtypeStruct((count,) + shape, jnp.bfloat16),
        grid_spec=pltpu.PrefetchScalarGridSpec(
            num_scalar_prefetch=2,
            grid=(count // 2,),
            in_specs=[pl.BlockSpec((1, micro, rows, own), owner(4)), pl.BlockSpec((1, micro, rows, own), owner(0))],
            out_specs=pl.BlockSpec((2,) + shape, lambda i, order, me: (i, 0, 0, 0)),
        ),
        compiler_params=params(),
        cost_estimate=pl.CostEstimate(flops=cost, bytes_accessed=1 << 10, transcendentals=0),
    )(order, me, hidden_grad, hidden_grad)


def small_call(kernel, shapes, *operands, cost=1 << 20):
    return pl.pallas_call(
        kernel,
        out_shape=shapes,
        in_specs=[VMEM_SPEC] * len(operands),
        out_specs=jax.tree.map(lambda _: VMEM_SPEC, shapes),
        compiler_params=params(),
        cost_estimate=pl.CostEstimate(flops=cost, bytes_accessed=1 << 10, transcendentals=0),
    )(*operands)


def core_sum_kernel(near_ref, came_ref, along_x_ref, along_y_ref, first_ref, second_ref):
    def total(place, half):
        return near_ref[place, half].astype(jnp.float32) + came_ref[place, half].astype(jnp.float32)

    for i in range(2):
        along_x_ref[i] = total(i, 0).astype(jnp.bfloat16)
        along_y_ref[i] = total(2 * i, 1).astype(jnp.bfloat16)
        first_ref[i] = total(2 + i, 0)
        second_ref[i] = total(1 + 2 * i, 1)


def pair_sum_kernel(first_ref, came_x_ref, second_ref, came_y_ref, along_y_ref, along_x_ref, kept_ref):
    along_y_ref[...] = (first_ref[0] + came_x_ref[0].astype(jnp.float32)).astype(jnp.bfloat16)
    along_x_ref[...] = (second_ref[0] + came_y_ref[0].astype(jnp.float32)).astype(jnp.bfloat16)
    kept_ref[0] = first_ref[1] + came_x_ref[1].astype(jnp.float32)
    kept_ref[1] = second_ref[1] + came_y_ref[1].astype(jnp.float32)


def unpack_kernel(pairs, kept_ref, came_y_ref, came_x_ref, out_ref):
    row, col = iotas()
    for half, came_ref in enumerate((came_y_ref, came_x_ref)):

        def total(rows):
            return kept_ref[half, rows] + came_ref[rows].astype(jnp.float32)

        tail = total(slice(pairs * BLK, None))
        for pair in range(pairs):
            value = total(slice(pair * BLK, (pair + 1) * BLK))
            turned = value.T
            at = (half * pairs + pair) * 2 * BLK
            out_ref[0, at:at + BLK] = jnp.where(col >= row, value, turned)
            second = jnp.where(col == row, tail[pair:pair + 1], turned)
            out_ref[0, at + BLK:at + 2 * BLK] = jnp.where(col < row, value, second)


def core_sum(near, came):
    one = near.shape[2:]
    sent = jax.ShapeDtypeStruct((2,) + one, jnp.bfloat16)
    kept = jax.ShapeDtypeStruct((2,) + one, jnp.float32)
    return small_call(core_sum_kernel, (sent, sent, kept, kept), near, came)


def pair_sum(first, came_x, second, came_y):
    last = jax.ShapeDtypeStruct(first.shape[1:], jnp.bfloat16)
    return small_call(pair_sum_kernel, (last, last, first), first, came_x, second, came_y)


def unpacked(kept, came_y, came_x):
    pairs = kept.shape[1] // BLK
    out = jax.ShapeDtypeStruct((1, 4 * pairs * BLK, BLK), jnp.float32)
    return small_call(functools.partial(unpack_kernel, pairs), out, kept, came_y, came_x)


def swapped(shard, axis, mask):
    return lax.ppermute(shard, axis, [(i, i ^ mask) for i in range(lax.axis_size(axis))])


def message_kernel(in_ref, gain_ref, repeats_ref, me_ref, *out_refs):
    _, rows, part = in_ref.shape
    chunks, gain_rows = part // BLK, gain_ref.shape[0]
    gain = gain_ref[...]
    high = gain.astype(jnp.bfloat16)
    low = (gain - high.astype(jnp.float32)).astype(jnp.bfloat16)
    count = jnp.full((16, BLK), repeats_ref[0], jnp.int32).astype(jnp.float32).astype(jnp.bfloat16)
    at = chunks * rows
    for mask, out_ref in enumerate(out_refs, 1):
        target = jnp.bitwise_xor(me_ref[0], mask)
        for chunk in range(chunks):
            out_ref[chunk * rows:(chunk + 1) * rows] = in_ref[target, :, chunk * BLK:(chunk + 1) * BLK]
        out_ref[at:at + gain_rows] = high
        out_ref[at + gain_rows:at + 2 * gain_rows] = low
        out_ref[at + 2 * gain_rows:] = count


def messages(inputs, gain, repeats, me):
    micro, rows, part = inputs.shape
    shape = jax.ShapeDtypeStruct((part // BLK * rows + 2 * gain.shape[0] + 16, BLK), jnp.bfloat16)
    return pl.pallas_call(
        message_kernel,
        out_shape=(shape,) * (micro - 1),
        in_specs=[VMEM_SPEC, VMEM_SPEC, SMEM_SPEC, SMEM_SPEC],
        out_specs=(VMEM_SPEC,) * (micro - 1),
        compiler_params=params(60 * 1024 * 1024),
        cost_estimate=pl.CostEstimate(flops=1 << 33, bytes_accessed=1 << 20, transcendentals=0),
    )(inputs, gain, repeats, me)


def relay_kernel(sections, owners, own_ref, gain_ref, repeats_ref, me_ref, *refs):
    received, out_refs, (held, gains) = refs[:sections - 1], refs[sections - 1:-2], refs[-2:]
    chunks, rows, _ = held.shape
    own = AWIN // owners // BLK
    width = chunks * BLK
    part = chunks // sections
    at = part * rows
    me = me_ref[0]
    none = jnp.zeros((rows, BLK), jnp.float32)

    def mean(total):
        return jnp.sum(total, axis=-1, keepdims=True) * (1.0 / width)

    gains[me, :chunks] = gain_ref[...]
    gains[me, chunks:] = jnp.full((8, BLK), repeats_ref[0], jnp.int32).astype(jnp.float32)
    total = none
    for chunk in range(part):
        value = own_ref[me, :, chunk * BLK:(chunk + 1) * BLK].astype(jnp.float32)
        held[me * part + chunk] = value
        total = total + value
    for mask, ref in enumerate(received, 1):
        source = jnp.bitwise_xor(me, mask)
        gains[source, :chunks] = ref[at:at + chunks].astype(jnp.float32) + ref[at + chunks:at + 2 * chunks].astype(jnp.float32)
        gains[source, chunks:] = ref[at + 2 * chunks:].astype(jnp.float32)[:8]
        for chunk in range(part):
            value = ref[chunk * rows:(chunk + 1) * rows].astype(jnp.float32)
            held[source * part + chunk] = value
            total = total + value
    center = mean(total)
    square = none
    for chunk in range(chunks):
        square = square + jnp.square(held[chunk] - center)
    start = (center, lax.rsqrt(mean(square) + 1e-05))

    def section(s, carry):
        repeats = jnp.max(gains[s, chunks:]).astype(jnp.int32)

        def apply(_, carry):
            center, scale = carry
            half = 0.5 * scale
            total, square = none, none
            for chunk in range(chunks):
                value = held[chunk]
                y = (value - center) * half * gains[s, chunk:chunk + 1]
                inner = y * (2.0 * ROOT + (8.0 * 0.044715 * ROOT) * (y * y))
                value = (value + (y + y * jnp.tanh(inner))).astype(jnp.bfloat16).astype(jnp.float32)
                held[chunk] = value
                moved = value - center
                total = total + moved
                square = square + moved * moved
            shift = mean(total)
            spread = jnp.maximum(mean(square) - shift * shift, 0.0)
            return center + shift, lax.rsqrt(spread + 1e-05)

        carry = lax.fori_loop(0, repeats + 1, apply, carry)
        center, scale = carry
        for mask, out_ref in enumerate(out_refs):
            place = jnp.bitwise_xor(me_ref[1], mask) * own
            for i in range(own):
                normed = (held[place + i] - center) * scale * gains[s, pl.ds(place + i, 1)]
                out_ref[s, :, i * BLK:(i + 1) * BLK] = normed.astype(jnp.bfloat16)
        return carry

    lax.fori_loop(0, sections, section, start)


def relay(inputs, gain, repeats, me, received, owners):
    sections, rows, part = inputs.shape
    chunks = sections * part // BLK
    shape = jax.ShapeDtypeStruct((sections, rows, AWIN // owners), jnp.bfloat16)
    return pl.pallas_call(
        functools.partial(relay_kernel, sections, owners),
        out_shape=(shape,) * owners,
        in_specs=[VMEM_SPEC, VMEM_SPEC, SMEM_SPEC, SMEM_SPEC] + [VMEM_SPEC] * len(received),
        out_specs=(VMEM_SPEC,) * owners,
        scratch_shapes=[pltpu.VMEM((chunks, rows, BLK), jnp.float32), pltpu.VMEM((sections, chunks + 8, BLK), jnp.float32)],
        compiler_params=params(),
        cost_estimate=pl.CostEstimate(flops=1 << 31, bytes_accessed=2 << 20, transcendentals=0),
    )(inputs, gain, repeats, me, *received)


HALF = BLK // 2
FEATURE_ROWS = BLK + HALF + 16


def pack_three(first, second, third):
    row, col = iotas()
    low_row, low_col = row[:HALF], col[:HALF]
    turned = pltpu.roll(third[HALF:], HALF, 1)
    two = jnp.where(col >= row, first, second)
    half = jnp.where(low_col < low_row, turned, third[:HALF])
    tail_row = lax.broadcasted_iota(jnp.int32, (16, BLK), 0)
    diagonal = jnp.sum(jnp.where(col == row, second, 0.0), axis=0, keepdims=True)
    last = jnp.sum(jnp.where(low_col == low_row + HALF, third[HALF:], 0.0), axis=0, keepdims=True)
    tail = jnp.where(tail_row == 0, diagonal, jnp.where(tail_row == 1, last, 0.0))
    return jnp.concatenate([two, half, tail], axis=0)


def unpack_three(packed):
    row, col = iotas()
    low_row, low_col = row[:HALF], col[:HALF]
    two, half, tail = packed[:BLK], packed[BLK:BLK + HALF], packed[BLK + HALF:]
    turned = two.T
    first = jnp.where(col >= row, two, turned)
    second = jnp.where(col < row, two, jnp.where(col == row, tail[0:1], turned))
    across = jnp.concatenate([half, jnp.zeros_like(half)], axis=0).T
    upper = jnp.where(low_col < low_row, across[:HALF], half)
    corner = pltpu.roll(jnp.where(low_col < low_row, half, across[:HALF]), HALF, 1)
    lower = jnp.where(low_col < HALF, across[HALF:], jnp.where(low_col == low_row + HALF, tail[1:2], corner))
    return jnp.concatenate([first, second, upper, lower], axis=0)


def feature_kernel(micro, scale, order_ref, me_ref, *refs):
    in_refs, (own_ref, *out_refs) = refs[:-micro], refs[-micro:]
    weight = batch_weight(order_ref, me_ref[0], micro) * scale
    for mask, out_ref in enumerate([own_ref] + out_refs):
        s = jnp.bitwise_xor(me_ref[0], mask)
        blocks = []
        for at in range(0, 3 * BLK, BLK):
            feats = jnp.concatenate([ref[s, :, at:at + BLK] for ref in in_refs], axis=0)
            blocks.append(gram(feats, feats) * weight)
        out_ref[...] = pack_three(*blocks).astype(out_ref.dtype)


def feature_terms(order, me, feats, micro, scale):
    return pl.pallas_call(
        functools.partial(feature_kernel, micro, scale),
        out_shape=(jax.ShapeDtypeStruct((FEATURE_ROWS, BLK), jnp.float32),)
        + (jax.ShapeDtypeStruct((FEATURE_ROWS, BLK), jnp.bfloat16),) * (micro - 1),
        in_specs=[SMEM_SPEC, SMEM_SPEC] + [VMEM_SPEC] * len(feats),
        out_specs=(VMEM_SPEC,) * micro,
        compiler_params=params(),
        cost_estimate=pl.CostEstimate(flops=1 << 31, bytes_accessed=1 << 20, transcendentals=0),
    )(order, me, *feats)


def feature_sum_kernel(*refs):
    total = refs[0][...]
    for ref in refs[1:-1]:
        total = total + ref[...].astype(jnp.float32)
    refs[-1][0] = unpack_three(total)


def fast_body(inputs, gain, repeats, order, hidden_grad):
    micro, tok_rows, _ = inputs.shape
    dp_count = lax.axis_size("dp")
    scale = 1.0 / (tok_rows * dp_count)
    gain = gain.reshape(-1, BLK)
    plane, place = lax.axis_index("section").reshape(1), lax.axis_index("dp").reshape(1)
    me = jnp.concatenate([plane, place])
    told, order = lax.optimization_barrier((messages(inputs, gain, repeats, plane), order))
    pieces = {mask: swapped(told[mask - 1], "section", mask) for mask in (2, 3, 1)}
    pieces = tuple(pieces[mask] for mask in (1, 2, 3))

    came = swapped(hidden_terms(order, hidden_grad, place ^ 1, dp_count, scale, 1 << 20), "dp", 1)
    near = hidden_terms(order, hidden_grad, place, dp_count, scale, 1 << 34)
    along_x, along_y, first, second = core_sum(near, came)
    came_x, came_y = swapped(along_x, "dp", 2), swapped(along_y, "dp", 4)
    pieces, first = lax.optimization_barrier((pieces, first))

    feats = relay(inputs, gain, repeats, me, pieces, dp_count)
    feats, came_x, came_y = lax.optimization_barrier((feats, came_x, came_y))
    gathered = [feats[0]] + [swapped(feats[mask], "dp", mask) for mask in (6, 7, 4, 2, 5, 3, 1)]
    own, *terms = feature_terms(order, plane, gathered, micro, scale)
    terms = [swapped(terms[mask - 1], "section", mask) for mask in (2, 3, 1)]
    own, first = lax.optimization_barrier((own, first))
    along_y, along_x, kept = pair_sum(first, came_x, second, came_y)
    came_y, came_x = swapped(along_y, "dp", 4), swapped(along_x, "dp", 2)
    feature_rows = small_call(feature_sum_kernel, jax.ShapeDtypeStruct((1, 3 * BLK, BLK), jnp.float32), own, *terms, cost=1 << 34)
    kept, feature_rows = lax.optimization_barrier((kept, feature_rows))
    hidden_rows = unpacked(kept, came_y, came_x)
    return (feature_rows, hidden_rows)


def normed(value, gain_row):
    center = jnp.mean(value, axis=-1, keepdims=True)
    spread = jnp.mean(jnp.square(value - center), axis=-1, keepdims=True)
    return (value - center) * lax.rsqrt(spread + 1e-05) * gain_row


def weighted_gram(feats, weights):
    shaped = feats.reshape(feats.shape[0], -1, BLK)
    scaled = shaped * weights[:, None, None].astype(shaped.dtype)
    return jnp.einsum("tbi,tbj->bij", scaled, shaped, preferred_element_type=jnp.float32)


def plain_body(inputs, gain, repeats, order, hidden_grad):
    micro, tok_rows, part = inputs.shape
    sections = lax.axis_size("section")
    total_tok = tok_rows * lax.axis_size("dp")
    slot_weight = 0.5 * jnp.power(0.5, micro - 1 - jnp.arange(micro, dtype=jnp.float32))
    hidden_weight = jnp.zeros((micro,), jnp.float32).at[order].set(slot_weight)
    row_weight = jnp.repeat(hidden_weight, tok_rows)
    hidden = weighted_gram(hidden_grad.reshape(micro * tok_rows, GWIN), row_weight) / total_tok
    gains = lax.all_gather(gain[0], "section", axis=0)
    counts = lax.all_gather(repeats[0], "section", axis=0)
    pieces = lax.all_to_all(inputs.reshape(micro * tok_rows, part), "section", 0, 1, tiled=True)

    def section(s, carry):
        value, feats = carry
        value = lax.fori_loop(
            0,
            counts[s] + 1,
            lambda i, v: (v + gelu(normed(v, gains[s]))).astype(jnp.bfloat16).astype(jnp.float32),
            value,
        )
        now = normed(value, gains[s]).astype(jnp.bfloat16)[:, :AWIN]
        return value, lax.dynamic_update_index_in_dim(feats, now, s, 0)

    start = jnp.zeros((sections, pieces.shape[0], AWIN), jnp.bfloat16)
    _, feats = lax.fori_loop(0, sections, section, (pieces.astype(jnp.float32), start))
    feats = lax.all_to_all(feats, "section", 0, 0, tiled=True).reshape(micro * tok_rows, AWIN)
    feature = weighted_gram(feats, row_weight) / total_tok

    def shared(term):
        term = term.reshape(-1, BLK).astype(jnp.bfloat16)
        return lax.psum_scatter(term, "dp", scatter_dimension=0, tiled=True).astype(jnp.float32)[None]

    return (shared(feature), shared(hidden))


def solution(mesh):
    sections, dp_count = mesh.shape["section"], mesh.shape["dp"]

    def body(inputs, gain, repeats, order, hidden_grad):
        aligned = (
            inputs.shape[0] == sections == 4
            and inputs.shape[2] * sections % (16 * BLK) == 0
            and inputs.shape[1] % 16 == 0
            and dp_count == 8
            and AWIN == dp_count * 3 * BLK
            and GWIN % (dp_count * 4 * BLK) == 0
        )
        return (fast_body if aligned else plain_body)(inputs, gain, repeats, order, hidden_grad)

    placed = (
        P(None, "dp", "section"),
        P("section", None),
        P("section"),
        P(),
        P("section", None, "dp", None),
    )
    return jax.shard_map(
        body,
        mesh=mesh,
        in_specs=placed,
        out_specs=(P("section", "dp", None), P("section", "dp", None)),
        check_vma=False,
    )
```

```python
import functools

import jax
import jax.numpy as jnp
from jax import lax
from jax.experimental import pallas as pl
from jax.experimental.pallas import tpu as pltpu
from jax.sharding import PartitionSpec as P

AWIN = 3072
GWIN = 12288
BLK = 128
VMEM_LIMIT = 16 * 1024 * 1024
ROOT = 0.7978845608028654

SMEM_SPEC = pl.BlockSpec(memory_space=pltpu.SMEM)
VMEM_SPEC = pl.BlockSpec(memory_space=pltpu.VMEM)


def params(limit=VMEM_LIMIT):
    return pltpu.CompilerParams(vmem_limit_bytes=limit)


def gelu(x):
    inner = ROOT * (x + 0.044715 * (x * x * x))
    return x * (0.5 * (1.0 + jnp.tanh(inner)))


def batch_weight(order_ref, batch_id, micro):
    weight = jnp.float32(0.0)
    for slot in range(micro):
        weight = jnp.where(order_ref[slot] == batch_id, jnp.float32(0.5 * 0.5 ** (micro - 1 - slot)), weight)
    return weight


def gram(left, right):
    return lax.dot_general(left, right, (((0,), (0,)), ((), ())), preferred_element_type=jnp.float32)


def iotas():
    row = lax.broadcasted_iota(jnp.int32, (BLK, BLK), 0)
    col = lax.broadcasted_iota(jnp.int32, (BLK, BLK), 1)
    return row, col


def packed_rows(pairs):
    return pairs * BLK + -(-pairs // 16) * 16


def hidden_kernel(micro, pairs, scale, order_ref, _, *refs):
    grad_refs, out_ref = refs[:-1], refs[-1]
    row, col = iotas()
    weights = [batch_weight(order_ref, m, micro) for m in range(micro)]
    tail_row = lax.broadcasted_iota(jnp.int32, (packed_rows(pairs) - pairs * BLK, BLK), 0)
    for place, grad_ref in enumerate(grad_refs):
        for half in range(2):
            tail = jnp.zeros(tail_row.shape, jnp.float32)
            for pair in range(pairs):
                at = (half * pairs + pair) * 2 * BLK
                parts = [grad_ref[0, m, :, at:at + 2 * BLK] for m in range(micro)]
                scaled = [(part.astype(jnp.float32) * weight).astype(jnp.bfloat16) for part, weight in zip(parts, weights)]
                both = gram(jnp.concatenate(scaled, axis=0), jnp.concatenate(parts, axis=0)) * scale
                first, second = both[:BLK, :BLK], both[BLK:, BLK:]
                packed = jnp.where(col >= row, first, second).astype(jnp.bfloat16)
                out_ref[place, half, pair * BLK:(pair + 1) * BLK] = packed
                diagonal = jnp.sum(jnp.where(col == row, second, 0.0), axis=0, keepdims=True)
                tail = jnp.where(tail_row == pair, diagonal, tail)
            out_ref[place, half, pairs * BLK:] = tail.astype(jnp.bfloat16)


def hidden_terms(order, hidden_grad, me, dp_count, scale, cost):
    _, micro, rows, width = hidden_grad.shape
    own = width // dp_count
    pairs = own // (4 * BLK)
    shape, count = (2, packed_rows(pairs), BLK), dp_count // 2

    def owner(flip):
        return lambda i, order, me: (0, 0, 0, jnp.bitwise_xor(me[0], 2 - 2 * i + flip))

    return pl.pallas_call(
        functools.partial(hidden_kernel, micro, pairs, scale),
        out_shape=jax.ShapeDtypeStruct((count,) + shape, jnp.bfloat16),
        grid_spec=pltpu.PrefetchScalarGridSpec(
            num_scalar_prefetch=2,
            grid=(count // 2,),
            in_specs=[pl.BlockSpec((1, micro, rows, own), owner(4)), pl.BlockSpec((1, micro, rows, own), owner(0))],
            out_specs=pl.BlockSpec((2,) + shape, lambda i, order, me: (i, 0, 0, 0)),
        ),
        compiler_params=params(),
        cost_estimate=pl.CostEstimate(flops=cost, bytes_accessed=1 << 10, transcendentals=0),
    )(order, me, hidden_grad, hidden_grad)


def small_call(kernel, shapes, *operands, cost=1 << 20):
    return pl.pallas_call(
        kernel,
        out_shape=shapes,
        in_specs=[VMEM_SPEC] * len(operands),
        out_specs=jax.tree.map(lambda _: VMEM_SPEC, shapes),
        compiler_params=params(),
        cost_estimate=pl.CostEstimate(flops=cost, bytes_accessed=1 << 10, transcendentals=0),
    )(*operands)


def core_sum_kernel(near_ref, came_ref, along_x_ref, along_y_ref, first_ref, second_ref):
    def total(place, half):
        return near_ref[place, half].astype(jnp.float32) + came_ref[place, half].astype(jnp.float32)

    for i in range(2):
        along_x_ref[i] = total(i, 0).astype(jnp.bfloat16)
        along_y_ref[i] = total(2 * i, 1).astype(jnp.bfloat16)
        first_ref[i] = total(2 + i, 0)
        second_ref[i] = total(1 + 2 * i, 1)


def pair_sum_kernel(first_ref, came_x_ref, second_ref, came_y_ref, along_y_ref, along_x_ref, kept_ref):
    along_y_ref[...] = (first_ref[0] + came_x_ref[0].astype(jnp.float32)).astype(jnp.bfloat16)
    along_x_ref[...] = (second_ref[0] + came_y_ref[0].astype(jnp.float32)).astype(jnp.bfloat16)
    kept_ref[0] = first_ref[1] + came_x_ref[1].astype(jnp.float32)
    kept_ref[1] = second_ref[1] + came_y_ref[1].astype(jnp.float32)


def unpack_kernel(pairs, kept_ref, came_y_ref, came_x_ref, out_ref):
    row, col = iotas()
    for half, came_ref in enumerate((came_y_ref, came_x_ref)):

        def total(rows):
            return kept_ref[half, rows] + came_ref[rows].astype(jnp.float32)

        tail = total(slice(pairs * BLK, None))
        for pair in range(pairs):
            value = total(slice(pair * BLK, (pair + 1) * BLK))
            turned = value.T
            at = (half * pairs + pair) * 2 * BLK
            out_ref[0, at:at + BLK] = jnp.where(col >= row, value, turned)
            second = jnp.where(col == row, tail[pair:pair + 1], turned)
            out_ref[0, at + BLK:at + 2 * BLK] = jnp.where(col < row, value, second)


def core_sum(near, came):
    one = near.shape[2:]
    sent = jax.ShapeDtypeStruct((2,) + one, jnp.bfloat16)
    kept = jax.ShapeDtypeStruct((2,) + one, jnp.float32)
    return small_call(core_sum_kernel, (sent, sent, kept, kept), near, came)


def pair_sum(first, came_x, second, came_y):
    last = jax.ShapeDtypeStruct(first.shape[1:], jnp.bfloat16)
    return small_call(pair_sum_kernel, (last, last, first), first, came_x, second, came_y)


def unpacked(kept, came_y, came_x):
    pairs = kept.shape[1] // BLK
    out = jax.ShapeDtypeStruct((1, 4 * pairs * BLK, BLK), jnp.float32)
    return small_call(functools.partial(unpack_kernel, pairs), out, kept, came_y, came_x)


def swapped(shard, axis, mask):
    return lax.ppermute(shard, axis, [(i, i ^ mask) for i in range(lax.axis_size(axis))])


def message_kernel(in_ref, gain_ref, repeats_ref, me_ref, *out_refs):
    _, rows, part = in_ref.shape
    chunks, gain_rows = part // BLK, gain_ref.shape[0]
    gain = gain_ref[...]
    high = gain.astype(jnp.bfloat16)
    low = (gain - high.astype(jnp.float32)).astype(jnp.bfloat16)
    count = jnp.full((16, BLK), repeats_ref[0], jnp.int32).astype(jnp.float32).astype(jnp.bfloat16)
    at = chunks * rows
    for mask, out_ref in enumerate(out_refs, 1):
        target = jnp.bitwise_xor(me_ref[0], mask)
        for chunk in range(chunks):
            out_ref[chunk * rows:(chunk + 1) * rows] = in_ref[target, :, chunk * BLK:(chunk + 1) * BLK]
        out_ref[at:at + gain_rows] = high
        out_ref[at + gain_rows:at + 2 * gain_rows] = low
        out_ref[at + 2 * gain_rows:] = count


def messages(inputs, gain, repeats, me):
    micro, rows, part = inputs.shape
    shape = jax.ShapeDtypeStruct((part // BLK * rows + 2 * gain.shape[0] + 16, BLK), jnp.bfloat16)
    return pl.pallas_call(
        message_kernel,
        out_shape=(shape,) * (micro - 1),
        in_specs=[VMEM_SPEC, VMEM_SPEC, SMEM_SPEC, SMEM_SPEC],
        out_specs=(VMEM_SPEC,) * (micro - 1),
        compiler_params=params(60 * 1024 * 1024),
        cost_estimate=pl.CostEstimate(flops=1 << 33, bytes_accessed=1 << 20, transcendentals=0),
    )(inputs, gain, repeats, me)


def relay_kernel(sections, owners, own_ref, gain_ref, repeats_ref, me_ref, *refs):
    received, out_refs, (held, gains) = refs[:sections - 1], refs[sections - 1:-2], refs[-2:]
    chunks, rows, _ = held.shape
    own = AWIN // owners // BLK
    width = chunks * BLK
    part = chunks // sections
    at = part * rows
    me = me_ref[0]
    none = jnp.zeros((rows, BLK), jnp.float32)

    def mean(total):
        return jnp.sum(total, axis=-1, keepdims=True) * (1.0 / width)

    gains[me, :chunks] = gain_ref[...]
    gains[me, chunks:] = jnp.full((8, BLK), repeats_ref[0], jnp.int32).astype(jnp.float32)
    total = none
    for chunk in range(part):
        value = own_ref[me, :, chunk * BLK:(chunk + 1) * BLK].astype(jnp.float32)
        held[me * part + chunk] = value
        total = total + value
    for mask, ref in enumerate(received, 1):
        source = jnp.bitwise_xor(me, mask)
        gains[source, :chunks] = ref[at:at + chunks].astype(jnp.float32) + ref[at + chunks:at + 2 * chunks].astype(jnp.float32)
        gains[source, chunks:] = ref[at + 2 * chunks:].astype(jnp.float32)[:8]
        for chunk in range(part):
            value = ref[chunk * rows:(chunk + 1) * rows].astype(jnp.float32)
            held[source * part + chunk] = value
            total = total + value
    center = mean(total)
    square = none
    for chunk in range(chunks):
        square = square + jnp.square(held[chunk] - center)
    start = (center, lax.rsqrt(mean(square) + 1e-05))

    def section(s, carry):
        repeats = jnp.max(gains[s, chunks:]).astype(jnp.int32)

        def apply(_, carry):
            center, scale = carry
            half = 0.5 * scale
            total, square = none, none
            for chunk in range(chunks):
                value = held[chunk]
                y = (value - center) * half * gains[s, chunk:chunk + 1]
                inner = y * (2.0 * ROOT + (8.0 * 0.044715 * ROOT) * (y * y))
                value = (value + (y + y * jnp.tanh(inner))).astype(jnp.bfloat16).astype(jnp.float32)
                held[chunk] = value
                moved = value - center
                total = total + moved
                square = square + moved * moved
            shift = mean(total)
            spread = jnp.maximum(mean(square) - shift * shift, 0.0)
            return center + shift, lax.rsqrt(spread + 1e-05)

        carry = lax.fori_loop(0, repeats + 1, apply, carry)
        center, scale = carry
        for mask, out_ref in enumerate(out_refs):
            place = jnp.bitwise_xor(me_ref[1], mask) * own
            for i in range(own):
                normed = (held[place + i] - center) * scale * gains[s, pl.ds(place + i, 1)]
                out_ref[s, :, i * BLK:(i + 1) * BLK] = normed.astype(jnp.bfloat16)
        return carry

    lax.fori_loop(0, sections, section, start)


def relay(inputs, gain, repeats, me, received, owners):
    sections, rows, part = inputs.shape
    chunks = sections * part // BLK
    shape = jax.ShapeDtypeStruct((sections, rows, AWIN // owners), jnp.bfloat16)
    return pl.pallas_call(
        functools.partial(relay_kernel, sections, owners),
        out_shape=(shape,) * owners,
        in_specs=[VMEM_SPEC, VMEM_SPEC, SMEM_SPEC, SMEM_SPEC] + [VMEM_SPEC] * len(received),
        out_specs=(VMEM_SPEC,) * owners,
        scratch_shapes=[pltpu.VMEM((chunks, rows, BLK), jnp.float32), pltpu.VMEM((sections, chunks + 8, BLK), jnp.float32)],
        compiler_params=params(),
        cost_estimate=pl.CostEstimate(flops=1 << 31, bytes_accessed=2 << 20, transcendentals=0),
    )(inputs, gain, repeats, me, *received)


HALF = BLK // 2
FEATURE_ROWS = BLK + HALF + 16


def pack_three(first, second, third):
    row, col = iotas()
    low_row, low_col = row[:HALF], col[:HALF]
    turned = pltpu.roll(third[HALF:], HALF, 1)
    two = jnp.where(col >= row, first, second)
    half = jnp.where(low_col < low_row, turned, third[:HALF])
    tail_row = lax.broadcasted_iota(jnp.int32, (16, BLK), 0)
    diagonal = jnp.sum(jnp.where(col == row, second, 0.0), axis=0, keepdims=True)
    last = jnp.sum(jnp.where(low_col == low_row + HALF, third[HALF:], 0.0), axis=0, keepdims=True)
    tail = jnp.where(tail_row == 0, diagonal, jnp.where(tail_row == 1, last, 0.0))
    return jnp.concatenate([two, half, tail], axis=0)


def unpack_three(packed):
    row, col = iotas()
    low_row, low_col = row[:HALF], col[:HALF]
    two, half, tail = packed[:BLK], packed[BLK:BLK + HALF], packed[BLK + HALF:]
    turned = two.T
    first = jnp.where(col >= row, two, turned)
    second = jnp.where(col < row, two, jnp.where(col == row, tail[0:1], turned))
    across = jnp.concatenate([half, jnp.zeros_like(half)], axis=0).T
    upper = jnp.where(low_col < low_row, across[:HALF], half)
    corner = pltpu.roll(jnp.where(low_col < low_row, half, across[:HALF]), HALF, 1)
    lower = jnp.where(low_col < HALF, across[HALF:], jnp.where(low_col == low_row + HALF, tail[1:2], corner))
    return jnp.concatenate([first, second, upper, lower], axis=0)


def feature_kernel(micro, scale, order_ref, me_ref, *refs):
    in_refs, (own_ref, *out_refs) = refs[:-micro], refs[-micro:]
    weight = batch_weight(order_ref, me_ref[0], micro) * scale
    for mask, out_ref in enumerate([own_ref] + out_refs):
        s = jnp.bitwise_xor(me_ref[0], mask)
        blocks = []
        for at in range(0, 3 * BLK, BLK):
            feats = jnp.concatenate([ref[s, :, at:at + BLK] for ref in in_refs], axis=0)
            blocks.append(gram(feats, feats) * weight)
        out_ref[...] = pack_three(*blocks).astype(out_ref.dtype)


def feature_terms(order, me, feats, micro, scale):
    return pl.pallas_call(
        functools.partial(feature_kernel, micro, scale),
        out_shape=(jax.ShapeDtypeStruct((FEATURE_ROWS, BLK), jnp.float32),)
        + (jax.ShapeDtypeStruct((FEATURE_ROWS, BLK), jnp.bfloat16),) * (micro - 1),
        in_specs=[SMEM_SPEC, SMEM_SPEC] + [VMEM_SPEC] * len(feats),
        out_specs=(VMEM_SPEC,) * micro,
        compiler_params=params(),
        cost_estimate=pl.CostEstimate(flops=1 << 31, bytes_accessed=1 << 20, transcendentals=0),
    )(order, me, *feats)


def feature_sum_kernel(*refs):
    total = refs[0][...]
    for ref in refs[1:-1]:
        total = total + ref[...].astype(jnp.float32)
    refs[-1][0] = unpack_three(total)


def fast_body(inputs, gain, repeats, order, hidden_grad):
    micro, tok_rows, _ = inputs.shape
    dp_count = lax.axis_size("dp")
    scale = 1.0 / (tok_rows * dp_count)
    gain = gain.reshape(-1, BLK)
    plane, place = lax.axis_index("section").reshape(1), lax.axis_index("dp").reshape(1)
    me = jnp.concatenate([plane, place])
    told, order = lax.optimization_barrier((messages(inputs, gain, repeats, plane), order))
    pieces = {mask: swapped(told[mask - 1], "section", mask) for mask in (2, 3, 1)}
    pieces = tuple(pieces[mask] for mask in (1, 2, 3))

    came = swapped(hidden_terms(order, hidden_grad, place ^ 1, dp_count, scale, 1 << 20), "dp", 1)
    near = hidden_terms(order, hidden_grad, place, dp_count, scale, 1 << 34)
    along_x, along_y, first, second = core_sum(near, came)
    came_x, came_y = swapped(along_x, "dp", 2), swapped(along_y, "dp", 4)
    pieces, first = lax.optimization_barrier((pieces, first))

    feats = relay(inputs, gain, repeats, me, pieces, dp_count)
    feats, came_x, came_y = lax.optimization_barrier((feats, came_x, came_y))
    gathered = [feats[0]] + [swapped(feats[mask], "dp", mask) for mask in (6, 7, 4, 2, 5, 3, 1)]
    own, *terms = feature_terms(order, plane, gathered, micro, scale)
    terms = [swapped(terms[mask - 1], "section", mask) for mask in (2, 3, 1)]
    own, first = lax.optimization_barrier((own, first))
    along_y, along_x, kept = pair_sum(first, came_x, second, came_y)
    came_y, came_x = swapped(along_y, "dp", 4), swapped(along_x, "dp", 2)
    hidden_rows = unpacked(kept, came_y, came_x)
    own, hidden_rows = lax.optimization_barrier((own, hidden_rows))
    feature_rows = small_call(feature_sum_kernel, jax.ShapeDtypeStruct((1, 3 * BLK, BLK), jnp.float32), own, *terms)
    return (feature_rows, hidden_rows)


def normed(value, gain_row):
    center = jnp.mean(value, axis=-1, keepdims=True)
    spread = jnp.mean(jnp.square(value - center), axis=-1, keepdims=True)
    return (value - center) * lax.rsqrt(spread + 1e-05) * gain_row


def weighted_gram(feats, weights):
    shaped = feats.reshape(feats.shape[0], -1, BLK)
    scaled = shaped * weights[:, None, None].astype(shaped.dtype)
    return jnp.einsum("tbi,tbj->bij", scaled, shaped, preferred_element_type=jnp.float32)


def plain_body(inputs, gain, repeats, order, hidden_grad):
    micro, tok_rows, part = inputs.shape
    sections = lax.axis_size("section")
    total_tok = tok_rows * lax.axis_size("dp")
    slot_weight = 0.5 * jnp.power(0.5, micro - 1 - jnp.arange(micro, dtype=jnp.float32))
    hidden_weight = jnp.zeros((micro,), jnp.float32).at[order].set(slot_weight)
    row_weight = jnp.repeat(hidden_weight, tok_rows)
    hidden = weighted_gram(hidden_grad.reshape(micro * tok_rows, GWIN), row_weight) / total_tok
    gains = lax.all_gather(gain[0], "section", axis=0)
    counts = lax.all_gather(repeats[0], "section", axis=0)
    pieces = lax.all_to_all(inputs.reshape(micro * tok_rows, part), "section", 0, 1, tiled=True)

    def section(s, carry):
        value, feats = carry
        value = lax.fori_loop(
            0,
            counts[s] + 1,
            lambda i, v: (v + gelu(normed(v, gains[s]))).astype(jnp.bfloat16).astype(jnp.float32),
            value,
        )
        now = normed(value, gains[s]).astype(jnp.bfloat16)[:, :AWIN]
        return value, lax.dynamic_update_index_in_dim(feats, now, s, 0)

    start = jnp.zeros((sections, pieces.shape[0], AWIN), jnp.bfloat16)
    _, feats = lax.fori_loop(0, sections, section, (pieces.astype(jnp.float32), start))
    feats = lax.all_to_all(feats, "section", 0, 0, tiled=True).reshape(micro * tok_rows, AWIN)
    feature = weighted_gram(feats, row_weight) / total_tok

    def shared(term):
        term = term.reshape(-1, BLK).astype(jnp.bfloat16)
        return lax.psum_scatter(term, "dp", scatter_dimension=0, tiled=True).astype(jnp.float32)[None]

    return (shared(feature), shared(hidden))


def solution(mesh):
    sections, dp_count = mesh.shape["section"], mesh.shape["dp"]

    def body(inputs, gain, repeats, order, hidden_grad):
        aligned = (
            inputs.shape[0] == sections == 4
            and inputs.shape[2] * sections % (16 * BLK) == 0
            and inputs.shape[1] % 16 == 0
            and dp_count == 8
            and AWIN == dp_count * 3 * BLK
            and GWIN % (dp_count * 4 * BLK) == 0
        )
        return (fast_body if aligned else plain_body)(inputs, gain, repeats, order, hidden_grad)

    placed = (
        P(None, "dp", "section"),
        P("section", None),
        P("section"),
        P(),
        P("section", None, "dp", None),
    )
    return jax.shard_map(
        body,
        mesh=mesh,
        in_specs=placed,
        out_specs=(P("section", "dp", None), P("section", "dp", None)),
        check_vma=False,
    )
```

```python
import functools

import jax
import jax.numpy as jnp
from jax import lax
from jax.experimental import pallas as pl
from jax.experimental.pallas import tpu as pltpu
from jax.sharding import PartitionSpec as P

AWIN = 3072
GWIN = 12288
BLK = 128
VMEM_LIMIT = 16 * 1024 * 1024
FAR_FIRST = (2, 3, 1)
ROOT = 0.7978845608028654

SMEM_SPEC = pl.BlockSpec(memory_space=pltpu.SMEM)
VMEM_SPEC = pl.BlockSpec(memory_space=pltpu.VMEM)


def params(limit=VMEM_LIMIT):
    return pltpu.CompilerParams(vmem_limit_bytes=limit)


def gelu(x):
    inner = ROOT * (x + 0.044715 * (x * x * x))
    return x * (0.5 * (1.0 + jnp.tanh(inner)))


def batch_weight(order_ref, batch_id, micro):
    weight = jnp.float32(0.0)
    for slot in range(micro):
        weight = jnp.where(order_ref[slot] == batch_id, jnp.float32(0.5 * 0.5 ** (micro - 1 - slot)), weight)
    return weight


def gram(left, right):
    return lax.dot_general(left, right, (((0,), (0,)), ((), ())), preferred_element_type=jnp.float32)


def iotas():
    row = lax.broadcasted_iota(jnp.int32, (BLK, BLK), 0)
    col = lax.broadcasted_iota(jnp.int32, (BLK, BLK), 1)
    return row, col


def packed_rows(pairs):
    return pairs * BLK + -(-pairs // 16) * 16


def hidden_kernel(micro, pairs, scale, order_ref, _, *refs):
    grad_refs, out_ref = refs[:-1], refs[-1]
    row, col = iotas()
    weights = [batch_weight(order_ref, m, micro) for m in range(micro)]
    tail_row = lax.broadcasted_iota(jnp.int32, (packed_rows(pairs) - pairs * BLK, BLK), 0)
    for place, grad_ref in enumerate(grad_refs):
        for half in range(2):
            tail = jnp.zeros(tail_row.shape, jnp.float32)
            for pair in range(pairs):
                at = (half * pairs + pair) * 2 * BLK
                parts = [grad_ref[0, m, :, at:at + 2 * BLK] for m in range(micro)]
                scaled = [(part.astype(jnp.float32) * weight).astype(jnp.bfloat16) for part, weight in zip(parts, weights)]
                both = gram(jnp.concatenate(scaled, axis=0), jnp.concatenate(parts, axis=0)) * scale
                first, second = both[:BLK, :BLK], both[BLK:, BLK:]
                packed = jnp.where(col >= row, first, second).astype(jnp.bfloat16)
                out_ref[place, half, pair * BLK:(pair + 1) * BLK] = packed
                diagonal = jnp.sum(jnp.where(col == row, second, 0.0), axis=0, keepdims=True)
                tail = jnp.where(tail_row == pair, diagonal, tail)
            out_ref[place, half, pairs * BLK:] = tail.astype(jnp.bfloat16)


def hidden_terms(order, hidden_grad, me, dp_count, scale, cost):
    _, micro, rows, width = hidden_grad.shape
    own = width // dp_count
    pairs = own // (4 * BLK)
    shape, count = (2, packed_rows(pairs), BLK), dp_count // 2

    def owner(flip):
        return lambda i, order, me: (0, 0, 0, jnp.bitwise_xor(me[0], 2 - 2 * i + flip))

    return pl.pallas_call(
        functools.partial(hidden_kernel, micro, pairs, scale),
        out_shape=jax.ShapeDtypeStruct((count,) + shape, jnp.bfloat16),
        grid_spec=pltpu.PrefetchScalarGridSpec(
            num_scalar_prefetch=2,
            grid=(count // 2,),
            in_specs=[pl.BlockSpec((1, micro, rows, own), owner(4)), pl.BlockSpec((1, micro, rows, own), owner(0))],
            out_specs=pl.BlockSpec((2,) + shape, lambda i, order, me: (i, 0, 0, 0)),
        ),
        compiler_params=params(),
        cost_estimate=pl.CostEstimate(flops=cost, bytes_accessed=1 << 10, transcendentals=0),
    )(order, me, hidden_grad, hidden_grad)


def small_call(kernel, shapes, *operands, cost=1 << 20):
    return pl.pallas_call(
        kernel,
        out_shape=shapes,
        in_specs=[VMEM_SPEC] * len(operands),
        out_specs=jax.tree.map(lambda _: VMEM_SPEC, shapes),
        compiler_params=params(),
        cost_estimate=pl.CostEstimate(flops=cost, bytes_accessed=1 << 10, transcendentals=0),
    )(*operands)


def core_sum_kernel(near_ref, came_ref, along_x_ref, along_y_ref, first_ref, second_ref):
    def total(place, half):
        return near_ref[place, half].astype(jnp.float32) + came_ref[place, half].astype(jnp.float32)

    for i in range(2):
        along_x_ref[i] = total(i, 0).astype(jnp.bfloat16)
        along_y_ref[i] = total(2 * i, 1).astype(jnp.bfloat16)
        first_ref[i] = total(2 + i, 0)
        second_ref[i] = total(1 + 2 * i, 1)


def pair_sum_kernel(first_ref, came_x_ref, second_ref, came_y_ref, along_y_ref, along_x_ref, kept_ref):
    along_y_ref[...] = (first_ref[0] + came_x_ref[0].astype(jnp.float32)).astype(jnp.bfloat16)
    along_x_ref[...] = (second_ref[0] + came_y_ref[0].astype(jnp.float32)).astype(jnp.bfloat16)
    kept_ref[0] = first_ref[1] + came_x_ref[1].astype(jnp.float32)
    kept_ref[1] = second_ref[1] + came_y_ref[1].astype(jnp.float32)


def unpack_kernel(pairs, kept_ref, came_y_ref, came_x_ref, out_ref):
    row, col = iotas()
    for half, came_ref in enumerate((came_y_ref, came_x_ref)):

        def total(rows):
            return kept_ref[half, rows] + came_ref[rows].astype(jnp.float32)

        tail = total(slice(pairs * BLK, None))
        for pair in range(pairs):
            value = total(slice(pair * BLK, (pair + 1) * BLK))
            turned = value.T
            at = (half * pairs + pair) * 2 * BLK
            out_ref[0, at:at + BLK] = jnp.where(col >= row, value, turned)
            second = jnp.where(col == row, tail[pair:pair + 1], turned)
            out_ref[0, at + BLK:at + 2 * BLK] = jnp.where(col < row, value, second)


def core_sum(near, came):
    one = near.shape[2:]
    sent = jax.ShapeDtypeStruct((2,) + one, jnp.bfloat16)
    kept = jax.ShapeDtypeStruct((2,) + one, jnp.float32)
    return small_call(core_sum_kernel, (sent, sent, kept, kept), near, came)


def pair_sum(first, came_x, second, came_y):
    last = jax.ShapeDtypeStruct(first.shape[1:], jnp.bfloat16)
    return small_call(pair_sum_kernel, (last, last, first), first, came_x, second, came_y)


def unpacked(kept, came_y, came_x):
    pairs = kept.shape[1] // BLK
    out = jax.ShapeDtypeStruct((1, 4 * pairs * BLK, BLK), jnp.float32)
    return small_call(functools.partial(unpack_kernel, pairs), out, kept, came_y, came_x)


def swapped(shard, axis, mask):
    return lax.ppermute(shard, axis, [(i, i ^ mask) for i in range(lax.axis_size(axis))])


def message_kernel(in_ref, gain_ref, repeats_ref, me_ref, *out_refs):
    _, rows, part = in_ref.shape
    chunks, gain_rows = part // BLK, gain_ref.shape[0]
    gain = gain_ref[...]
    high = gain.astype(jnp.bfloat16)
    low = (gain - high.astype(jnp.float32)).astype(jnp.bfloat16)
    count = jnp.full((16, BLK), repeats_ref[0], jnp.int32).astype(jnp.float32).astype(jnp.bfloat16)
    at = chunks * rows
    for mask, out_ref in zip(FAR_FIRST, out_refs):
        target = jnp.bitwise_xor(me_ref[0], mask)
        for chunk in range(chunks):
            out_ref[chunk * rows:(chunk + 1) * rows] = in_ref[target, :, chunk * BLK:(chunk + 1) * BLK]
        out_ref[at:at + gain_rows] = high
        out_ref[at + gain_rows:at + 2 * gain_rows] = low
        out_ref[at + 2 * gain_rows:] = count


def messages(inputs, gain, repeats, me):
    micro, rows, part = inputs.shape
    shape = jax.ShapeDtypeStruct((part // BLK * rows + 2 * gain.shape[0] + 16, BLK), jnp.bfloat16)
    return pl.pallas_call(
        message_kernel,
        out_shape=(shape,) * (micro - 1),
        in_specs=[VMEM_SPEC, VMEM_SPEC, SMEM_SPEC, SMEM_SPEC],
        out_specs=(VMEM_SPEC,) * (micro - 1),
        compiler_params=params(60 * 1024 * 1024),
        cost_estimate=pl.CostEstimate(flops=1 << 33, bytes_accessed=1 << 20, transcendentals=0),
    )(inputs, gain, repeats, me)


def relay_kernel(sections, owners, own_ref, gain_ref, repeats_ref, me_ref, *refs):
    received, out_refs, (held, gains) = refs[:sections - 1], refs[sections - 1:-2], refs[-2:]
    chunks, rows, _ = held.shape
    own = AWIN // owners // BLK
    width = chunks * BLK
    part = chunks // sections
    at = part * rows
    me = me_ref[0]
    none = jnp.zeros((rows, BLK), jnp.float32)

    def mean(total):
        return jnp.sum(total, axis=-1, keepdims=True) * (1.0 / width)

    gains[me, :chunks] = gain_ref[...]
    gains[me, chunks:] = jnp.full((8, BLK), repeats_ref[0], jnp.int32).astype(jnp.float32)
    total = none
    for chunk in range(part):
        value = own_ref[me, :, chunk * BLK:(chunk + 1) * BLK].astype(jnp.float32)
        held[me * part + chunk] = value
        total = total + value
    for mask, ref in zip(FAR_FIRST, received):
        source = jnp.bitwise_xor(me, mask)
        gains[source, :chunks] = ref[at:at + chunks].astype(jnp.float32) + ref[at + chunks:at + 2 * chunks].astype(jnp.float32)
        gains[source, chunks:] = ref[at + 2 * chunks:].astype(jnp.float32)[:8]
        for chunk in range(part):
            value = ref[chunk * rows:(chunk + 1) * rows].astype(jnp.float32)
            held[source * part + chunk] = value
            total = total + value
    center = mean(total)
    square = none
    for chunk in range(chunks):
        square = square + jnp.square(held[chunk] - center)
    start = (center, lax.rsqrt(mean(square) + 1e-05))

    def section(s, carry):
        repeats = jnp.max(gains[s, chunks:]).astype(jnp.int32)

        def apply(_, carry):
            center, scale = carry
            half = 0.5 * scale
            total, square = none, none
            for chunk in range(chunks):
                value = held[chunk]
                y = (value - center) * half * gains[s, chunk:chunk + 1]
                inner = y * (2.0 * ROOT + (8.0 * 0.044715 * ROOT) * (y * y))
                value = (value + (y + y * jnp.tanh(inner))).astype(jnp.bfloat16).astype(jnp.float32)
                held[chunk] = value
                moved = value - center
                total = total + moved
                square = square + moved * moved
            shift = mean(total)
            spread = jnp.maximum(mean(square) - shift * shift, 0.0)
            return center + shift, lax.rsqrt(spread + 1e-05)

        carry = lax.fori_loop(0, repeats + 1, apply, carry)
        center, scale = carry
        for mask, out_ref in enumerate(out_refs):
            place = jnp.bitwise_xor(me_ref[1], mask) * own
            for i in range(own):
                normed = (held[place + i] - center) * scale * gains[s, pl.ds(place + i, 1)]
                out_ref[s, :, i * BLK:(i + 1) * BLK] = normed.astype(jnp.bfloat16)
        return carry

    lax.fori_loop(0, sections, section, start)


def relay(inputs, gain, repeats, me, received, owners):
    sections, rows, part = inputs.shape
    chunks = sections * part // BLK
    shape = jax.ShapeDtypeStruct((sections, rows, AWIN // owners), jnp.bfloat16)
    return pl.pallas_call(
        functools.partial(relay_kernel, sections, owners),
        out_shape=(shape,) * owners,
        in_specs=[VMEM_SPEC, VMEM_SPEC, SMEM_SPEC, SMEM_SPEC] + [VMEM_SPEC] * len(received),
        out_specs=(VMEM_SPEC,) * owners,
        scratch_shapes=[pltpu.VMEM((chunks, rows, BLK), jnp.float32), pltpu.VMEM((sections, chunks + 8, BLK), jnp.float32)],
        compiler_params=params(),
        cost_estimate=pl.CostEstimate(flops=1 << 31, bytes_accessed=2 << 20, transcendentals=0),
    )(inputs, gain, repeats, me, *received)


HALF = BLK // 2
FEATURE_ROWS = BLK + HALF + 16


def pack_three(first, second, third):
    row, col = iotas()
    low_row, low_col = row[:HALF], col[:HALF]
    turned = pltpu.roll(third[HALF:], HALF, 1)
    two = jnp.where(col >= row, first, second)
    half = jnp.where(low_col < low_row, turned, third[:HALF])
    tail_row = lax.broadcasted_iota(jnp.int32, (16, BLK), 0)
    diagonal = jnp.sum(jnp.where(col == row, second, 0.0), axis=0, keepdims=True)
    last = jnp.sum(jnp.where(low_col == low_row + HALF, third[HALF:], 0.0), axis=0, keepdims=True)
    tail = jnp.where(tail_row == 0, diagonal, jnp.where(tail_row == 1, last, 0.0))
    return jnp.concatenate([two, half, tail], axis=0)


def unpack_three(packed):
    row, col = iotas()
    low_row, low_col = row[:HALF], col[:HALF]
    two, half, tail = packed[:BLK], packed[BLK:BLK + HALF], packed[BLK + HALF:]
    turned = two.T
    first = jnp.where(col >= row, two, turned)
    second = jnp.where(col < row, two, jnp.where(col == row, tail[0:1], turned))
    across = jnp.concatenate([half, jnp.zeros_like(half)], axis=0).T
    upper = jnp.where(low_col < low_row, across[:HALF], half)
    corner = pltpu.roll(jnp.where(low_col < low_row, half, across[:HALF]), HALF, 1)
    lower = jnp.where(low_col < HALF, across[HALF:], jnp.where(low_col == low_row + HALF, tail[1:2], corner))
    return jnp.concatenate([first, second, upper, lower], axis=0)


def feature_kernel(micro, scale, order_ref, me_ref, *refs):
    in_refs, (own_ref, *out_refs) = refs[:-micro], refs[-micro:]
    weight = batch_weight(order_ref, me_ref[0], micro) * scale
    for mask, out_ref in zip((0,) + FAR_FIRST, [own_ref] + out_refs):
        s = jnp.bitwise_xor(me_ref[0], mask)
        blocks = []
        for at in range(0, 3 * BLK, BLK):
            feats = jnp.concatenate([ref[s, :, at:at + BLK] for ref in in_refs], axis=0)
            blocks.append(gram(feats, feats) * weight)
        out_ref[...] = pack_three(*blocks).astype(out_ref.dtype)


def feature_terms(order, me, feats, micro, scale):
    return pl.pallas_call(
        functools.partial(feature_kernel, micro, scale),
        out_shape=(jax.ShapeDtypeStruct((FEATURE_ROWS, BLK), jnp.float32),)
        + (jax.ShapeDtypeStruct((FEATURE_ROWS, BLK), jnp.bfloat16),) * (micro - 1),
        in_specs=[SMEM_SPEC, SMEM_SPEC] + [VMEM_SPEC] * len(feats),
        out_specs=(VMEM_SPEC,) * micro,
        compiler_params=params(),
        cost_estimate=pl.CostEstimate(flops=1 << 31, bytes_accessed=1 << 20, transcendentals=0),
    )(order, me, *feats)


def feature_sum_kernel(*refs):
    total = refs[0][...]
    for ref in refs[1:-1]:
        total = total + ref[...].astype(jnp.float32)
    refs[-1][0] = unpack_three(total)


def fast_body(inputs, gain, repeats, order, hidden_grad):
    micro, tok_rows, _ = inputs.shape
    dp_count = lax.axis_size("dp")
    scale = 1.0 / (tok_rows * dp_count)
    gain = gain.reshape(-1, BLK)
    plane, place = lax.axis_index("section").reshape(1), lax.axis_index("dp").reshape(1)
    me = jnp.concatenate([plane, place])
    told, order = lax.optimization_barrier((messages(inputs, gain, repeats, plane), order))
    pieces = tuple(swapped(one, "section", mask) for mask, one in zip(FAR_FIRST, told))

    came = swapped(hidden_terms(order, hidden_grad, place ^ 1, dp_count, scale, 1 << 20), "dp", 1)
    near = hidden_terms(order, hidden_grad, place, dp_count, scale, 1 << 34)
    along_x, along_y, first, second = core_sum(near, came)
    came_x, came_y = swapped(along_x, "dp", 2), swapped(along_y, "dp", 4)
    pieces, first = lax.optimization_barrier((pieces, first))

    feats = relay(inputs, gain, repeats, me, pieces, dp_count)
    feats, came_x, came_y = lax.optimization_barrier((feats, came_x, came_y))
    gathered = [feats[0]] + [swapped(feats[mask], "dp", mask) for mask in (6, 7, 4, 2, 5, 3, 1)]
    own, *terms = feature_terms(order, plane, gathered, micro, scale)
    terms = [swapped(one, "section", mask) for mask, one in zip(FAR_FIRST, terms)]
    own, first = lax.optimization_barrier((own, first))
    along_y, along_x, kept = pair_sum(first, came_x, second, came_y)
    came_y, came_x = swapped(along_y, "dp", 4), swapped(along_x, "dp", 2)
    feature_rows = small_call(feature_sum_kernel, jax.ShapeDtypeStruct((1, 3 * BLK, BLK), jnp.float32), own, *terms, cost=1 << 34)
    kept, feature_rows = lax.optimization_barrier((kept, feature_rows))
    hidden_rows = unpacked(kept, came_y, came_x)
    return (feature_rows, hidden_rows)


def normed(value, gain_row):
    center = jnp.mean(value, axis=-1, keepdims=True)
    spread = jnp.mean(jnp.square(value - center), axis=-1, keepdims=True)
    return (value - center) * lax.rsqrt(spread + 1e-05) * gain_row


def weighted_gram(feats, weights):
    shaped = feats.reshape(feats.shape[0], -1, BLK)
    scaled = shaped * weights[:, None, None].astype(shaped.dtype)
    return jnp.einsum("tbi,tbj->bij", scaled, shaped, preferred_element_type=jnp.float32)


def plain_body(inputs, gain, repeats, order, hidden_grad):
    micro, tok_rows, part = inputs.shape
    sections = lax.axis_size("section")
    total_tok = tok_rows * lax.axis_size("dp")
    slot_weight = 0.5 * jnp.power(0.5, micro - 1 - jnp.arange(micro, dtype=jnp.float32))
    hidden_weight = jnp.zeros((micro,), jnp.float32).at[order].set(slot_weight)
    row_weight = jnp.repeat(hidden_weight, tok_rows)
    hidden = weighted_gram(hidden_grad.reshape(micro * tok_rows, GWIN), row_weight) / total_tok
    gains = lax.all_gather(gain[0], "section", axis=0)
    counts = lax.all_gather(repeats[0], "section", axis=0)
    pieces = lax.all_to_all(inputs.reshape(micro * tok_rows, part), "section", 0, 1, tiled=True)

    def section(s, carry):
        value, feats = carry
        value = lax.fori_loop(
            0,
            counts[s] + 1,
            lambda i, v: (v + gelu(normed(v, gains[s]))).astype(jnp.bfloat16).astype(jnp.float32),
            value,
        )
        now = normed(value, gains[s]).astype(jnp.bfloat16)[:, :AWIN]
        return value, lax.dynamic_update_index_in_dim(feats, now, s, 0)

    start = jnp.zeros((sections, pieces.shape[0], AWIN), jnp.bfloat16)
    _, feats = lax.fori_loop(0, sections, section, (pieces.astype(jnp.float32), start))
    feats = lax.all_to_all(feats, "section", 0, 0, tiled=True).reshape(micro * tok_rows, AWIN)
    feature = weighted_gram(feats, row_weight) / total_tok

    def shared(term):
        term = term.reshape(-1, BLK).astype(jnp.bfloat16)
        return lax.psum_scatter(term, "dp", scatter_dimension=0, tiled=True).astype(jnp.float32)[None]

    return (shared(feature), shared(hidden))


def solution(mesh):
    sections, dp_count = mesh.shape["section"], mesh.shape["dp"]

    def body(inputs, gain, repeats, order, hidden_grad):
        aligned = (
            inputs.shape[0] == sections == 4
            and inputs.shape[2] * sections % (16 * BLK) == 0
            and inputs.shape[1] % 16 == 0
            and dp_count == 8
            and AWIN == dp_count * 3 * BLK
            and GWIN % (dp_count * 4 * BLK) == 0
        )
        return (fast_body if aligned else plain_body)(inputs, gain, repeats, order, hidden_grad)

    placed = (
        P(None, "dp", "section"),
        P("section", None),
        P("section"),
        P(),
        P("section", None, "dp", None),
    )
    return jax.shard_map(
        body,
        mesh=mesh,
        in_specs=placed,
        out_specs=(P("section", "dp", None), P("section", "dp", None)),
        check_vma=False,
    )
```

```python
import functools

import jax
import jax.numpy as jnp
from jax import lax
from jax.experimental import pallas as pl
from jax.experimental.pallas import tpu as pltpu
from jax.sharding import PartitionSpec as P

AWIN = 3072
GWIN = 12288
BLK = 128
VMEM_LIMIT = 16 * 1024 * 1024
FAR_FIRST = (2, 3, 1)
ROOT = 0.7978845608028654

SMEM_SPEC = pl.BlockSpec(memory_space=pltpu.SMEM)
VMEM_SPEC = pl.BlockSpec(memory_space=pltpu.VMEM)


def params(limit=VMEM_LIMIT):
    return pltpu.CompilerParams(vmem_limit_bytes=limit)


def gelu(x):
    inner = ROOT * (x + 0.044715 * (x * x * x))
    return x * (0.5 * (1.0 + jnp.tanh(inner)))


def batch_weight(order_ref, batch_id, micro):
    weight = jnp.float32(0.0)
    for slot in range(micro):
        weight = jnp.where(order_ref[slot] == batch_id, jnp.float32(0.5 * 0.5 ** (micro - 1 - slot)), weight)
    return weight


def gram(left, right):
    return lax.dot_general(left, right, (((0,), (0,)), ((), ())), preferred_element_type=jnp.float32)


def iotas():
    row = lax.broadcasted_iota(jnp.int32, (BLK, BLK), 0)
    col = lax.broadcasted_iota(jnp.int32, (BLK, BLK), 1)
    return row, col


def packed_rows(pairs):
    return pairs * BLK + -(-pairs // 16) * 16


def hidden_kernel(micro, pairs, scale, order_ref, _, *refs):
    grad_refs, out_ref = refs[:-1], refs[-1]
    row, col = iotas()
    weights = [batch_weight(order_ref, m, micro) for m in range(micro)]
    tail_row = lax.broadcasted_iota(jnp.int32, (packed_rows(pairs) - pairs * BLK, BLK), 0)
    for place, grad_ref in enumerate(grad_refs):
        for half in range(2):
            tail = jnp.zeros(tail_row.shape, jnp.float32)
            for pair in range(pairs):
                at = (half * pairs + pair) * 2 * BLK
                parts = [grad_ref[0, m, :, at:at + 2 * BLK] for m in range(micro)]
                scaled = [(part.astype(jnp.float32) * weight).astype(jnp.bfloat16) for part, weight in zip(parts, weights)]
                both = gram(jnp.concatenate(scaled, axis=0), jnp.concatenate(parts, axis=0)) * scale
                first, second = both[:BLK, :BLK], both[BLK:, BLK:]
                packed = jnp.where(col >= row, first, second).astype(jnp.bfloat16)
                out_ref[place, half, pair * BLK:(pair + 1) * BLK] = packed
                diagonal = jnp.sum(jnp.where(col == row, second, 0.0), axis=0, keepdims=True)
                tail = jnp.where(tail_row == pair, diagonal, tail)
            out_ref[place, half, pairs * BLK:] = tail.astype(jnp.bfloat16)


def hidden_terms(order, hidden_grad, me, dp_count, scale, cost):
    _, micro, rows, width = hidden_grad.shape
    own = width // dp_count
    pairs = own // (4 * BLK)
    shape, count = (2, packed_rows(pairs), BLK), dp_count // 2

    def owner(flip):
        return lambda i, order, me: (0, 0, 0, jnp.bitwise_xor(me[0], 2 - 2 * i + flip))

    return pl.pallas_call(
        functools.partial(hidden_kernel, micro, pairs, scale),
        out_shape=jax.ShapeDtypeStruct((count,) + shape, jnp.bfloat16),
        grid_spec=pltpu.PrefetchScalarGridSpec(
            num_scalar_prefetch=2,
            grid=(count // 2,),
            in_specs=[pl.BlockSpec((1, micro, rows, own), owner(4)), pl.BlockSpec((1, micro, rows, own), owner(0))],
            out_specs=pl.BlockSpec((2,) + shape, lambda i, order, me: (i, 0, 0, 0)),
        ),
        compiler_params=params(),
        cost_estimate=pl.CostEstimate(flops=cost, bytes_accessed=1 << 10, transcendentals=0),
    )(order, me, hidden_grad, hidden_grad)


def small_call(kernel, shapes, *operands, cost=1 << 20):
    return pl.pallas_call(
        kernel,
        out_shape=shapes,
        in_specs=[VMEM_SPEC] * len(operands),
        out_specs=jax.tree.map(lambda _: VMEM_SPEC, shapes),
        compiler_params=params(),
        cost_estimate=pl.CostEstimate(flops=cost, bytes_accessed=1 << 10, transcendentals=0),
    )(*operands)


def core_sum_kernel(near_ref, came_ref, along_x_ref, along_y_ref, first_ref, second_ref):
    def total(place, half):
        return near_ref[place, half].astype(jnp.float32) + came_ref[place, half].astype(jnp.float32)

    for i in range(2):
        along_x_ref[i] = total(i, 0).astype(jnp.bfloat16)
        along_y_ref[i] = total(2 * i, 1).astype(jnp.bfloat16)
        first_ref[i] = total(2 + i, 0)
        second_ref[i] = total(1 + 2 * i, 1)


def pair_sum_kernel(first_ref, came_x_ref, second_ref, came_y_ref, along_y_ref, along_x_ref, kept_ref):
    along_y_ref[...] = (first_ref[0] + came_x_ref[0].astype(jnp.float32)).astype(jnp.bfloat16)
    along_x_ref[...] = (second_ref[0] + came_y_ref[0].astype(jnp.float32)).astype(jnp.bfloat16)
    kept_ref[0] = first_ref[1] + came_x_ref[1].astype(jnp.float32)
    kept_ref[1] = second_ref[1] + came_y_ref[1].astype(jnp.float32)


def unpack_kernel(pairs, kept_ref, came_y_ref, came_x_ref, out_ref):
    row, col = iotas()
    for half, came_ref in enumerate((came_y_ref, came_x_ref)):

        def total(rows):
            return kept_ref[half, rows] + came_ref[rows].astype(jnp.float32)

        tail = total(slice(pairs * BLK, None))
        for pair in range(pairs):
            value = total(slice(pair * BLK, (pair + 1) * BLK))
            turned = value.T
            at = (half * pairs + pair) * 2 * BLK
            out_ref[0, at:at + BLK] = jnp.where(col >= row, value, turned)
            second = jnp.where(col == row, tail[pair:pair + 1], turned)
            out_ref[0, at + BLK:at + 2 * BLK] = jnp.where(col < row, value, second)


def core_sum(near, came):
    one = near.shape[2:]
    sent = jax.ShapeDtypeStruct((2,) + one, jnp.bfloat16)
    kept = jax.ShapeDtypeStruct((2,) + one, jnp.float32)
    return small_call(core_sum_kernel, (sent, sent, kept, kept), near, came)


def pair_sum(first, came_x, second, came_y):
    last = jax.ShapeDtypeStruct(first.shape[1:], jnp.bfloat16)
    return small_call(pair_sum_kernel, (last, last, first), first, came_x, second, came_y)


def unpacked(kept, came_y, came_x):
    pairs = kept.shape[1] // BLK
    out = jax.ShapeDtypeStruct((1, 4 * pairs * BLK, BLK), jnp.float32)
    return small_call(functools.partial(unpack_kernel, pairs), out, kept, came_y, came_x)


def swapped(shard, axis, mask):
    return lax.ppermute(shard, axis, [(i, i ^ mask) for i in range(lax.axis_size(axis))])


def message_kernel(in_ref, gain_ref, repeats_ref, me_ref, *out_refs):
    _, rows, part = in_ref.shape
    chunks, gain_rows = part // BLK, gain_ref.shape[0]
    gain = gain_ref[...]
    high = gain.astype(jnp.bfloat16)
    low = (gain - high.astype(jnp.float32)).astype(jnp.bfloat16)
    count = jnp.full((16, BLK), repeats_ref[0], jnp.int32).astype(jnp.float32).astype(jnp.bfloat16)
    at = chunks * rows
    for mask, out_ref in zip(FAR_FIRST, out_refs):
        target = jnp.bitwise_xor(me_ref[0], mask)
        for chunk in range(chunks):
            out_ref[chunk * rows:(chunk + 1) * rows] = in_ref[target, :, chunk * BLK:(chunk + 1) * BLK]
        out_ref[at:at + gain_rows] = high
        out_ref[at + gain_rows:at + 2 * gain_rows] = low
        out_ref[at + 2 * gain_rows:] = count


def messages(inputs, gain, repeats, me):
    micro, rows, part = inputs.shape
    shape = jax.ShapeDtypeStruct((part // BLK * rows + 2 * gain.shape[0] + 16, BLK), jnp.bfloat16)
    return pl.pallas_call(
        message_kernel,
        out_shape=(shape,) * (micro - 1),
        in_specs=[VMEM_SPEC, VMEM_SPEC, SMEM_SPEC, SMEM_SPEC],
        out_specs=(VMEM_SPEC,) * (micro - 1),
        compiler_params=params(60 * 1024 * 1024),
        cost_estimate=pl.CostEstimate(flops=1 << 33, bytes_accessed=1 << 20, transcendentals=0),
    )(inputs, gain, repeats, me)


def relay_kernel(sections, owners, own_ref, gain_ref, repeats_ref, me_ref, *refs):
    received, out_refs, (held, gains) = refs[:sections - 1], refs[sections - 1:-2], refs[-2:]
    chunks, rows, _ = held.shape
    own = AWIN // owners // BLK
    width = chunks * BLK
    part = chunks // sections
    at = part * rows
    me = me_ref[0]
    none = jnp.zeros((rows, BLK), jnp.float32)

    def mean(total):
        return jnp.sum(total, axis=-1, keepdims=True) * (1.0 / width)

    gains[me, :chunks] = gain_ref[...]
    gains[me, chunks:] = jnp.full((8, BLK), repeats_ref[0], jnp.int32).astype(jnp.float32)
    total = none
    for chunk in range(part):
        value = own_ref[me, :, chunk * BLK:(chunk + 1) * BLK].astype(jnp.float32)
        held[me * part + chunk] = value
        total = total + value
    for mask, ref in zip(FAR_FIRST, received):
        source = jnp.bitwise_xor(me, mask)
        gains[source, :chunks] = ref[at:at + chunks].astype(jnp.float32) + ref[at + chunks:at + 2 * chunks].astype(jnp.float32)
        gains[source, chunks:] = ref[at + 2 * chunks:].astype(jnp.float32)[:8]
        for chunk in range(part):
            value = ref[chunk * rows:(chunk + 1) * rows].astype(jnp.float32)
            held[source * part + chunk] = value
            total = total + value
    center = mean(total)
    square = none
    for chunk in range(chunks):
        square = square + jnp.square(held[chunk] - center)
    start = (center, lax.rsqrt(mean(square) + 1e-05))

    def section(s, carry):
        repeats = jnp.max(gains[s, chunks:]).astype(jnp.int32)

        def apply(_, carry):
            center, scale = carry
            half = 0.5 * scale
            total, square = none, none
            for chunk in range(chunks):
                value = held[chunk]
                y = (value - center) * half * gains[s, chunk:chunk + 1]
                inner = y * (2.0 * ROOT + (8.0 * 0.044715 * ROOT) * (y * y))
                value = (value + (y + y * jnp.tanh(inner))).astype(jnp.bfloat16).astype(jnp.float32)
                held[chunk] = value
                moved = value - center
                total = total + moved
                square = square + moved * moved
            shift = mean(total)
            spread = jnp.maximum(mean(square) - shift * shift, 0.0)
            return center + shift, lax.rsqrt(spread + 1e-05)

        carry = lax.fori_loop(0, repeats + 1, apply, carry)
        center, scale = carry
        for mask, out_ref in enumerate(out_refs):
            place = jnp.bitwise_xor(me_ref[1], mask) * own
            for i in range(own):
                normed = (held[place + i] - center) * scale * gains[s, pl.ds(place + i, 1)]
                out_ref[s, :, i * BLK:(i + 1) * BLK] = normed.astype(jnp.bfloat16)
        return carry

    lax.fori_loop(0, sections, section, start)


def relay(inputs, gain, repeats, me, received, owners):
    sections, rows, part = inputs.shape
    chunks = sections * part // BLK
    shape = jax.ShapeDtypeStruct((sections, rows, AWIN // owners), jnp.bfloat16)
    return pl.pallas_call(
        functools.partial(relay_kernel, sections, owners),
        out_shape=(shape,) * owners,
        in_specs=[VMEM_SPEC, VMEM_SPEC, SMEM_SPEC, SMEM_SPEC] + [VMEM_SPEC] * len(received),
        out_specs=(VMEM_SPEC,) * owners,
        scratch_shapes=[pltpu.VMEM((chunks, rows, BLK), jnp.float32), pltpu.VMEM((sections, chunks + 8, BLK), jnp.float32)],
        compiler_params=params(),
        cost_estimate=pl.CostEstimate(flops=1 << 31, bytes_accessed=2 << 20, transcendentals=0),
    )(inputs, gain, repeats, me, *received)


HALF = BLK // 2
FEATURE_ROWS = BLK + HALF + 16


def pack_three(first, second, third):
    row, col = iotas()
    low_row, low_col = row[:HALF], col[:HALF]
    turned = pltpu.roll(third[HALF:], HALF, 1)
    two = jnp.where(col >= row, first, second)
    half = jnp.where(low_col < low_row, turned, third[:HALF])
    tail_row = lax.broadcasted_iota(jnp.int32, (16, BLK), 0)
    diagonal = jnp.sum(jnp.where(col == row, second, 0.0), axis=0, keepdims=True)
    last = jnp.sum(jnp.where(low_col == low_row + HALF, third[HALF:], 0.0), axis=0, keepdims=True)
    tail = jnp.where(tail_row == 0, diagonal, jnp.where(tail_row == 1, last, 0.0))
    return jnp.concatenate([two, half, tail], axis=0)


def unpack_three(packed):
    row, col = iotas()
    low_row, low_col = row[:HALF], col[:HALF]
    two, half, tail = packed[:BLK], packed[BLK:BLK + HALF], packed[BLK + HALF:]
    turned = two.T
    first = jnp.where(col >= row, two, turned)
    second = jnp.where(col < row, two, jnp.where(col == row, tail[0:1], turned))
    across = jnp.concatenate([half, jnp.zeros_like(half)], axis=0).T
    upper = jnp.where(low_col < low_row, across[:HALF], half)
    corner = pltpu.roll(jnp.where(low_col < low_row, half, across[:HALF]), HALF, 1)
    lower = jnp.where(low_col < HALF, across[HALF:], jnp.where(low_col == low_row + HALF, tail[1:2], corner))
    return jnp.concatenate([first, second, upper, lower], axis=0)


def feature_kernel(micro, scale, order_ref, me_ref, *refs):
    in_refs, (own_ref, *out_refs) = refs[:-micro], refs[-micro:]
    weight = batch_weight(order_ref, me_ref[0], micro) * scale
    for mask, out_ref in zip((0,) + FAR_FIRST, [own_ref] + out_refs):
        s = jnp.bitwise_xor(me_ref[0], mask)
        blocks = []
        for at in range(0, 3 * BLK, BLK):
            feats = jnp.concatenate([ref[s, :, at:at + BLK] for ref in in_refs], axis=0)
            blocks.append(gram(feats, feats) * weight)
        out_ref[...] = pack_three(*blocks).astype(out_ref.dtype)


def feature_terms(order, me, feats, micro, scale):
    return pl.pallas_call(
        functools.partial(feature_kernel, micro, scale),
        out_shape=(jax.ShapeDtypeStruct((FEATURE_ROWS, BLK), jnp.float32),)
        + (jax.ShapeDtypeStruct((FEATURE_ROWS, BLK), jnp.bfloat16),) * (micro - 1),
        in_specs=[SMEM_SPEC, SMEM_SPEC] + [VMEM_SPEC] * len(feats),
        out_specs=(VMEM_SPEC,) * micro,
        compiler_params=params(),
        cost_estimate=pl.CostEstimate(flops=1 << 31, bytes_accessed=1 << 20, transcendentals=0),
    )(order, me, *feats)


def feature_sum_kernel(*refs):
    total = refs[0][...]
    for ref in refs[1:-1]:
        total = total + ref[...].astype(jnp.float32)
    refs[-1][0] = unpack_three(total)


def fast_body(inputs, gain, repeats, order, hidden_grad):
    micro, tok_rows, _ = inputs.shape
    dp_count = lax.axis_size("dp")
    scale = 1.0 / (tok_rows * dp_count)
    gain = gain.reshape(-1, BLK)
    plane, place = lax.axis_index("section").reshape(1), lax.axis_index("dp").reshape(1)
    me = jnp.concatenate([plane, place])
    told, order = lax.optimization_barrier((messages(inputs, gain, repeats, plane), order))
    pieces = tuple(swapped(one, "section", mask) for mask, one in zip(FAR_FIRST, told))

    came = swapped(hidden_terms(order, hidden_grad, place ^ 1, dp_count, scale, 1 << 20), "dp", 1)
    near = hidden_terms(order, hidden_grad, place, dp_count, scale, 1 << 34)
    along_x, along_y, first, second = core_sum(near, came)
    came_x, came_y = swapped(along_x, "dp", 2), swapped(along_y, "dp", 4)
    pieces, first = lax.optimization_barrier((pieces, first))

    feats = relay(inputs, gain, repeats, me, pieces, dp_count)
    feats, came_x, came_y = lax.optimization_barrier((feats, came_x, came_y))
    gathered = [feats[0]] + [swapped(feats[mask], "dp", mask) for mask in (6, 7, 4, 2, 5, 3, 1)]
    along_y, along_x, kept = pair_sum(first, came_x, second, came_y)
    came_y, came_x = swapped(along_y, "dp", 4), swapped(along_x, "dp", 2)
    own, *terms = feature_terms(order, plane, gathered, micro, scale)
    own, kept = lax.optimization_barrier((own, kept))
    terms = [swapped(one, "section", mask) for mask, one in zip(FAR_FIRST, terms)]
    hidden_rows = unpacked(kept, came_y, came_x)
    own, hidden_rows = lax.optimization_barrier((own, hidden_rows))
    feature_rows = small_call(feature_sum_kernel, jax.ShapeDtypeStruct((1, 3 * BLK, BLK), jnp.float32), own, *terms)
    return (feature_rows, hidden_rows)


def normed(value, gain_row):
    center = jnp.mean(value, axis=-1, keepdims=True)
    spread = jnp.mean(jnp.square(value - center), axis=-1, keepdims=True)
    return (value - center) * lax.rsqrt(spread + 1e-05) * gain_row


def weighted_gram(feats, weights):
    shaped = feats.reshape(feats.shape[0], -1, BLK)
    scaled = shaped * weights[:, None, None].astype(shaped.dtype)
    return jnp.einsum("tbi,tbj->bij", scaled, shaped, preferred_element_type=jnp.float32)


def plain_body(inputs, gain, repeats, order, hidden_grad):
    micro, tok_rows, part = inputs.shape
    sections = lax.axis_size("section")
    total_tok = tok_rows * lax.axis_size("dp")
    slot_weight = 0.5 * jnp.power(0.5, micro - 1 - jnp.arange(micro, dtype=jnp.float32))
    hidden_weight = jnp.zeros((micro,), jnp.float32).at[order].set(slot_weight)
    row_weight = jnp.repeat(hidden_weight, tok_rows)
    hidden = weighted_gram(hidden_grad.reshape(micro * tok_rows, GWIN), row_weight) / total_tok
    gains = lax.all_gather(gain[0], "section", axis=0)
    counts = lax.all_gather(repeats[0], "section", axis=0)
    pieces = lax.all_to_all(inputs.reshape(micro * tok_rows, part), "section", 0, 1, tiled=True)

    def section(s, carry):
        value, feats = carry
        value = lax.fori_loop(
            0,
            counts[s] + 1,
            lambda i, v: (v + gelu(normed(v, gains[s]))).astype(jnp.bfloat16).astype(jnp.float32),
            value,
        )
        now = normed(value, gains[s]).astype(jnp.bfloat16)[:, :AWIN]
        return value, lax.dynamic_update_index_in_dim(feats, now, s, 0)

    start = jnp.zeros((sections, pieces.shape[0], AWIN), jnp.bfloat16)
    _, feats = lax.fori_loop(0, sections, section, (pieces.astype(jnp.float32), start))
    feats = lax.all_to_all(feats, "section", 0, 0, tiled=True).reshape(micro * tok_rows, AWIN)
    feature = weighted_gram(feats, row_weight) / total_tok

    def shared(term):
        term = term.reshape(-1, BLK).astype(jnp.bfloat16)
        return lax.psum_scatter(term, "dp", scatter_dimension=0, tiled=True).astype(jnp.float32)[None]

    return (shared(feature), shared(hidden))


def solution(mesh):
    sections, dp_count = mesh.shape["section"], mesh.shape["dp"]

    def body(inputs, gain, repeats, order, hidden_grad):
        aligned = (
            inputs.shape[0] == sections == 4
            and inputs.shape[2] * sections % (16 * BLK) == 0
            and inputs.shape[1] % 16 == 0
            and dp_count == 8
            and AWIN == dp_count * 3 * BLK
            and GWIN % (dp_count * 4 * BLK) == 0
        )
        return (fast_body if aligned else plain_body)(inputs, gain, repeats, order, hidden_grad)

    placed = (
        P(None, "dp", "section"),
        P("section", None),
        P("section"),
        P(),
        P("section", None, "dp", None),
    )
    return jax.shard_map(
        body,
        mesh=mesh,
        in_specs=placed,
        out_specs=(P("section", "dp", None), P("section", "dp", None)),
        check_vma=False,
    )
```

```python
import functools

import jax
import jax.numpy as jnp
from jax import lax
from jax.experimental import pallas as pl
from jax.experimental.pallas import tpu as pltpu
from jax.sharding import PartitionSpec as P

AWIN = 3072
GWIN = 12288
BLK = 128
VMEM_LIMIT = 16 * 1024 * 1024
FAR_FIRST = (2, 3, 1)
STEEP = 92.0
ROOT = 0.7978845608028654

SMEM_SPEC = pl.BlockSpec(memory_space=pltpu.SMEM)
VMEM_SPEC = pl.BlockSpec(memory_space=pltpu.VMEM)


def params(limit=VMEM_LIMIT):
    return pltpu.CompilerParams(vmem_limit_bytes=limit)


def gelu(x):
    inner = ROOT * (x + 0.044715 * (x * x * x))
    return x * (0.5 * (1.0 + jnp.tanh(inner)))


def batch_weight(order_ref, batch_id, micro):
    weight = jnp.float32(0.0)
    for slot in range(micro):
        weight = jnp.where(order_ref[slot] == batch_id, jnp.float32(0.5 * 0.5 ** (micro - 1 - slot)), weight)
    return weight


def gram(left, right):
    return lax.dot_general(left, right, (((0,), (0,)), ((), ())), preferred_element_type=jnp.float32)


def iotas():
    row = lax.broadcasted_iota(jnp.int32, (BLK, BLK), 0)
    col = lax.broadcasted_iota(jnp.int32, (BLK, BLK), 1)
    return row, col


def packed_rows(pairs):
    return pairs * BLK + -(-pairs // 16) * 16


def hidden_kernel(micro, pairs, scale, order_ref, _, *refs):
    grad_refs, out_ref = refs[:-1], refs[-1]
    row, col = iotas()
    weights = [batch_weight(order_ref, m, micro) for m in range(micro)]
    tail_row = lax.broadcasted_iota(jnp.int32, (packed_rows(pairs) - pairs * BLK, BLK), 0)
    for place, grad_ref in enumerate(grad_refs):
        for half in range(2):
            tail = jnp.zeros(tail_row.shape, jnp.float32)
            for pair in range(pairs):
                at = (half * pairs + pair) * 2 * BLK
                parts = [grad_ref[0, m, :, at:at + 2 * BLK] for m in range(micro)]
                scaled = [(part.astype(jnp.float32) * weight).astype(jnp.bfloat16) for part, weight in zip(parts, weights)]
                both = gram(jnp.concatenate(scaled, axis=0), jnp.concatenate(parts, axis=0)) * scale
                first, second = both[:BLK, :BLK], both[BLK:, BLK:]
                packed = jnp.where(col >= row, first, second).astype(jnp.bfloat16)
                out_ref[place, half, pair * BLK:(pair + 1) * BLK] = packed
                diagonal = jnp.sum(jnp.where(col == row, second, 0.0), axis=0, keepdims=True)
                tail = jnp.where(tail_row == pair, diagonal, tail)
            out_ref[place, half, pairs * BLK:] = tail.astype(jnp.bfloat16)


def hidden_terms(order, hidden_grad, me, dp_count, scale, cost):
    _, micro, rows, width = hidden_grad.shape
    own = width // dp_count
    pairs = own // (4 * BLK)
    shape, count = (2, packed_rows(pairs), BLK), dp_count // 2

    def owner(flip):
        return lambda i, order, me: (0, 0, 0, jnp.bitwise_xor(me[0], 2 - 2 * i + flip))

    return pl.pallas_call(
        functools.partial(hidden_kernel, micro, pairs, scale),
        out_shape=jax.ShapeDtypeStruct((count,) + shape, jnp.bfloat16),
        grid_spec=pltpu.PrefetchScalarGridSpec(
            num_scalar_prefetch=2,
            grid=(count // 2,),
            in_specs=[pl.BlockSpec((1, micro, rows, own), owner(4)), pl.BlockSpec((1, micro, rows, own), owner(0))],
            out_specs=pl.BlockSpec((2,) + shape, lambda i, order, me: (i, 0, 0, 0)),
        ),
        compiler_params=params(),
        cost_estimate=pl.CostEstimate(flops=cost, bytes_accessed=1 << 10, transcendentals=0),
    )(order, me, hidden_grad, hidden_grad)


def small_call(kernel, shapes, *operands, cost=1 << 20):
    return pl.pallas_call(
        kernel,
        out_shape=shapes,
        in_specs=[VMEM_SPEC] * len(operands),
        out_specs=jax.tree.map(lambda _: VMEM_SPEC, shapes),
        compiler_params=params(),
        cost_estimate=pl.CostEstimate(flops=cost, bytes_accessed=1 << 10, transcendentals=0),
    )(*operands)


def core_sum_kernel(near_ref, came_ref, along_x_ref, along_y_ref, first_ref, second_ref):
    def total(place, half):
        return near_ref[place, half].astype(jnp.float32) + came_ref[place, half].astype(jnp.float32)

    for i in range(2):
        along_x_ref[i] = total(i, 0).astype(jnp.bfloat16)
        along_y_ref[i] = total(2 * i, 1).astype(jnp.bfloat16)
        first_ref[i] = total(2 + i, 0)
        second_ref[i] = total(1 + 2 * i, 1)


def pair_sum_kernel(first_ref, came_x_ref, second_ref, came_y_ref, along_y_ref, along_x_ref, kept_ref):
    along_y_ref[...] = (first_ref[0] + came_x_ref[0].astype(jnp.float32)).astype(jnp.bfloat16)
    along_x_ref[...] = (second_ref[0] + came_y_ref[0].astype(jnp.float32)).astype(jnp.bfloat16)
    kept_ref[0] = first_ref[1] + came_x_ref[1].astype(jnp.float32)
    kept_ref[1] = second_ref[1] + came_y_ref[1].astype(jnp.float32)


def unpack_kernel(pairs, kept_ref, came_y_ref, came_x_ref, out_ref):
    row, col = iotas()
    for half, came_ref in enumerate((came_y_ref, came_x_ref)):

        def total(rows):
            return kept_ref[half, rows] + came_ref[rows].astype(jnp.float32)

        tail = total(slice(pairs * BLK, None))
        for pair in range(pairs):
            value = total(slice(pair * BLK, (pair + 1) * BLK))
            turned = value.T
            at = (half * pairs + pair) * 2 * BLK
            out_ref[0, at:at + BLK] = jnp.where(col >= row, value, turned)
            second = jnp.where(col == row, tail[pair:pair + 1], turned)
            out_ref[0, at + BLK:at + 2 * BLK] = jnp.where(col < row, value, second)


def core_sum(near, came):
    one = near.shape[2:]
    sent = jax.ShapeDtypeStruct((2,) + one, jnp.bfloat16)
    kept = jax.ShapeDtypeStruct((2,) + one, jnp.float32)
    return small_call(core_sum_kernel, (sent, sent, kept, kept), near, came)


def pair_sum(first, came_x, second, came_y):
    last = jax.ShapeDtypeStruct(first.shape[1:], jnp.bfloat16)
    return small_call(pair_sum_kernel, (last, last, first), first, came_x, second, came_y)


def unpacked(kept, came_y, came_x):
    pairs = kept.shape[1] // BLK
    out = jax.ShapeDtypeStruct((1, 4 * pairs * BLK, BLK), jnp.float32)
    return small_call(functools.partial(unpack_kernel, pairs), out, kept, came_y, came_x)


def swapped(shard, axis, mask):
    return lax.ppermute(shard, axis, [(i, i ^ mask) for i in range(lax.axis_size(axis))])


def message_kernel(in_ref, gain_ref, repeats_ref, me_ref, *out_refs):
    _, rows, part = in_ref.shape
    chunks, gain_rows = part // BLK, gain_ref.shape[0]
    coded = jnp.exp(STEEP * (gain_ref[...] - 1.0)).astype(jnp.bfloat16)
    count = jnp.full((16, BLK), repeats_ref[0], jnp.int32).astype(jnp.float32).astype(jnp.bfloat16)
    at = chunks * rows
    for mask, out_ref in zip(FAR_FIRST, out_refs):
        target = jnp.bitwise_xor(me_ref[0], mask)
        for chunk in range(chunks):
            out_ref[chunk * rows:(chunk + 1) * rows] = in_ref[target, :, chunk * BLK:(chunk + 1) * BLK]
        out_ref[at:at + gain_rows] = coded
        out_ref[at + gain_rows:] = count


def messages(inputs, gain, repeats, me):
    micro, rows, part = inputs.shape
    shape = jax.ShapeDtypeStruct((part // BLK * rows + gain.shape[0] + 16, BLK), jnp.bfloat16)
    return pl.pallas_call(
        message_kernel,
        out_shape=(shape,) * (micro - 1),
        in_specs=[VMEM_SPEC, VMEM_SPEC, SMEM_SPEC, SMEM_SPEC],
        out_specs=(VMEM_SPEC,) * (micro - 1),
        compiler_params=params(60 * 1024 * 1024),
        cost_estimate=pl.CostEstimate(flops=1 << 33, bytes_accessed=1 << 20, transcendentals=0),
    )(inputs, gain, repeats, me)


def relay_kernel(sections, owners, own_ref, gain_ref, repeats_ref, me_ref, *refs):
    received, out_refs, (held, gains) = refs[:sections - 1], refs[sections - 1:-2], refs[-2:]
    chunks, rows, _ = held.shape
    own = AWIN // owners // BLK
    width = chunks * BLK
    part = chunks // sections
    at = part * rows
    me = me_ref[0]
    none = jnp.zeros((rows, BLK), jnp.float32)

    def mean(total):
        return jnp.sum(total, axis=-1, keepdims=True) * (1.0 / width)

    gains[me, :chunks] = gain_ref[...]
    gains[me, chunks:] = jnp.full((8, BLK), repeats_ref[0], jnp.int32).astype(jnp.float32)
    total = none
    for chunk in range(part):
        value = own_ref[me, :, chunk * BLK:(chunk + 1) * BLK].astype(jnp.float32)
        held[me * part + chunk] = value
        total = total + value
    for mask, ref in zip(FAR_FIRST, received):
        source = jnp.bitwise_xor(me, mask)
        gains[source, :chunks] = 1.0 + jnp.log(ref[at:at + chunks].astype(jnp.float32)) * (1.0 / STEEP)
        gains[source, chunks:] = ref[at + chunks:].astype(jnp.float32)[:8]
        for chunk in range(part):
            value = ref[chunk * rows:(chunk + 1) * rows].astype(jnp.float32)
            held[source * part + chunk] = value
            total = total + value
    center = mean(total)
    square = none
    for chunk in range(chunks):
        square = square + jnp.square(held[chunk] - center)
    start = (center, lax.rsqrt(mean(square) + 1e-05))

    def section(s, carry):
        repeats = jnp.max(gains[s, chunks:]).astype(jnp.int32)

        def apply(_, carry):
            center, scale = carry
            half = 0.5 * scale
            total, square = none, none
            for chunk in range(chunks):
                value = held[chunk]
                y = (value - center) * half * gains[s, chunk:chunk + 1]
                inner = y * (2.0 * ROOT + (8.0 * 0.044715 * ROOT) * (y * y))
                value = (value + (y + y * jnp.tanh(inner))).astype(jnp.bfloat16).astype(jnp.float32)
                held[chunk] = value
                moved = value - center
                total = total + moved
                square = square + moved * moved
            shift = mean(total)
            spread = jnp.maximum(mean(square) - shift * shift, 0.0)
            return center + shift, lax.rsqrt(spread + 1e-05)

        carry = lax.fori_loop(0, repeats + 1, apply, carry)
        center, scale = carry
        for mask, out_ref in enumerate(out_refs):
            place = jnp.bitwise_xor(me_ref[1], mask) * own
            for i in range(own):
                normed = (held[place + i] - center) * scale * gains[s, pl.ds(place + i, 1)]
                out_ref[s, :, i * BLK:(i + 1) * BLK] = normed.astype(jnp.bfloat16)
        return carry

    lax.fori_loop(0, sections, section, start)


def relay(inputs, gain, repeats, me, received, owners):
    sections, rows, part = inputs.shape
    chunks = sections * part // BLK
    shape = jax.ShapeDtypeStruct((sections, rows, AWIN // owners), jnp.bfloat16)
    return pl.pallas_call(
        functools.partial(relay_kernel, sections, owners),
        out_shape=(shape,) * owners,
        in_specs=[VMEM_SPEC, VMEM_SPEC, SMEM_SPEC, SMEM_SPEC] + [VMEM_SPEC] * len(received),
        out_specs=(VMEM_SPEC,) * owners,
        scratch_shapes=[pltpu.VMEM((chunks, rows, BLK), jnp.float32), pltpu.VMEM((sections, chunks + 8, BLK), jnp.float32)],
        compiler_params=params(),
        cost_estimate=pl.CostEstimate(flops=1 << 31, bytes_accessed=2 << 20, transcendentals=0),
    )(inputs, gain, repeats, me, *received)


HALF = BLK // 2
FEATURE_ROWS = BLK + HALF + 16


def pack_three(first, second, third):
    row, col = iotas()
    low_row, low_col = row[:HALF], col[:HALF]
    turned = pltpu.roll(third[HALF:], HALF, 1)
    two = jnp.where(col >= row, first, second)
    half = jnp.where(low_col < low_row, turned, third[:HALF])
    tail_row = lax.broadcasted_iota(jnp.int32, (16, BLK), 0)
    diagonal = jnp.sum(jnp.where(col == row, second, 0.0), axis=0, keepdims=True)
    last = jnp.sum(jnp.where(low_col == low_row + HALF, third[HALF:], 0.0), axis=0, keepdims=True)
    tail = jnp.where(tail_row == 0, diagonal, jnp.where(tail_row == 1, last, 0.0))
    return jnp.concatenate([two, half, tail], axis=0)


def unpack_three(packed):
    row, col = iotas()
    low_row, low_col = row[:HALF], col[:HALF]
    two, half, tail = packed[:BLK], packed[BLK:BLK + HALF], packed[BLK + HALF:]
    turned = two.T
    first = jnp.where(col >= row, two, turned)
    second = jnp.where(col < row, two, jnp.where(col == row, tail[0:1], turned))
    across = jnp.concatenate([half, jnp.zeros_like(half)], axis=0).T
    upper = jnp.where(low_col < low_row, across[:HALF], half)
    corner = pltpu.roll(jnp.where(low_col < low_row, half, across[:HALF]), HALF, 1)
    lower = jnp.where(low_col < HALF, across[HALF:], jnp.where(low_col == low_row + HALF, tail[1:2], corner))
    return jnp.concatenate([first, second, upper, lower], axis=0)


def feature_kernel(micro, scale, order_ref, me_ref, *refs):
    in_refs, (own_ref, *out_refs) = refs[:-micro], refs[-micro:]
    weight = batch_weight(order_ref, me_ref[0], micro) * scale
    for mask, out_ref in zip((0,) + FAR_FIRST, [own_ref] + out_refs):
        s = jnp.bitwise_xor(me_ref[0], mask)
        blocks = []
        for at in range(0, 3 * BLK, BLK):
            feats = jnp.concatenate([ref[s, :, at:at + BLK] for ref in in_refs], axis=0)
            blocks.append(gram(feats, feats) * weight)
        out_ref[...] = pack_three(*blocks).astype(out_ref.dtype)


def feature_terms(order, me, feats, micro, scale):
    return pl.pallas_call(
        functools.partial(feature_kernel, micro, scale),
        out_shape=(jax.ShapeDtypeStruct((FEATURE_ROWS, BLK), jnp.float32),)
        + (jax.ShapeDtypeStruct((FEATURE_ROWS, BLK), jnp.bfloat16),) * (micro - 1),
        in_specs=[SMEM_SPEC, SMEM_SPEC] + [VMEM_SPEC] * len(feats),
        out_specs=(VMEM_SPEC,) * micro,
        compiler_params=params(),
        cost_estimate=pl.CostEstimate(flops=1 << 31, bytes_accessed=1 << 20, transcendentals=0),
    )(order, me, *feats)


def feature_sum_kernel(*refs):
    total = refs[0][...]
    for ref in refs[1:-1]:
        total = total + ref[...].astype(jnp.float32)
    refs[-1][0] = unpack_three(total)


def fast_body(inputs, gain, repeats, order, hidden_grad):
    micro, tok_rows, _ = inputs.shape
    dp_count = lax.axis_size("dp")
    scale = 1.0 / (tok_rows * dp_count)
    gain = gain.reshape(-1, BLK)
    plane, place = lax.axis_index("section").reshape(1), lax.axis_index("dp").reshape(1)
    me = jnp.concatenate([plane, place])
    told, order = lax.optimization_barrier((messages(inputs, gain, repeats, plane), order))
    pieces = tuple(swapped(one, "section", mask) for mask, one in zip(FAR_FIRST, told))

    came = swapped(hidden_terms(order, hidden_grad, place ^ 1, dp_count, scale, 1 << 20), "dp", 1)
    near = hidden_terms(order, hidden_grad, place, dp_count, scale, 1 << 34)
    along_x, along_y, first, second = core_sum(near, came)
    came_x, came_y = swapped(along_x, "dp", 2), swapped(along_y, "dp", 4)
    pieces, first = lax.optimization_barrier((pieces, first))

    feats = relay(inputs, gain, repeats, me, pieces, dp_count)
    feats, came_x, came_y = lax.optimization_barrier((feats, came_x, came_y))
    gathered = [feats[0]] + [swapped(feats[mask], "dp", mask) for mask in (1, 4, 2, 6, 7, 5, 3)]
    along_y, along_x, kept = pair_sum(first, came_x, second, came_y)
    came_y, came_x = swapped(along_y, "dp", 4), swapped(along_x, "dp", 2)
    own, *terms = feature_terms(order, plane, gathered, micro, scale)
    own, kept = lax.optimization_barrier((own, kept))
    terms = [swapped(one, "section", mask) for mask, one in zip(FAR_FIRST, terms)]
    hidden_rows = unpacked(kept, came_y, came_x)
    own, hidden_rows = lax.optimization_barrier((own, hidden_rows))
    feature_rows = small_call(feature_sum_kernel, jax.ShapeDtypeStruct((1, 3 * BLK, BLK), jnp.float32), own, *terms)
    return (feature_rows, hidden_rows)


def normed(value, gain_row):
    center = jnp.mean(value, axis=-1, keepdims=True)
    spread = jnp.mean(jnp.square(value - center), axis=-1, keepdims=True)
    return (value - center) * lax.rsqrt(spread + 1e-05) * gain_row


def weighted_gram(feats, weights):
    shaped = feats.reshape(feats.shape[0], -1, BLK)
    scaled = shaped * weights[:, None, None].astype(shaped.dtype)
    return jnp.einsum("tbi,tbj->bij", scaled, shaped, preferred_element_type=jnp.float32)


def plain_body(inputs, gain, repeats, order, hidden_grad):
    micro, tok_rows, part = inputs.shape
    sections = lax.axis_size("section")
    total_tok = tok_rows * lax.axis_size("dp")
    slot_weight = 0.5 * jnp.power(0.5, micro - 1 - jnp.arange(micro, dtype=jnp.float32))
    hidden_weight = jnp.zeros((micro,), jnp.float32).at[order].set(slot_weight)
    row_weight = jnp.repeat(hidden_weight, tok_rows)
    hidden = weighted_gram(hidden_grad.reshape(micro * tok_rows, GWIN), row_weight) / total_tok
    gains = lax.all_gather(gain[0], "section", axis=0)
    counts = lax.all_gather(repeats[0], "section", axis=0)
    pieces = lax.all_to_all(inputs.reshape(micro * tok_rows, part), "section", 0, 1, tiled=True)

    def section(s, carry):
        value, feats = carry
        value = lax.fori_loop(
            0,
            counts[s] + 1,
            lambda i, v: (v + gelu(normed(v, gains[s]))).astype(jnp.bfloat16).astype(jnp.float32),
            value,
        )
        now = normed(value, gains[s]).astype(jnp.bfloat16)[:, :AWIN]
        return value, lax.dynamic_update_index_in_dim(feats, now, s, 0)

    start = jnp.zeros((sections, pieces.shape[0], AWIN), jnp.bfloat16)
    _, feats = lax.fori_loop(0, sections, section, (pieces.astype(jnp.float32), start))
    feats = lax.all_to_all(feats, "section", 0, 0, tiled=True).reshape(micro * tok_rows, AWIN)
    feature = weighted_gram(feats, row_weight) / total_tok

    def shared(term):
        term = term.reshape(-1, BLK).astype(jnp.bfloat16)
        return lax.psum_scatter(term, "dp", scatter_dimension=0, tiled=True).astype(jnp.float32)[None]

    return (shared(feature), shared(hidden))


def solution(mesh):
    sections, dp_count = mesh.shape["section"], mesh.shape["dp"]

    def body(inputs, gain, repeats, order, hidden_grad):
        aligned = (
            inputs.shape[0] == sections == 4
            and inputs.shape[2] * sections % (16 * BLK) == 0
            and inputs.shape[1] % 16 == 0
            and dp_count == 8
            and AWIN == dp_count * 3 * BLK
            and GWIN % (dp_count * 4 * BLK) == 0
        )
        return (fast_body if aligned else plain_body)(inputs, gain, repeats, order, hidden_grad)

    placed = (
        P(None, "dp", "section"),
        P("section", None),
        P("section"),
        P(),
        P("section", None, "dp", None),
    )
    return jax.shard_map(
        body,
        mesh=mesh,
        in_specs=placed,
        out_specs=(P("section", "dp", None), P("section", "dp", None)),
        check_vma=False,
    )
```

```python
import functools

import jax
import jax.numpy as jnp
from jax import lax
from jax.experimental import pallas as pl
from jax.experimental.pallas import tpu as pltpu
from jax.sharding import PartitionSpec as P

AWIN = 3072
GWIN = 12288
BLK = 128
VMEM_LIMIT = 16 * 1024 * 1024
FAR_FIRST = (2, 3, 1)
STEEP = 92.0
ROOT = 0.7978845608028654

SMEM_SPEC = pl.BlockSpec(memory_space=pltpu.SMEM)
VMEM_SPEC = pl.BlockSpec(memory_space=pltpu.VMEM)


def params(limit=VMEM_LIMIT):
    return pltpu.CompilerParams(vmem_limit_bytes=limit)


def gelu(x):
    inner = ROOT * (x + 0.044715 * (x * x * x))
    return x * (0.5 * (1.0 + jnp.tanh(inner)))


def batch_weight(order_ref, batch_id, micro):
    weight = jnp.float32(0.0)
    for slot in range(micro):
        weight = jnp.where(order_ref[slot] == batch_id, jnp.float32(0.5 * 0.5 ** (micro - 1 - slot)), weight)
    return weight


def gram(left, right):
    return lax.dot_general(left, right, (((0,), (0,)), ((), ())), preferred_element_type=jnp.float32)


def iotas():
    row = lax.broadcasted_iota(jnp.int32, (BLK, BLK), 0)
    col = lax.broadcasted_iota(jnp.int32, (BLK, BLK), 1)
    return row, col


def packed_rows(pairs):
    return pairs * BLK + -(-pairs // 16) * 16


def hidden_kernel(micro, pairs, scale, order_ref, _, *refs):
    grad_refs, out_ref = refs[:-1], refs[-1]
    row, col = iotas()
    weights = [batch_weight(order_ref, m, micro) for m in range(micro)]
    tail_row = lax.broadcasted_iota(jnp.int32, (packed_rows(pairs) - pairs * BLK, BLK), 0)
    for place, grad_ref in enumerate(grad_refs):
        for half in range(2):
            tail = jnp.zeros(tail_row.shape, jnp.float32)
            for pair in range(pairs):
                at = (half * pairs + pair) * 2 * BLK
                parts = [grad_ref[0, m, :, at:at + 2 * BLK] for m in range(micro)]
                scaled = [(part.astype(jnp.float32) * weight).astype(jnp.bfloat16) for part, weight in zip(parts, weights)]
                both = gram(jnp.concatenate(scaled, axis=0), jnp.concatenate(parts, axis=0)) * scale
                first, second = both[:BLK, :BLK], both[BLK:, BLK:]
                packed = jnp.where(col >= row, first, second).astype(jnp.bfloat16)
                out_ref[place, half, pair * BLK:(pair + 1) * BLK] = packed
                diagonal = jnp.sum(jnp.where(col == row, second, 0.0), axis=0, keepdims=True)
                tail = jnp.where(tail_row == pair, diagonal, tail)
            out_ref[place, half, pairs * BLK:] = tail.astype(jnp.bfloat16)


def hidden_terms(order, hidden_grad, me, dp_count, scale, cost):
    _, micro, rows, width = hidden_grad.shape
    own = width // dp_count
    pairs = own // (4 * BLK)
    shape, count = (2, packed_rows(pairs), BLK), dp_count // 2

    def owner(flip):
        return lambda i, order, me: (0, 0, 0, jnp.bitwise_xor(me[0], 2 - 2 * i + flip))

    return pl.pallas_call(
        functools.partial(hidden_kernel, micro, pairs, scale),
        out_shape=jax.ShapeDtypeStruct((count,) + shape, jnp.bfloat16),
        grid_spec=pltpu.PrefetchScalarGridSpec(
            num_scalar_prefetch=2,
            grid=(count // 2,),
            in_specs=[pl.BlockSpec((1, micro, rows, own), owner(4)), pl.BlockSpec((1, micro, rows, own), owner(0))],
            out_specs=pl.BlockSpec((2,) + shape, lambda i, order, me: (i, 0, 0, 0)),
        ),
        compiler_params=params(),
        cost_estimate=pl.CostEstimate(flops=cost, bytes_accessed=1 << 10, transcendentals=0),
    )(order, me, hidden_grad, hidden_grad)


def small_call(kernel, shapes, *operands, cost=1 << 20):
    return pl.pallas_call(
        kernel,
        out_shape=shapes,
        in_specs=[VMEM_SPEC] * len(operands),
        out_specs=jax.tree.map(lambda _: VMEM_SPEC, shapes),
        compiler_params=params(),
        cost_estimate=pl.CostEstimate(flops=cost, bytes_accessed=1 << 10, transcendentals=0),
    )(*operands)


def core_sum_kernel(near_ref, came_ref, along_x_ref, along_y_ref, first_ref, second_ref):
    def total(place, half):
        return near_ref[place, half].astype(jnp.float32) + came_ref[place, half].astype(jnp.float32)

    for i in range(2):
        along_x_ref[i] = total(i, 0).astype(jnp.bfloat16)
        along_y_ref[i] = total(2 * i, 1).astype(jnp.bfloat16)
        first_ref[i] = total(2 + i, 0)
        second_ref[i] = total(1 + 2 * i, 1)


def pair_sum_kernel(first_ref, came_x_ref, second_ref, came_y_ref, along_y_ref, along_x_ref, kept_ref):
    along_y_ref[...] = (first_ref[0] + came_x_ref[0].astype(jnp.float32)).astype(jnp.bfloat16)
    along_x_ref[...] = (second_ref[0] + came_y_ref[0].astype(jnp.float32)).astype(jnp.bfloat16)
    kept_ref[0] = first_ref[1] + came_x_ref[1].astype(jnp.float32)
    kept_ref[1] = second_ref[1] + came_y_ref[1].astype(jnp.float32)


def unpack_kernel(pairs, kept_ref, came_y_ref, came_x_ref, out_ref):
    row, col = iotas()
    for half, came_ref in enumerate((came_y_ref, came_x_ref)):

        def total(rows):
            return kept_ref[half, rows] + came_ref[rows].astype(jnp.float32)

        tail = total(slice(pairs * BLK, None))
        for pair in range(pairs):
            value = total(slice(pair * BLK, (pair + 1) * BLK))
            turned = value.T
            at = (half * pairs + pair) * 2 * BLK
            out_ref[0, at:at + BLK] = jnp.where(col >= row, value, turned)
            second = jnp.where(col == row, tail[pair:pair + 1], turned)
            out_ref[0, at + BLK:at + 2 * BLK] = jnp.where(col < row, value, second)


def core_sum(near, came):
    one = near.shape[2:]
    sent = jax.ShapeDtypeStruct((2,) + one, jnp.bfloat16)
    kept = jax.ShapeDtypeStruct((2,) + one, jnp.float32)
    return small_call(core_sum_kernel, (sent, sent, kept, kept), near, came)


def pair_sum(first, came_x, second, came_y):
    last = jax.ShapeDtypeStruct(first.shape[1:], jnp.bfloat16)
    return small_call(pair_sum_kernel, (last, last, first), first, came_x, second, came_y)


def unpacked(kept, came_y, came_x):
    pairs = kept.shape[1] // BLK
    out = jax.ShapeDtypeStruct((1, 4 * pairs * BLK, BLK), jnp.float32)
    return small_call(functools.partial(unpack_kernel, pairs), out, kept, came_y, came_x)


def swapped(shard, axis, mask):
    return lax.ppermute(shard, axis, [(i, i ^ mask) for i in range(lax.axis_size(axis))])


def message_kernel(in_ref, gain_ref, repeats_ref, me_ref, *out_refs):
    _, rows, part = in_ref.shape
    chunks, gain_rows = part // BLK, gain_ref.shape[0]
    coded = jnp.exp(STEEP * (gain_ref[...] - 1.0)).astype(jnp.bfloat16)
    count = jnp.full((16, BLK), repeats_ref[0], jnp.int32).astype(jnp.float32).astype(jnp.bfloat16)
    at = chunks * rows
    for mask, out_ref in zip(FAR_FIRST, out_refs):
        target = jnp.bitwise_xor(me_ref[0], mask)
        for chunk in range(chunks):
            out_ref[chunk * rows:(chunk + 1) * rows] = in_ref[target, :, chunk * BLK:(chunk + 1) * BLK]
        out_ref[at:at + gain_rows] = coded
        out_ref[at + gain_rows:] = count


def messages(inputs, gain, repeats, me):
    micro, rows, part = inputs.shape
    shape = jax.ShapeDtypeStruct((part // BLK * rows + gain.shape[0] + 16, BLK), jnp.bfloat16)
    return pl.pallas_call(
        message_kernel,
        out_shape=(shape,) * (micro - 1),
        in_specs=[VMEM_SPEC, VMEM_SPEC, SMEM_SPEC, SMEM_SPEC],
        out_specs=(VMEM_SPEC,) * (micro - 1),
        compiler_params=params(60 * 1024 * 1024),
        cost_estimate=pl.CostEstimate(flops=1 << 33, bytes_accessed=1 << 20, transcendentals=0),
    )(inputs, gain, repeats, me)


def relay_kernel(sections, owners, own_ref, gain_ref, repeats_ref, me_ref, *refs):
    received, out_refs, (held, gains) = refs[:sections - 1], refs[sections - 1:-2], refs[-2:]
    chunks, rows, _ = held.shape
    own = AWIN // owners // BLK
    width = chunks * BLK
    part = chunks // sections
    at = part * rows
    me = me_ref[0]
    none = jnp.zeros((rows, BLK), jnp.float32)

    def mean(total):
        return jnp.sum(total, axis=-1, keepdims=True) * (1.0 / width)

    gains[me, :chunks] = gain_ref[...]
    gains[me, chunks:] = jnp.full((8, BLK), repeats_ref[0], jnp.int32).astype(jnp.float32)
    total = none
    for chunk in range(part):
        value = own_ref[me, :, chunk * BLK:(chunk + 1) * BLK].astype(jnp.float32)
        held[me * part + chunk] = value
        total = total + value
    for mask, ref in zip(FAR_FIRST, received):
        source = jnp.bitwise_xor(me, mask)
        gains[source, :chunks] = 1.0 + jnp.log(ref[at:at + chunks].astype(jnp.float32)) * (1.0 / STEEP)
        gains[source, chunks:] = ref[at + chunks:].astype(jnp.float32)[:8]
        for chunk in range(part):
            value = ref[chunk * rows:(chunk + 1) * rows].astype(jnp.float32)
            held[source * part + chunk] = value
            total = total + value
    center = mean(total)
    square = none
    for chunk in range(chunks):
        square = square + jnp.square(held[chunk] - center)
    start = (center, lax.rsqrt(mean(square) + 1e-05))

    def section(s, carry):
        repeats = jnp.max(gains[s, chunks:]).astype(jnp.int32)

        def apply(_, carry):
            center, scale = carry
            half = 0.5 * scale
            total, square = none, none
            for chunk in range(chunks):
                value = held[chunk]
                y = (value - center) * half * gains[s, chunk:chunk + 1]
                inner = y * (2.0 * ROOT + (8.0 * 0.044715 * ROOT) * (y * y))
                value = (value + (y + y * jnp.tanh(inner))).astype(jnp.bfloat16).astype(jnp.float32)
                held[chunk] = value
                moved = value - center
                total = total + moved
                square = square + moved * moved
            shift = mean(total)
            spread = jnp.maximum(mean(square) - shift * shift, 0.0)
            return center + shift, lax.rsqrt(spread + 1e-05)

        carry = lax.fori_loop(0, repeats + 1, apply, carry)
        center, scale = carry
        for mask, out_ref in enumerate(out_refs):
            place = jnp.bitwise_xor(me_ref[1], mask) * own
            for i in range(own):
                normed = (held[place + i] - center) * scale * gains[s, pl.ds(place + i, 1)]
                out_ref[s, :, i * BLK:(i + 1) * BLK] = normed.astype(jnp.bfloat16)
        return carry

    lax.fori_loop(0, sections, section, start)


def relay(inputs, gain, repeats, me, received, owners):
    sections, rows, part = inputs.shape
    chunks = sections * part // BLK
    shape = jax.ShapeDtypeStruct((sections, rows, AWIN // owners), jnp.bfloat16)
    return pl.pallas_call(
        functools.partial(relay_kernel, sections, owners),
        out_shape=(shape,) * owners,
        in_specs=[VMEM_SPEC, VMEM_SPEC, SMEM_SPEC, SMEM_SPEC] + [VMEM_SPEC] * len(received),
        out_specs=(VMEM_SPEC,) * owners,
        scratch_shapes=[pltpu.VMEM((chunks, rows, BLK), jnp.float32), pltpu.VMEM((sections, chunks + 8, BLK), jnp.float32)],
        compiler_params=params(),
        cost_estimate=pl.CostEstimate(flops=1 << 31, bytes_accessed=2 << 20, transcendentals=0),
    )(inputs, gain, repeats, me, *received)


HALF = BLK // 2
FEATURE_ROWS = BLK + HALF + 16


def pack_three(first, second, third):
    row, col = iotas()
    low_row, low_col = row[:HALF], col[:HALF]
    turned = pltpu.roll(third[HALF:], HALF, 1)
    two = jnp.where(col >= row, first, second)
    half = jnp.where(low_col < low_row, turned, third[:HALF])
    tail_row = lax.broadcasted_iota(jnp.int32, (16, BLK), 0)
    diagonal = jnp.sum(jnp.where(col == row, second, 0.0), axis=0, keepdims=True)
    last = jnp.sum(jnp.where(low_col == low_row + HALF, third[HALF:], 0.0), axis=0, keepdims=True)
    tail = jnp.where(tail_row == 0, diagonal, jnp.where(tail_row == 1, last, 0.0))
    return jnp.concatenate([two, half, tail], axis=0)


def unpack_three(packed):
    row, col = iotas()
    low_row, low_col = row[:HALF], col[:HALF]
    two, half, tail = packed[:BLK], packed[BLK:BLK + HALF], packed[BLK + HALF:]
    turned = two.T
    first = jnp.where(col >= row, two, turned)
    second = jnp.where(col < row, two, jnp.where(col == row, tail[0:1], turned))
    across = jnp.concatenate([half, jnp.zeros_like(half)], axis=0).T
    upper = jnp.where(low_col < low_row, across[:HALF], half)
    corner = pltpu.roll(jnp.where(low_col < low_row, half, across[:HALF]), HALF, 1)
    lower = jnp.where(low_col < HALF, across[HALF:], jnp.where(low_col == low_row + HALF, tail[1:2], corner))
    return jnp.concatenate([first, second, upper, lower], axis=0)


def feature_kernel(micro, scale, order_ref, me_ref, *refs):
    in_refs, (own_ref, *out_refs) = refs[:-micro], refs[-micro:]
    weight = batch_weight(order_ref, me_ref[0], micro) * scale
    for mask, out_ref in zip((0,) + FAR_FIRST, [own_ref] + out_refs):
        s = jnp.bitwise_xor(me_ref[0], mask)
        blocks = []
        for at in range(0, 3 * BLK, BLK):
            feats = jnp.concatenate([ref[s, :, at:at + BLK] for ref in in_refs], axis=0)
            blocks.append(gram(feats, feats) * weight)
        out_ref[...] = pack_three(*blocks).astype(out_ref.dtype)


def feature_terms(order, me, feats, micro, scale):
    return pl.pallas_call(
        functools.partial(feature_kernel, micro, scale),
        out_shape=(jax.ShapeDtypeStruct((FEATURE_ROWS, BLK), jnp.float32),)
        + (jax.ShapeDtypeStruct((FEATURE_ROWS, BLK), jnp.bfloat16),) * (micro - 1),
        in_specs=[SMEM_SPEC, SMEM_SPEC] + [VMEM_SPEC] * len(feats),
        out_specs=(VMEM_SPEC,) * micro,
        compiler_params=params(),
        cost_estimate=pl.CostEstimate(flops=1 << 31, bytes_accessed=1 << 20, transcendentals=0),
    )(order, me, *feats)


def feature_sum_kernel(*refs):
    total = refs[0][...]
    for ref in refs[1:-1]:
        total = total + ref[...].astype(jnp.float32)
    refs[-1][0] = unpack_three(total)


def fast_body(inputs, gain, repeats, order, hidden_grad):
    micro, tok_rows, _ = inputs.shape
    dp_count = lax.axis_size("dp")
    scale = 1.0 / (tok_rows * dp_count)
    gain = gain.reshape(-1, BLK)
    plane, place = lax.axis_index("section").reshape(1), lax.axis_index("dp").reshape(1)
    me = jnp.concatenate([plane, place])
    told, order = lax.optimization_barrier((messages(inputs, gain, repeats, plane), order))
    pieces = tuple(swapped(one, "section", mask) for mask, one in zip(FAR_FIRST, told))

    came = swapped(hidden_terms(order, hidden_grad, place ^ 1, dp_count, scale, 1 << 20), "dp", 1)
    near = hidden_terms(order, hidden_grad, place, dp_count, scale, 1 << 34)
    along_x, along_y, first, second = core_sum(near, came)
    came_x, came_y = swapped(along_x, "dp", 2), swapped(along_y, "dp", 4)
    pieces, first = lax.optimization_barrier((pieces, first))

    feats = relay(inputs, gain, repeats, me, pieces, dp_count)
    feats, came_x, came_y = lax.optimization_barrier((feats, came_x, came_y))
    gathered = [feats[0]] + [swapped(feats[mask], "dp", mask) for mask in (1, 4, 2, 5, 6, 7, 3)]
    along_y, along_x, kept = pair_sum(first, came_x, second, came_y)
    came_y, came_x = swapped(along_y, "dp", 4), swapped(along_x, "dp", 2)
    own, *terms = feature_terms(order, plane, gathered, micro, scale)
    own, kept = lax.optimization_barrier((own, kept))
    terms = [swapped(one, "section", mask) for mask, one in zip(FAR_FIRST, terms)]
    hidden_rows = unpacked(kept, came_y, came_x)
    own, hidden_rows = lax.optimization_barrier((own, hidden_rows))
    feature_rows = small_call(feature_sum_kernel, jax.ShapeDtypeStruct((1, 3 * BLK, BLK), jnp.float32), own, *terms)
    return (feature_rows, hidden_rows)


def normed(value, gain_row):
    center = jnp.mean(value, axis=-1, keepdims=True)
    spread = jnp.mean(jnp.square(value - center), axis=-1, keepdims=True)
    return (value - center) * lax.rsqrt(spread + 1e-05) * gain_row


def weighted_gram(feats, weights):
    shaped = feats.reshape(feats.shape[0], -1, BLK)
    scaled = shaped * weights[:, None, None].astype(shaped.dtype)
    return jnp.einsum("tbi,tbj->bij", scaled, shaped, preferred_element_type=jnp.float32)


def plain_body(inputs, gain, repeats, order, hidden_grad):
    micro, tok_rows, part = inputs.shape
    sections = lax.axis_size("section")
    total_tok = tok_rows * lax.axis_size("dp")
    slot_weight = 0.5 * jnp.power(0.5, micro - 1 - jnp.arange(micro, dtype=jnp.float32))
    hidden_weight = jnp.zeros((micro,), jnp.float32).at[order].set(slot_weight)
    row_weight = jnp.repeat(hidden_weight, tok_rows)
    hidden = weighted_gram(hidden_grad.reshape(micro * tok_rows, GWIN), row_weight) / total_tok
    gains = lax.all_gather(gain[0], "section", axis=0)
    counts = lax.all_gather(repeats[0], "section", axis=0)
    pieces = lax.all_to_all(inputs.reshape(micro * tok_rows, part), "section", 0, 1, tiled=True)

    def section(s, carry):
        value, feats = carry
        value = lax.fori_loop(
            0,
            counts[s] + 1,
            lambda i, v: (v + gelu(normed(v, gains[s]))).astype(jnp.bfloat16).astype(jnp.float32),
            value,
        )
        now = normed(value, gains[s]).astype(jnp.bfloat16)[:, :AWIN]
        return value, lax.dynamic_update_index_in_dim(feats, now, s, 0)

    start = jnp.zeros((sections, pieces.shape[0], AWIN), jnp.bfloat16)
    _, feats = lax.fori_loop(0, sections, section, (pieces.astype(jnp.float32), start))
    feats = lax.all_to_all(feats, "section", 0, 0, tiled=True).reshape(micro * tok_rows, AWIN)
    feature = weighted_gram(feats, row_weight) / total_tok

    def shared(term):
        term = term.reshape(-1, BLK).astype(jnp.bfloat16)
        return lax.psum_scatter(term, "dp", scatter_dimension=0, tiled=True).astype(jnp.float32)[None]

    return (shared(feature), shared(hidden))


def solution(mesh):
    sections, dp_count = mesh.shape["section"], mesh.shape["dp"]

    def body(inputs, gain, repeats, order, hidden_grad):
        aligned = (
            inputs.shape[0] == sections == 4
            and inputs.shape[2] * sections % (16 * BLK) == 0
            and inputs.shape[1] % 16 == 0
            and dp_count == 8
            and AWIN == dp_count * 3 * BLK
            and GWIN % (dp_count * 4 * BLK) == 0
        )
        return (fast_body if aligned else plain_body)(inputs, gain, repeats, order, hidden_grad)

    placed = (
        P(None, "dp", "section"),
        P("section", None),
        P("section"),
        P(),
        P("section", None, "dp", None),
    )
    return jax.shard_map(
        body,
        mesh=mesh,
        in_specs=placed,
        out_specs=(P("section", "dp", None), P("section", "dp", None)),
        check_vma=False,
    )
```
